32 devices in a mesh: dp: 2 (over y), row: 4 (over z), col: 4 (over x, core).
Axes of the slice: x: 2, y: 2, z: 4, core: 2. Of those that a mesh axis runs over, the one named last changes fastest.
Arguments:
- hidden_in: bfloat16 [4096, 1600], P(('dp', 'col'), 'row'), may hold values from -6 to 6
- upstream: bfloat16 [4096, 1600], P(('dp', 'col'), 'row')
- segment_ids: int32 [4096], P('dp'), may hold values from 1 to 3, as said below
- qkv_weight: float32 [1600, 4800], P(('row', 'dp'), 'col')
- proj_weight: float32 [1600, 1600], P(('col', 'dp'), 'row'), may hold values from -0.625 to 0.625
- up_weight: float32 [1600, 6400], P(('row', 'dp'), 'col'), may hold values from -0.15625 to 0.15625
- down_weight: float32 [6400, 1600], P(('col', 'dp'), 'row'), may hold values from -0.078125 to 0.078125
- vectors: float32 [8, 1600], replicated
- up_bias: float32 [6400], replicated, may hold values from -3 to 3
- qkv_moments: float32 [2, 1600, 4800], P(None, ('row', 'dp'), 'col'), as said below
- proj_moments: float32 [2, 1600, 1600], P(None, ('col', 'dp'), 'row'), as said below
- up_moments: float32 [2, 1600, 6400], P(None, ('row', 'dp'), 'col'), as said below
- down_moments: float32 [2, 6400, 1600], P(None, ('col', 'dp'), 'row'), as said below
- vector_moments: float32 [2, 8, 1600], replicated, as said below
- bias_moments: float32 [2, 6400], replicated, as said below
Outputs:
- block_out: bfloat16 [4096, 1600], P(('dp', 'col'), 'row')
- input_grad: bfloat16 [4096, 1600], P(('dp', 'col'), 'row')
- qkv_grad: float32 [1600, 4800], P(('row', 'dp'), 'col')
- proj_grad: float32 [1600, 1600], P(('col', 'dp'), 'row')
- up_grad: float32 [1600, 6400], P(('row', 'dp'), 'col')
- down_grad: float32 [6400, 1600], P(('col', 'dp'), 'row')
- vector_grad: float32 [8, 1600], replicated
- bias_grad: float32 [6400], replicated
- new_qkv: float32 [1600, 4800], P(('row', 'dp'), 'col')
- new_proj: float32 [1600, 1600], P(('col', 'dp'), 'row')
- new_up: float32 [1600, 6400], P(('row', 'dp'), 'col')
- new_down: float32 [6400, 1600], P(('col', 'dp'), 'row')
- new_vectors: float32 [8, 1600], replicated
- new_bias: float32 [6400], replicated
- qkv_state: float32 [2, 1600, 4800], P(None, ('row', 'dp'), 'col')
- proj_state: float32 [2, 1600, 1600], P(None, ('col', 'dp'), 'row')
- up_state: float32 [2, 1600, 6400], P(None, ('row', 'dp'), 'col')
- down_state: float32 [2, 6400, 1600], P(None, ('col', 'dp'), 'row')
- vector_state: float32 [2, 8, 1600], replicated
- bias_state: float32 [2, 6400], replicated
The draws below stay inside these ranges and needn't reach their ends.
Inputs may be any that keep to these rules, and one draw needn't show every extreme that they name: `segment_ids`: ids never fall; a sequence is a run of equal ids; no sequence crosses a multiple of 2048 tokens; the first 2048 tokens form one sequence. `qkv_moments`: the second row is positive. `proj_moments`: the second row is positive. `up_moments`: the second row is positive. `down_moments`: the second row is positive. `vector_moments`: the second row is positive. `bias_moments`: the second row is positive.
All inputs are finite; a program needn't handle non-finite values.
Results may differ from the reference program's by a relative error of at most 0.025.
Values may be sent and summed in bfloat16 or wider, within the bound.
No kernel may reach another device: no remote copies, remote signals or barrier semaphores. Data moves between devices by JAX's collectives and lax.ppermute only.
A program may use at most 256 MiB of HBM per device.

```python
import math
import jax
import jax.numpy as jnp
from jax import lax

D = 1600
HEADS = 25
HEAD_DIM = 64
FF = 6400
MAXLEN = 2048
STEP = 3
GROUP = 2048
TOKENS = 4096
N_ROW = 4
N_COL = 4


def moment_pair(key, shape_dims, grad_size):
    first_key, second_key = jax.random.split(key)
    first_moment = jax.random.normal(first_key, shape_dims, jnp.float32) * (0.1 * grad_size)
    factor = jnp.exp(jax.random.uniform(second_key, shape_dims, jnp.float32, math.log(0.5), math.log(8.0)))
    second = factor * (0.05 / 0.95 * grad_size * grad_size)
    return jnp.stack([first_moment, second])


def draw_upstream(key, part):
    spread = 0.5 / math.sqrt(TOKENS)
    return (jnp.clip(jax.random.normal(key, (TOKENS, D), jnp.float32), -6.0, 6.0) * spread).astype(jnp.bfloat16)


def draw_segment_ids(key, part):
    blocks = TOKENS // MAXLEN
    cut_points = jax.random.randint(key, (blocks,), 0, MAXLEN).astype(jnp.int32)
    cut_points = cut_points.at[0].set(0)
    position = jnp.arange(TOKENS, dtype=jnp.int32)
    block_of = position // MAXLEN
    inner_pos = position % MAXLEN
    return (2 * block_of + (inner_pos >= cut_points[block_of]).astype(jnp.int32)).astype(jnp.int32)


def draw_qkv_weight(key, part):
    base_key = jax.random.fold_in(key, 0)
    return jax.random.normal(base_key, (D, 3 * D), jnp.float32) * (1.0 / math.sqrt(D))


def draw_vectors(key, part):
    gain_key, shift_key = jax.random.split(key)
    gain_draw = jax.random.uniform(gain_key, (8, D), jnp.float32, 0.5, 1.5)
    shifts = jax.random.normal(shift_key, (8, D), jnp.float32) * 0.5
    row_number = jnp.arange(8)
    is_gain = (row_number == 0) | (row_number == 5)
    return jnp.where(is_gain[:, None], gain_draw, shifts)


def draw_qkv_moments(key, part):
    return moment_pair(key, (D, 3 * D), 0.7)


def draw_proj_moments(key, part):
    return moment_pair(key, (D, D), 0.2)


def draw_up_moments(key, part):
    return moment_pair(key, (D, FF), 0.18)


def draw_down_moments(key, part):
    return moment_pair(key, (FF, D), 0.3)


def draw_vector_moments(key, part):
    return moment_pair(key, (8, D), 0.75)


def draw_bias_moments(key, part):
    return moment_pair(key, (FF,), 0.18)


def levels(key, extent, cuts, smallest, largest):
    loudness = 1.0
    for dim, shards_of in cuts:
        heights = jax.random.uniform(jax.random.fold_in(jax.random.fold_in(key, 6), dim), (shards_of,), jnp.float32, smallest / len(cuts), largest / len(cuts))
        loudness = loudness * jnp.repeat(jnp.exp(heights), extent[dim] // shards_of).reshape((-1,) + (1,) * (len(extent) - 1 - dim))
    return loudness


def scatter_about(rng, extent, width, reach, cuts=(), kind=jnp.bfloat16):
    result = jax.random.normal(rng, extent, jnp.float32) * width
    if len(cuts) > 0:
        result = levels(rng, extent, cuts, -0.22, 0.18) * result
    return jnp.clip(result, min=-reach, max=reach).astype(kind)


def setup_inputs(seed: int = 0) -> dict:
    streams_of = jax.random.split(jax.random.key(seed), 16)
    hidden_in = scatter_about(streams_of[0], (TOKENS, D), 1.0, 6.0, ((0, 8), (1, 4)))
    upstream = draw_upstream(jax.random.fold_in(streams_of[15], 71), 0)
    segment_ids = draw_segment_ids(jax.random.fold_in(streams_of[15], 71), 0)
    qkv_weight = draw_qkv_weight(jax.random.fold_in(streams_of[15], 71), 0)
    proj_weight = scatter_about(streams_of[4], (D, D), (D // 16) ** -0.5, 0.625, ((0, 8), (1, 4)), jnp.float32)
    up_weight = scatter_about(streams_of[5], (D, FF), D ** -0.5, 0.15625, ((0, 8), (1, 4)), jnp.float32)
    down_weight = scatter_about(streams_of[6], (FF, D), FF ** -0.5, 0.078125, ((0, 8), (1, 4)), jnp.float32)
    vectors = draw_vectors(jax.random.fold_in(streams_of[15], 71), 0)
    up_bias = scatter_about(streams_of[8], (FF,), 0.5, 3.0, (), jnp.float32)
    qkv_moments = draw_qkv_moments(jax.random.fold_in(streams_of[15], 71), 0)
    proj_moments = draw_proj_moments(jax.random.fold_in(streams_of[15], 71), 0)
    up_moments = draw_up_moments(jax.random.fold_in(streams_of[15], 71), 0)
    down_moments = draw_down_moments(jax.random.fold_in(streams_of[15], 71), 0)
    vector_moments = draw_vector_moments(jax.random.fold_in(streams_of[15], 71), 0)
    bias_moments = draw_bias_moments(jax.random.fold_in(streams_of[15], 71), 0)
    return {"hidden_in": hidden_in, "upstream": upstream, "segment_ids": segment_ids, "qkv_weight": qkv_weight, "proj_weight": proj_weight, "up_weight": up_weight, "down_weight": down_weight, "vectors": vectors, "up_bias": up_bias, "qkv_moments": qkv_moments, "proj_moments": proj_moments, "up_moments": up_moments, "down_moments": down_moments, "vector_moments": vector_moments, "bias_moments": bias_moments}


EPS_NORM = 1e-05
BETA_ONE = 0.9
BETA_TWO = 0.95
EPS_ADAM = 1e-08
LR_MATRIX = 0.08
LR_VECTOR = 0.3
DECAY = 0.1
NEG_FILL = -1e+30
GELU_COEF = 0.7978845608028654
GELU_CUBE = 0.044715

def gelu_tanh(pre_act):
    inside = GELU_COEF * (pre_act + GELU_CUBE * pre_act * pre_act * pre_act)
    return 0.5 * pre_act * (1.0 + jnp.tanh(inside))

def gelu_slope(pre_act):
    inside = GELU_COEF * (pre_act + GELU_CUBE * pre_act * pre_act * pre_act)
    tanh_val = jnp.tanh(inside)
    return 0.5 * (1.0 + tanh_val) + 0.5 * pre_act * (1.0 - tanh_val * tanh_val) * GELU_COEF * (1.0 + 3.0 * GELU_CUBE * pre_act * pre_act)

def split_product(left_side, right_side, pieces):
    block_width = left_side.shape[1] // pieces
    total_sum = jnp.zeros((left_side.shape[0], right_side.shape[1]), jnp.float32)
    for piece_index in range(pieces):
        lower = piece_index * block_width
        partial_rows = jnp.dot(left_side[:, lower:lower + block_width], right_side[lower:lower + block_width], preferred_element_type=jnp.float32)
        total_sum = total_sum + lax.optimization_barrier(partial_rows.astype(jnp.bfloat16)).astype(jnp.float32)
    return total_sum

def norm_forward(values, gain_vec, shift_vec):
    center = lax.optimization_barrier(jnp.mean(values, axis=1, keepdims=True))
    spread = lax.optimization_barrier(jnp.mean(values * values, axis=1, keepdims=True)) - center * center
    inverse = lax.rsqrt(spread + EPS_NORM)
    normed = (values - center) * inverse
    return (normed, inverse, (normed * gain_vec + shift_vec).astype(jnp.bfloat16))

def norm_backward(grad_normed, normed, inverse, gain_vec):
    scaled = grad_normed * gain_vec
    first_mean = lax.optimization_barrier(jnp.mean(scaled, axis=1, keepdims=True))
    second_mean = lax.optimization_barrier(jnp.mean(scaled * normed, axis=1, keepdims=True))
    return inverse * (scaled - first_mean - normed * second_mean)

def heads_of(matrix):
    return matrix.reshape(matrix.shape[0], HEADS, HEAD_DIM).transpose(1, 0, 2)

def rows_of(stacked):
    return stacked.transpose(1, 0, 2).reshape(stacked.shape[1], HEADS * HEAD_DIM)

def head_scores(query_rows, key_rows, allowed, factor):
    scores = jnp.dot(query_rows, key_rows.T, preferred_element_type=jnp.float32) * factor
    return jnp.where(allowed, scores, NEG_FILL)

def head_forward(query_rows, key_rows, value_rows, allowed, factor):
    scores = head_scores(query_rows, key_rows, allowed, factor)
    row_max = lax.optimization_barrier(jnp.max(scores, axis=1, keepdims=True))
    log_total = row_max + jnp.log(lax.optimization_barrier(jnp.sum(jnp.exp(scores - row_max), axis=1, keepdims=True)))
    chances = jnp.exp(scores - log_total)
    mixed_out = jnp.dot(chances.astype(jnp.bfloat16), value_rows, preferred_element_type=jnp.float32)
    return (mixed_out.astype(jnp.bfloat16), log_total)

def head_backward(query_rows, key_rows, value_rows, log_total, grad_rows, allowed, factor):
    chances = jnp.exp(head_scores(query_rows, key_rows, allowed, factor) - log_total)
    grad_chances = jnp.dot(grad_rows, value_rows.T, preferred_element_type=jnp.float32)
    row_dot = lax.optimization_barrier(jnp.sum(chances * grad_chances, axis=1, keepdims=True))
    grad_scores = (chances * (grad_chances - row_dot)).astype(jnp.bfloat16)
    grad_query = jnp.dot(grad_scores, key_rows, preferred_element_type=jnp.float32) * factor
    grad_key = jnp.dot(grad_scores.T, query_rows, preferred_element_type=jnp.float32) * factor
    grad_value = jnp.dot(chances.astype(jnp.bfloat16).T, grad_rows, preferred_element_type=jnp.float32)
    return (grad_query, grad_key, grad_value)

def adam_step(weight, gradient, moments, rate):
    first_moment = BETA_ONE * moments[0] + (1.0 - BETA_ONE) * gradient
    second = BETA_TWO * moments[1] + (1.0 - BETA_TWO) * gradient * gradient
    first_fix = 1.0 - BETA_ONE ** STEP
    second_fix = 1.0 - BETA_TWO ** STEP
    stepped = weight - rate * (first_moment / first_fix / (jnp.sqrt(second / second_fix) + EPS_ADAM) + DECAY * weight)
    return (stepped, jnp.stack([first_moment, second]))

def reference(hidden_in, upstream, segment_ids, qkv_weight, proj_weight, up_weight, down_weight, vectors, up_bias, qkv_moments, proj_moments, up_moments, down_moments, vector_moments, bias_moments):
    w_qkv = qkv_weight.astype(jnp.bfloat16)
    w_proj = proj_weight.astype(jnp.bfloat16)
    w_up = up_weight.astype(jnp.bfloat16)
    w_down = down_weight.astype(jnp.bfloat16)
    factor = 1.0 / math.sqrt(HEAD_DIM)
    qkv_shift = jnp.concatenate([vectors[2], jnp.zeros((D,), jnp.float32), vectors[3]])
    position = jnp.arange(GROUP, dtype=jnp.int32)

    def group_step(carry, block_items):
        inputs_bf, upstream_bf, segment_rows = block_items
        allowed = (segment_rows[:, None] == segment_rows[None, :]) & (position[None, :] <= position[:, None])
        inputs_f = inputs_bf.astype(jnp.float32)
        normed_one, inverse_one, ln_one = norm_forward(inputs_f, vectors[0], vectors[1])
        qkv_rows = (split_product(ln_one, w_qkv, N_ROW) + qkv_shift).astype(jnp.bfloat16)
        queries = heads_of(qkv_rows[:, :D])
        keys_heads = heads_of(qkv_rows[:, D:2 * D])
        values_heads = heads_of(qkv_rows[:, 2 * D:])
        attn_heads, log_totals = lax.map(lambda head_items: head_forward(head_items[0], head_items[1], head_items[2], allowed, factor), (queries, keys_heads, values_heads))
        attn_rows = rows_of(attn_heads)
        resid_mid = inputs_f + split_product(attn_rows, w_proj, N_COL) + vectors[4]
        normed_two, inverse_two, ln_two = norm_forward(resid_mid, vectors[5], vectors[6])
        pre_act = split_product(ln_two, w_up, N_ROW) + up_bias
        activated = gelu_tanh(pre_act).astype(jnp.bfloat16)
        block_rows = (resid_mid + split_product(activated, w_down, N_COL) + vectors[7]).astype(jnp.bfloat16)
        grad_top = upstream_bf.astype(jnp.float32)
        down_part = jnp.dot(activated.T, upstream_bf, preferred_element_type=jnp.float32)
        grad_pre = split_product(upstream_bf, w_down.T, N_ROW) * gelu_slope(pre_act)
        grad_pre_half = grad_pre.astype(jnp.bfloat16)
        up_part = jnp.dot(ln_two.T, grad_pre_half, preferred_element_type=jnp.float32)
        grad_ln_two = split_product(grad_pre_half, w_up.T, N_COL)
        grad_mid = grad_top + norm_backward(grad_ln_two, normed_two, inverse_two, vectors[5])
        grad_mid_half = grad_mid.astype(jnp.bfloat16)
        proj_part = jnp.dot(attn_rows.T, grad_mid_half, preferred_element_type=jnp.float32)
        grad_attn = split_product(grad_mid_half, w_proj.T, N_ROW).astype(jnp.bfloat16)
        grad_queries, grad_keys, grad_values = lax.map(lambda head_items: head_backward(head_items[0], head_items[1], head_items[2], head_items[3], head_items[4], allowed, factor), (queries, keys_heads, values_heads, log_totals, heads_of(grad_attn)))
        grad_query_rows = rows_of(grad_queries)
        grad_value_rows = rows_of(grad_values)
        grad_qkv = jnp.concatenate([grad_query_rows, rows_of(grad_keys), grad_value_rows], axis=1).astype(jnp.bfloat16)
        qkv_part = jnp.dot(ln_one.T, grad_qkv, preferred_element_type=jnp.float32)
        grad_ln_one = split_product(grad_qkv, w_qkv.T, N_COL)
        grad_input = grad_mid + norm_backward(grad_ln_one, normed_one, inverse_one, vectors[0])
        vector_part = jnp.stack([lax.optimization_barrier(jnp.sum(grad_ln_one * normed_one, axis=0)), lax.optimization_barrier(jnp.sum(grad_ln_one, axis=0)), lax.optimization_barrier(jnp.sum(grad_query_rows, axis=0)), lax.optimization_barrier(jnp.sum(grad_value_rows, axis=0)), lax.optimization_barrier(jnp.sum(grad_mid, axis=0)), lax.optimization_barrier(jnp.sum(grad_ln_two * normed_two, axis=0)), lax.optimization_barrier(jnp.sum(grad_ln_two, axis=0)), lax.optimization_barrier(jnp.sum(grad_top, axis=0))])
        bias_part = lax.optimization_barrier(jnp.sum(grad_pre, axis=0))
        new_carry = jax.tree.map(lambda older, newer: older + newer, carry, (qkv_part, proj_part, up_part, down_part, vector_part, bias_part))
        return (new_carry, (block_rows, grad_input.astype(jnp.bfloat16)))
    initial = (jnp.zeros((D, 3 * D), jnp.float32), jnp.zeros((D, D), jnp.float32), jnp.zeros((D, FF), jnp.float32), jnp.zeros((FF, D), jnp.float32), jnp.zeros((8, D), jnp.float32), jnp.zeros((FF,), jnp.float32))
    groups = TOKENS // GROUP
    summed, (out_rows, grad_rows) = lax.scan(group_step, initial, (hidden_in.reshape(groups, GROUP, D), upstream.reshape(groups, GROUP, D), segment_ids.reshape(groups, GROUP)))
    qkv_grad, proj_grad, up_grad, down_grad, vector_grad, bias_grad = summed
    new_qkv, qkv_state = adam_step(qkv_weight, qkv_grad, qkv_moments, LR_MATRIX)
    new_proj, proj_state = adam_step(proj_weight, proj_grad, proj_moments, LR_MATRIX)
    new_up, up_state = adam_step(up_weight, up_grad, up_moments, LR_MATRIX)
    new_down, down_state = adam_step(down_weight, down_grad, down_moments, LR_MATRIX)
    new_vectors, vector_state = adam_step(vectors, vector_grad, vector_moments, LR_VECTOR)
    new_bias, bias_state = adam_step(up_bias, bias_grad, bias_moments, LR_VECTOR)
    return (out_rows.reshape(TOKENS, D), grad_rows.reshape(TOKENS, D), qkv_grad, proj_grad, up_grad, down_grad, vector_grad, bias_grad, new_qkv, new_proj, new_up, new_down, new_vectors, new_bias, qkv_state, proj_state, up_state, down_state, vector_state, bias_state)
```

```python
import math

import jax
import jax.numpy as jnp
import numpy as np
from jax import lax
from jax.experimental import pallas as pl
from jax.experimental.pallas import tpu as pltpu
from jax.sharding import PartitionSpec as P

D = 1600
HEADS = 25
HEAD_DIM = 64
STEP = 3

EPS_NORM = 1e-05
BETA_ONE = 0.9
BETA_TWO = 0.95
EPS_ADAM = 1e-08
LR_MATRIX = 0.08
LR_VECTOR = 0.3
DECAY = 0.1
NEG_FILL = -1e30
GELU_COEF = 0.7978845608028654
GELU_CUBE = 0.044715
UNIT = 16

F32 = jnp.float32
BF16 = jnp.bfloat16


def mm(spec, left, right):
    return jnp.einsum(spec, left, right, preferred_element_type=F32)


def adam_step(weight, gradient, moments, rate):
    first_moment = BETA_ONE * moments[0] + (1.0 - BETA_ONE) * gradient
    second = BETA_TWO * moments[1] + (1.0 - BETA_TWO) * gradient * gradient
    first_fix = 1.0 - BETA_ONE**STEP
    second_fix = 1.0 - BETA_TWO**STEP
    stepped = weight - rate * (
        first_moment / first_fix / (jnp.sqrt(second / second_fix) + EPS_ADAM) + DECAY * weight
    )
    return (stepped, jnp.stack([first_moment, second]))


def head_tables(rows, cols):
    slots = -(-HEADS // rows)
    per_block = 3 * D // cols // UNIT
    per_head = HEAD_DIM // UNIT
    lists = [[[] for _ in range(rows)] for _ in range(cols)]
    for g in range(3 * D // UNIT):
        head = (g // per_head) % HEADS
        lists[g // per_block][head % rows].append(g)
    longest = max(len(entry) for block in lists for entry in block)
    width = -(-longest // 8) * 8
    source = np.full((cols, rows, width * UNIT), -1, np.int32)
    unpack_block = np.full((rows, 3 * slots * per_head), -1, np.int32)
    unpack_rank = np.zeros((rows, 3 * slots * per_head), np.int32)
    pack_final = np.full((rows, cols, width), -1, np.int32)
    for c in range(cols):
        for z in range(rows):
            for rank, g in enumerate(lists[c][z]):
                local = g - c * per_block
                source[c, z, rank * UNIT : (rank + 1) * UNIT] = local * UNIT + np.arange(UNIT)
                part, head = g // per_head // HEADS, (g // per_head) % HEADS
                final = (part * slots + head // rows) * per_head + g % per_head
                unpack_block[z, final] = c
                unpack_rank[z, final] = rank
                pack_final[z, c, rank] = final
    return slots, width, source, unpack_block, unpack_rank, pack_final


def move_units(table, values, bias, out_rows, out_dtype):
    width = values.shape[1]
    count = out_rows // UNIT

    def body(tab, val, off, out):
        for i in range(count):
            src = tab[i]
            rows = pl.ds(i * UNIT, UNIT)
            safe = pl.multiple_of(jnp.maximum(src, 0) * UNIT, UNIT)
            block = val[pl.ds(safe, UNIT), :].astype(F32)
            block = jnp.where(src >= 0, block, 0.0)
            out[rows, :] = (block + off[rows, :]).astype(out_dtype)

    return pl.pallas_call(
        body,
        out_shape=jax.ShapeDtypeStruct((out_rows, width), out_dtype),
        in_specs=[
            pl.BlockSpec(memory_space=pltpu.SMEM),
            pl.BlockSpec(memory_space=pltpu.VMEM),
            pl.BlockSpec(memory_space=pltpu.VMEM),
        ],
        out_specs=pl.BlockSpec(memory_space=pltpu.VMEM),
        compiler_params=pltpu.CompilerParams(vmem_limit_bytes=32 * 2**20),
        name="move_units",
    )(table, values, bias)


def dot_tn(left, right):
    return lax.dot_general(left, right, (((0,), (0,)), ((), ())), preferred_element_type=F32)


def dot_nt(left, right):
    return lax.dot_general(left, right, (((1,), (1,)), ((), ())), preferred_element_type=F32)


def dot_nn(left, right):
    return lax.dot_general(left, right, (((1,), (0,)), ((), ())), preferred_element_type=F32)


def key_mask(block, me, start, keys, queries, diagonal):
    key_pos = block * keys + lax.broadcasted_iota(jnp.int32, (keys, queries), 0)
    mask = key_pos >= start
    if diagonal:
        query_pos = me * queries + lax.broadcasted_iota(jnp.int32, (keys, queries), 1)
        mask = mask & (key_pos <= query_pos)
    return mask


def attention_forward(me, start, query, key_values, offsets):
    rows, tokens = query.shape
    slots = rows // HEAD_DIM
    factor = 1.0 / math.sqrt(HEAD_DIM)
    n = len(offsets)

    def body(me_ref, start_ref, q_ref, *refs):
        kv, (o_ref, lse_ref), (top, total, acc) = refs[: 2 * n], refs[2 * n : 2 * n + 2], refs[2 * n + 2 :]
        my = me_ref[0]
        start_row = start_ref[...]
        q = q_ref[...] * jnp.asarray(factor, BF16)
        for i, off in enumerate(offsets):
            block = my ^ off
            k_ref, v_ref = kv[2 * i], kv[2 * i + 1]

            def run(first=(i == 0), off=off, block=block, k_ref=k_ref, v_ref=v_ref):
                s = dot_tn(k_ref[...], q)
                mask = key_mask(block, my, start_row, tokens, tokens, off == 0)
                s = jnp.where(mask, s, NEG_FILL)
                high = jnp.max(s, axis=0, keepdims=True)
                if not first:
                    high = jnp.maximum(high, top[...])
                p = jnp.exp(s - high)
                part = jnp.sum(p, axis=0, keepdims=True)
                mixed = dot_nn(v_ref[...], p.astype(BF16))
                if first:
                    total[...] = part
                    acc[...] = mixed
                else:
                    scale = jnp.exp(top[...] - high)
                    total[...] = total[...] * scale + part
                    acc[...] = acc[...] * scale + mixed
                top[...] = high

            if off == 0:
                run()
            else:
                pl.when(block < my)(run)
        o_ref[...] = (acc[...] / total[...]).astype(BF16)
        lse_ref[0] = top[...] + jnp.log(total[...])

    piece = (HEAD_DIM, tokens)
    specs = [
        pl.BlockSpec(memory_space=pltpu.SMEM),
        pl.BlockSpec((1, tokens), lambda j: (0, 0)),
        pl.BlockSpec(piece, lambda j: (j, 0)),
    ]
    args = [me, start, query]
    for array in key_values:
        specs += [pl.BlockSpec(piece, lambda j: (j, 0)), pl.BlockSpec(piece, lambda j: (slots + j, 0))]
        args += [array, array]
    return pl.pallas_call(
        body,
        grid=(slots,),
        in_specs=specs,
        out_specs=[
            pl.BlockSpec(piece, lambda j: (j, 0)),
            pl.BlockSpec((1, 1, tokens), lambda j: (j, 0, 0)),
        ],
        out_shape=[
            jax.ShapeDtypeStruct((rows, tokens), BF16),
            jax.ShapeDtypeStruct((slots, 1, tokens), F32),
        ],
        scratch_shapes=[
            pltpu.VMEM((1, tokens), F32),
            pltpu.VMEM((1, tokens), F32),
            pltpu.VMEM((HEAD_DIM, tokens), F32),
        ],
        compiler_params=pltpu.CompilerParams(vmem_limit_bytes=32 * 2**20),
        name="attention_forward",
    )(*args)


def attention_backward(me, start, query, key_values, offsets, out_rows, lse, grad_rows):
    rows, tokens = query.shape
    slots = rows // HEAD_DIM
    factor = 1.0 / math.sqrt(HEAD_DIM)
    n = len(offsets)

    def body(me_ref, start_ref, q_ref, o_ref, lse_ref, g_ref, *refs):
        kv, outs, (acc,) = refs[: 2 * n], refs[2 * n : -1], refs[-1:]
        dq_ref, dq_sum, dv_sum = outs[:3]
        grads = outs[3:]
        my = me_ref[0]
        start_row = start_ref[...]
        q = q_ref[...] * jnp.asarray(factor, BF16)
        g = g_ref[...]
        log_total = lse_ref[0]
        row_dot = jnp.sum(g.astype(F32) * o_ref[...].astype(F32), axis=0, keepdims=True)
        for i, off in enumerate(offsets):
            block = my ^ off
            k_ref, v_ref = kv[2 * i], kv[2 * i + 1]
            dk_ref, dv_ref = grads[2 * i], grads[2 * i + 1]

            def run(first=(i == 0), off=off, block=block, k_ref=k_ref, v_ref=v_ref, dk_ref=dk_ref, dv_ref=dv_ref):
                k = k_ref[...]
                s = dot_tn(k, q)
                mask = key_mask(block, my, start_row, tokens, tokens, off == 0)
                p = jnp.exp(jnp.where(mask, s, NEG_FILL) - log_total)
                dp = dot_tn(v_ref[...], g)
                ds = (p * (dp - row_dot)).astype(BF16)
                dv = dot_nt(g, p.astype(BF16))
                dv_ref[...] = dv.astype(BF16)
                dk_ref[...] = dot_nt(q, ds).astype(BF16)
                dq = dot_nn(k, ds)
                value_total = jnp.sum(dv, axis=1, keepdims=True)
                if first:
                    acc[...] = dq
                    dv_sum[...] = value_total
                else:
                    acc[...] += dq
                    dv_sum[...] += value_total

            def skip(dk_ref=dk_ref, dv_ref=dv_ref):
                dk_ref[...] = jnp.zeros_like(dk_ref)
                dv_ref[...] = jnp.zeros_like(dv_ref)

            if off == 0:
                run()
            else:
                pl.when(block < my)(run)
                pl.when(block >= my)(skip)
        dq = acc[...] * factor
        dq_ref[...] = dq.astype(BF16)
        dq_sum[...] = jnp.sum(dq, axis=1, keepdims=True)

    piece = (HEAD_DIM, tokens)
    head_spec = pl.BlockSpec(piece, lambda j: (j, 0))
    column = pl.BlockSpec((HEAD_DIM, 1), lambda j: (j, 0))
    specs = [
        pl.BlockSpec(memory_space=pltpu.SMEM),
        pl.BlockSpec((1, tokens), lambda j: (0, 0)),
        head_spec,
        head_spec,
        pl.BlockSpec((1, 1, tokens), lambda j: (j, 0, 0)),
        head_spec,
    ]
    args = [me, start, query, out_rows, lse, grad_rows]
    for array in key_values:
        specs += [head_spec, pl.BlockSpec(piece, lambda j: (slots + j, 0))]
        args += [array, array]
    full = jax.ShapeDtypeStruct((rows, tokens), BF16)
    thin = jax.ShapeDtypeStruct((rows, 1), F32)
    return pl.pallas_call(
        body,
        grid=(slots,),
        in_specs=specs,
        out_specs=[head_spec, column, column] + [head_spec] * (2 * n),
        out_shape=[full, thin, thin] + [full] * (2 * n),
        scratch_shapes=[pltpu.VMEM(piece, F32)],
        compiler_params=pltpu.CompilerParams(vmem_limit_bytes=32 * 2**20),
        name="attention_backward",
    )(*args)


def make_block(mesh):
    rows, dps, cols = mesh.shape["row"], mesh.shape["dp"], mesh.shape["col"]
    slots, width, source, unpack_block, unpack_rank, pack_final = head_tables(rows, cols)
    packed = width * UNIT
    offsets = list(range(0, cols, 2)) + list(range(1, cols, 2))
    even = [(d, b) for d in range(dps) for b in range(0, cols, 2)]
    plane = even + [(d, b + 1) for d, b in even]
    place = {entry: i for i, entry in enumerate(plane)}

    def to_row(values, k):
        return lax.ppermute(values, "row", [(i, (i + k) % rows) for i in range(rows)])

    def row_gather(values):
        return [values] + [to_row(values, rows - k) for k in range(1, rows)]

    def row_exchange(chunks):
        return [chunks[0]] + [to_row(chunks[rows - k], rows - k) for k in range(1, rows)]

    def row_reduce(chunks):
        total = chunks[0].astype(F32)
        for k in range(1, rows):
            total = total + to_row(chunks[k], k).astype(F32)
        return total

    def to_plane(values, d, b):
        return lax.ppermute(
            values,
            ("dp", "col"),
            [(y * cols + c, (y ^ d) * cols + (c ^ b)) for y in range(dps) for c in range(cols)],
        )

    def plane_gather(values):
        first = [values] + [to_plane(values, d, b) for d, b in even[1:]]
        return first + [to_plane(item, 0, 1) for item in first]

    def plane_reduce(pieces):
        half = len(even)
        sums = [
            pieces[i].astype(F32) + to_plane(pieces[half + i], 0, 1).astype(F32) for i in range(half)
        ]
        total = sums[0]
        for (d, b), item in list(zip(even, sums))[1:]:
            total = total + to_plane(item.astype(BF16), d, b).astype(F32)
        return total

    def dp_exchange(chunks):
        return [chunks[0]] + [
            lax.ppermute(chunks[d], "dp", [(y, y ^ d) for y in range(dps)]) for d in range(1, dps)
        ]

    def sum_everywhere(values):
        for axis, size in (("col", cols), ("dp", dps), ("row", rows)):
            step = 1
            while step < size:
                values = values + lax.ppermute(values, axis, [(i, i ^ step) for i in range(size)])
                step *= 2
        return values

    def sum_rows(values):
        step = 1
        while step < rows:
            values = values + lax.ppermute(values, "row", [(i, i ^ step) for i in range(rows)])
            step *= 2
        return values

    def at(array, index, axis=0):
        return lax.dynamic_index_in_dim(array, index, axis, keepdims=False)

    def per_device(
        hidden_in,
        upstream,
        segment_ids,
        qkv_weight,
        proj_weight,
        up_weight,
        down_weight,
        vectors,
        up_bias,
        qkv_moments,
        proj_moments,
        up_moments,
        down_moments,
        vector_moments,
        bias_moments,
    ):
        z, y, c = lax.axis_index("row"), lax.axis_index("dp"), lax.axis_index("col")
        tokens, feats = hidden_in.shape
        few = tokens // rows
        half = feats // dps
        hidden = down_weight.shape[0]
        group = segment_ids.shape[0]

        def swapped(blocks, axis):
            return jnp.stack([at(blocks, y ^ d, axis) for d in range(dps)], axis=axis)

        def rolled(array, axis):
            return jnp.stack([at(array, (z + k) % rows, axis) for k in range(rows)], axis=axis)

        def unrolled(pieces, axis):
            stacked = jnp.stack(pieces)
            return jnp.concatenate([at(stacked, (t - z) % rows) for t in range(rows)], axis=axis)

        def token_chunks(array):
            return [
                lax.dynamic_slice_in_dim(array, ((z + k) % rows) * few, few, array.ndim - 1)
                for k in range(rows)
            ]

        vec_rel = rolled(vectors.reshape(8, rows, feats), 1)
        vec_swap = swapped(vec_rel.reshape(8, rows, dps, half), 2).reshape(8, D)
        vec_rel = vec_rel.reshape(8, D)

        columns = rolled(at(jnp.asarray(source), c), 0).reshape(rows * packed)
        local_cols = qkv_weight.shape[1]
        select = (
            lax.broadcasted_iota(jnp.int32, (local_cols, rows * packed), 0) == columns[None, :]
        ).astype(BF16)
        sorted_cols = mm("fn,nm->fm", qkv_weight.astype(BF16), select).astype(BF16)
        arrived = row_exchange([sorted_cols[:, k * packed : (k + 1) * packed] for k in range(rows)])
        qkv_pieces = plane_gather(jnp.stack(arrived))
        w_qkv = jnp.stack(
            [
                jnp.concatenate([qkv_pieces[place[(d, b)]] for b in offsets], axis=2)
                for d in range(dps)
            ],
            axis=1,
        ).reshape(D, cols * packed)

        x_own = swapped(hidden_in.T.reshape(dps, half, tokens), 0).reshape(feats, tokens)
        x_all = jnp.concatenate(row_gather(x_own), axis=0)
        up_chunks = token_chunks(upstream.T)
        top_few = jnp.concatenate(row_exchange(up_chunks), axis=0)
        top_all = jnp.concatenate(plane_gather(top_few), axis=1)

        w_proj = jnp.concatenate(
            plane_gather(jnp.concatenate(row_gather(proj_weight.astype(BF16)), axis=1)), axis=0
        )
        up_parts = up_weight.astype(BF16).reshape(half, dps, hidden).transpose(1, 0, 2)
        up_arrived = dp_exchange([at(up_parts, y ^ d) for d in range(dps)])
        up_rows = swapped(jnp.stack(up_arrived), 0).reshape(feats, hidden)
        w_up = jnp.concatenate(row_gather(up_rows), axis=0)
        w_down = jnp.concatenate(row_gather(down_weight.astype(BF16)), axis=1)

        x_f = x_all.astype(F32)
        mean_one = jnp.mean(x_f, axis=0, keepdims=True)
        spread_one = jnp.mean(x_f * x_f, axis=0, keepdims=True) - mean_one * mean_one
        inverse_one = lax.rsqrt(spread_one + EPS_NORM)
        normed_one = (x_f - mean_one) * inverse_one
        h1 = (normed_one * vec_swap[0][:, None] + vec_swap[1][:, None]).astype(BF16)
        qkv_packed = mm("fn,ft->nt", w_qkv, h1)

        order = np.argsort(np.asarray(offsets)).astype(np.int32)
        where_block = at(jnp.asarray(unpack_block), z)
        unpack = jnp.where(
            where_block >= 0,
            jnp.asarray(order)[c ^ jnp.maximum(where_block, 0)] * width + at(jnp.asarray(unpack_rank), z),
            -1,
        )

        def own_heads(vector):
            padded = jnp.pad(vector, (0, (rows * slots - HEADS) * HEAD_DIM))
            return at(padded.reshape(slots, rows, HEAD_DIM), z, 1).reshape(slots * HEAD_DIM)

        wide = slots * HEAD_DIM
        shift = jnp.concatenate([own_heads(vectors[2]), jnp.zeros((wide,), F32), own_heads(vectors[3])])
        qkv_rows = move_units(unpack, qkv_packed, shift[:, None], 3 * wide, BF16)
        query = qkv_rows[:wide]
        own_kv = qkv_rows[wide:]

        held = [own_kv]
        for b in offsets[1 : cols // 2]:
            held.append(lax.ppermute(own_kv, "col", [(i, i ^ b) for i in range(cols) if (i ^ b) > i]))
        key_values = held + [
            lax.ppermute(item, "col", [(i, i ^ 1) for i in range(cols)]) for item in held
        ]
        me = c.astype(jnp.int32).reshape(1)
        query_ids = lax.dynamic_slice_in_dim(segment_ids, c * tokens, tokens)
        start = jnp.sum((segment_ids[:, None] < query_ids[None, :]).astype(jnp.int32), axis=0)[None, :]
        attn, lse = attention_forward(me, start, query, key_values, offsets)

        attn_pieces = row_exchange(token_chunks(attn))
        attn_abs = unrolled([item.reshape(slots, 1, HEAD_DIM, few) for item in attn_pieces], 1)
        attn_abs = attn_abs.reshape(rows * wide, few)[:D]
        blocks = attn_abs.reshape(cols, dps, D // cols // dps, few)
        attn_rel = jnp.concatenate([at(at(blocks, c ^ b), y ^ d) for d, b in plane], axis=0)
        x_few = lax.dynamic_slice_in_dim(x_all, z * few, few, 1)
        x_few = swapped(x_few.reshape(rows, dps, half, few), 1).reshape(D, few).astype(F32)
        mid = x_few + mm("rf,rt->ft", w_proj, attn_rel) + vec_rel[4][:, None]
        mean_two = jnp.mean(mid, axis=0, keepdims=True)
        spread_two = jnp.mean(mid * mid, axis=0, keepdims=True) - mean_two * mean_two
        inverse_two = lax.rsqrt(spread_two + EPS_NORM)
        normed_two = (mid - mean_two) * inverse_two
        h2 = (normed_two * vec_rel[5][:, None] + vec_rel[6][:, None]).astype(BF16)
        h2_all = jnp.concatenate(plane_gather(h2), axis=1)

        up_shift = lax.dynamic_slice_in_dim(up_bias, (c * dps + y) * hidden, hidden)
        pre = mm("fh,ft->ht", w_up, h2_all) + up_shift[:, None]
        inside = GELU_COEF * (pre + GELU_CUBE * pre * pre * pre)
        tanh_val = jnp.tanh(inside)
        act = (0.5 * pre * (1.0 + tanh_val)).astype(BF16)
        slope = 0.5 * (1.0 + tanh_val) + 0.5 * pre * (1.0 - tanh_val * tanh_val) * GELU_COEF * (
            1.0 + 3.0 * GELU_CUBE * pre * pre
        )
        grad_pre = mm("hf,ft->ht", w_down, top_all) * slope
        grad_pre_half = grad_pre.astype(BF16)
        bias_part = jnp.sum(grad_pre, axis=1)

        def by_plane(array):
            return [array[:, i * few : (i + 1) * few] for i in range(len(plane))]

        grad_ln_two = plane_reduce(by_plane(mm("fh,ht->ft", w_up, grad_pre_half).astype(BF16)))
        down_sum = plane_reduce(by_plane(mm("hf,ht->ft", w_down, act).astype(BF16)))
        out_few = (mid + down_sum + vec_rel[7][:, None]).astype(BF16)
        block_out = unrolled(
            row_exchange([out_few[k * feats : (k + 1) * feats] for k in range(rows)]), 1
        ).T

        down_part = mm("ht,ft->hf", act, top_all).astype(BF16)
        down_grad = row_reduce([down_part[:, k * feats : (k + 1) * feats] for k in range(rows)])
        up_part = mm("ft,ht->fh", h2_all, grad_pre_half).astype(BF16)
        up_sum = row_reduce([up_part[k * feats : (k + 1) * feats] for k in range(rows)]).astype(BF16)
        up_blocks = up_sum.reshape(dps, half, hidden)
        up_back = dp_exchange([at(up_blocks, y ^ d) for d in range(dps)])
        up_grad = swapped(jnp.stack(up_back), 0).transpose(1, 0, 2).reshape(half, dps * hidden).astype(F32)

        scaled = grad_ln_two * vec_rel[5][:, None]
        first_mean = jnp.mean(scaled, axis=0, keepdims=True)
        second_mean = jnp.mean(scaled * normed_two, axis=0, keepdims=True)
        grad_mid = top_few.astype(F32) + inverse_two * (scaled - first_mean - normed_two * second_mean)
        grad_mid_half = grad_mid.astype(BF16)
        grad_attn = mm("rf,ft->rt", w_proj, grad_mid_half).astype(BF16)
        n_rows = D // cols // dps
        natural = jnp.stack(
            [
                jnp.stack([grad_attn[place[(d, b)] * n_rows : (place[(d, b)] + 1) * n_rows] for d in range(dps)])
                for b in range(cols)
            ]
        )
        natural = swapped(natural, 1)
        grad_abs = jnp.stack([at(natural, c ^ b) for b in range(cols)]).reshape(D, few)
        grad_abs = jnp.pad(grad_abs, ((0, rows * wide - D), (0, 0))).reshape(slots, rows, HEAD_DIM, few)
        grad_heads = unrolled(
            row_exchange([at(grad_abs, (z + k) % rows, 1).reshape(wide, few) for k in range(rows)]), 1
        )
        proj_part = mm("rt,ft->rf", attn_rel, grad_mid_half).astype(BF16)
        proj_sum = plane_reduce([proj_part[i * n_rows : (i + 1) * n_rows] for i in range(len(plane))])
        proj_sum = proj_sum.astype(BF16)
        proj_grad = row_reduce([proj_sum[:, k * feats : (k + 1) * feats] for k in range(rows)])
        grad_mid_own = unrolled(
            row_exchange([grad_mid_half[k * feats : (k + 1) * feats] for k in range(rows)]), 1
        )

        results = attention_backward(me, start, query, key_values, offsets, attn, lse, grad_heads)
        grad_query, query_total, value_total = results[:3]
        kv_grads = [jnp.concatenate(results[3 + 2 * i : 5 + 2 * i], axis=0) for i in range(cols)]
        half_cols = cols // 2
        kv_sums = [
            kv_grads[i].astype(F32)
            + lax.ppermute(kv_grads[half_cols + i], "col", [(j, j ^ 1) for j in range(cols)]).astype(F32)
            for i in range(half_cols)
        ]
        own_sum = kv_sums[0]
        for i in range(1, half_cols):
            b = offsets[i]
            own_sum = own_sum + lax.ppermute(
                kv_sums[i].astype(BF16), "col", [(j, j ^ b) for j in range(cols) if (j ^ b) < j]
            ).astype(F32)
        grad_qkv = jnp.concatenate([grad_query, own_sum.astype(BF16)], axis=0)
        finals = at(jnp.asarray(pack_final), z)
        pack = jnp.concatenate([at(finals, c ^ b) for b in offsets])
        grad_packed = move_units(pack, grad_qkv, jnp.zeros((cols * packed, 1), F32), cols * packed, BF16)

        grad_ln_part = mm("fn,nt->ft", w_qkv, grad_packed)
        gain_one = vec_swap[0][:, None]
        scaled_part = grad_ln_part * gain_one
        stats = sum_rows(
            jnp.stack([jnp.sum(scaled_part, axis=0), jnp.sum(scaled_part * normed_one, axis=0)])
        )
        part_half = grad_ln_part.astype(BF16)
        grad_ln_own = row_reduce([part_half[k * feats : (k + 1) * feats] for k in range(rows)])
        first_row, second_row = stats[0:1] / D, stats[1:2] / D
        inner = inverse_one * (
            grad_ln_own * gain_one[:feats] - first_row - normed_one[:feats] * second_row
        )
        inner = swapped(inner.reshape(dps, half, tokens), 0).reshape(feats, tokens)
        input_grad = (grad_mid_own.astype(F32) + inner).astype(BF16).T

        qkv_part = mm("ft,nt->fn", h1, grad_packed).astype(BF16).reshape(rows, dps, half, cols * packed)
        qkv_sum = plane_reduce(
            [
                qkv_part[:, d, :, offsets.index(b) * packed : (offsets.index(b) + 1) * packed]
                for d, b in plane
            ]
        ).astype(BF16)
        qkv_back = jnp.concatenate(row_exchange([qkv_sum[k] for k in range(rows)]), axis=1)
        qkv_grad = mm("fm,nm->fn", qkv_back, select)

        def back_from_rel(vector):
            blocks = vector.reshape(rows, feats)
            return jnp.concatenate([at(blocks, (t - z) % rows) for t in range(rows)])

        def back_from_swap(vector):
            return back_from_rel(swapped(vector.reshape(rows, dps, half), 1).reshape(D))

        def from_heads(vector):
            blocks = vector.reshape(slots, 1, HEAD_DIM)
            mine = (jnp.arange(rows) == z)[None, :, None]
            return jnp.where(mine, blocks, 0.0).reshape(rows * wide)[:D]

        top_sum = jnp.sum(upstream.astype(F32), axis=0)
        parts = jnp.stack(
            [
                back_from_swap(jnp.sum(grad_ln_part * normed_one, axis=1)),
                back_from_swap(jnp.sum(grad_ln_part, axis=1)),
                from_heads(query_total[:, 0]),
                from_heads(value_total[:, 0]),
                back_from_rel(jnp.sum(grad_mid, axis=1)),
                back_from_rel(jnp.sum(grad_ln_two * normed_two, axis=1)),
                back_from_rel(jnp.sum(grad_ln_two, axis=1)),
                lax.dynamic_update_slice_in_dim(jnp.zeros((D,), F32), top_sum, z * feats, 0),
            ]
        )
        bias_full = lax.dynamic_update_slice_in_dim(
            jnp.zeros((up_bias.shape[0],), F32), bias_part, (c * dps + y) * hidden, 0
        )
        summed = sum_everywhere(jnp.concatenate([parts.reshape(-1), bias_full]))
        vector_grad = summed[: 8 * D].reshape(8, D)
        bias_grad = summed[8 * D :]

        new_qkv, qkv_state = adam_step(qkv_weight, qkv_grad, qkv_moments, LR_MATRIX)
        new_proj, proj_state = adam_step(proj_weight, proj_grad, proj_moments, LR_MATRIX)
        new_up, up_state = adam_step(up_weight, up_grad, up_moments, LR_MATRIX)
        new_down, down_state = adam_step(down_weight, down_grad, down_moments, LR_MATRIX)
        new_vectors, vector_state = adam_step(vectors, vector_grad, vector_moments, LR_VECTOR)
        new_bias, bias_state = adam_step(up_bias, bias_grad, bias_moments, LR_VECTOR)
        return (
            block_out,
            input_grad,
            qkv_grad,
            proj_grad,
            up_grad,
            down_grad,
            vector_grad,
            bias_grad,
            new_qkv,
            new_proj,
            new_up,
            new_down,
            new_vectors,
            new_bias,
            qkv_state,
            proj_state,
            up_state,
            down_state,
            vector_state,
            bias_state,
        )

    return per_device


def solution(mesh):
    acts = P(("dp", "col"), "row")
    wide = P(("row", "dp"), "col")
    tall = P(("col", "dp"), "row")
    wide_pair = P(None, ("row", "dp"), "col")
    tall_pair = P(None, ("col", "dp"), "row")
    return jax.shard_map(
        make_block(mesh),
        mesh=mesh,
        in_specs=(
            acts,
            acts,
            P("dp"),
            wide,
            tall,
            wide,
            tall,
            P(),
            P(),
            wide_pair,
            tall_pair,
            wide_pair,
            tall_pair,
            P(),
            P(),
        ),
        out_specs=(
            acts,
            acts,
            wide,
            tall,
            wide,
            tall,
            P(),
            P(),
            wide,
            tall,
            wide,
            tall,
            P(),
            P(),
            wide_pair,
            tall_pair,
            wide_pair,
            tall_pair,
            P(),
            P(),
        ),
        check_vma=False,
    )
```

```python
import math

import jax
import jax.numpy as jnp
import numpy as np
from jax import lax
from jax.experimental import pallas as pl
from jax.experimental.pallas import tpu as pltpu
from jax.sharding import PartitionSpec as P

D = 1600
HEADS = 25
HEAD_DIM = 64
STEP = 3

EPS_NORM = 1e-05
BETA_ONE = 0.9
BETA_TWO = 0.95
EPS_ADAM = 1e-08
LR_MATRIX = 0.08
LR_VECTOR = 0.3
DECAY = 0.1
NEG_FILL = -1e30
GELU_COEF = 0.7978845608028654
GELU_CUBE = 0.044715
UNIT = 16

F32 = jnp.float32
BF16 = jnp.bfloat16


def mm(spec, left, right):
    return jnp.einsum(spec, left, right, preferred_element_type=F32)


def adam_step(weight, gradient, moments, rate):
    first_moment = BETA_ONE * moments[0] + (1.0 - BETA_ONE) * gradient
    second = BETA_TWO * moments[1] + (1.0 - BETA_TWO) * gradient * gradient
    first_fix = 1.0 - BETA_ONE**STEP
    second_fix = 1.0 - BETA_TWO**STEP
    stepped = weight - rate * (
        first_moment / first_fix / (jnp.sqrt(second / second_fix) + EPS_ADAM) + DECAY * weight
    )
    return (stepped, jnp.stack([first_moment, second]))


def head_tables(rows, cols):
    slots = -(-HEADS // rows)
    per_block = 3 * D // cols // UNIT
    per_head = HEAD_DIM // UNIT
    lists = [[[] for _ in range(rows)] for _ in range(cols)]
    for g in range(3 * D // UNIT):
        head = (g // per_head) % HEADS
        lists[g // per_block][head % rows].append(g)
    longest = max(len(entry) for block in lists for entry in block)
    width = -(-longest // 8) * 8
    source = np.full((cols, rows, width * UNIT), -1, np.int32)
    unpack_block = np.full((rows, 3 * slots * per_head), -1, np.int32)
    unpack_rank = np.zeros((rows, 3 * slots * per_head), np.int32)
    pack_final = np.full((rows, cols, width), -1, np.int32)
    for c in range(cols):
        for z in range(rows):
            for rank, g in enumerate(lists[c][z]):
                local = g - c * per_block
                source[c, z, rank * UNIT : (rank + 1) * UNIT] = local * UNIT + np.arange(UNIT)
                part, head = g // per_head // HEADS, (g // per_head) % HEADS
                final = (part * slots + head // rows) * per_head + g % per_head
                unpack_block[z, final] = c
                unpack_rank[z, final] = rank
                pack_final[z, c, rank] = final
    return slots, width, source, unpack_block, unpack_rank, pack_final


def move_units(table, sources, bias, out_rows, out_dtype):
    width = sources[0].shape[1]
    units = sources[0].shape[0] // UNIT
    count = out_rows // UNIT

    def body(tab, *refs):
        vals, out = refs[: len(sources)], refs[-1]
        for i in range(count):
            src = tab[i]
            rows = pl.ds(i * UNIT, UNIT)
            block = jnp.zeros((UNIT, width), F32)
            for n, val in enumerate(vals):
                own = src - n * units
                safe = pl.multiple_of(jnp.clip(own, 0, units - 1) * UNIT, UNIT)
                inside = jnp.logical_and(own >= 0, own < units)
                block = jnp.where(inside, val[pl.ds(safe, UNIT), :].astype(F32), block)
            if bias is not None:
                block = block + refs[len(sources)][rows, :]
            out[rows, :] = block.astype(out_dtype)

    extra = [] if bias is None else [bias]
    return pl.pallas_call(
        body,
        out_shape=jax.ShapeDtypeStruct((out_rows, width), out_dtype),
        in_specs=[pl.BlockSpec(memory_space=pltpu.SMEM)]
        + [pl.BlockSpec(memory_space=pltpu.VMEM)] * (len(sources) + len(extra)),
        out_specs=pl.BlockSpec(memory_space=pltpu.VMEM),
        compiler_params=pltpu.CompilerParams(vmem_limit_bytes=32 * 2**20),
        name="move_units",
    )(table, *sources, *extra)


def qkv_product(weight, rows_in):
    dps, blocks, rows, packed = weight.shape
    tokens = rows_in.shape[2]

    def body(w_ref, h_ref, out):
        total = dot_tn(w_ref[0, 0], h_ref[0])
        for d in range(1, dps):
            total = total + dot_tn(w_ref[d, 0], h_ref[d])
        out[...] = total

    return pl.pallas_call(
        body,
        grid=(blocks,),
        in_specs=[
            pl.BlockSpec((dps, 1, rows, packed), lambda i: (0, i, 0, 0)),
            pl.BlockSpec((dps, rows, tokens), lambda i: (0, 0, 0)),
        ],
        out_specs=pl.BlockSpec((packed, tokens), lambda i: (i, 0)),
        out_shape=jax.ShapeDtypeStruct((blocks * packed, tokens), F32),
        compiler_params=pltpu.CompilerParams(vmem_limit_bytes=40 * 2**20),
        name="qkv_product",
    )(weight, rows_in)


def qkv_weight_part(rows_in, grads, blocks, packed):
    dps, rows, tokens = rows_in.shape

    def body(h_ref, g_ref, out):
        out[0, 0] = dot_nt(h_ref[0], g_ref[...]).astype(BF16)

    return pl.pallas_call(
        body,
        grid=(dps, blocks),
        in_specs=[
            pl.BlockSpec((1, rows, tokens), lambda d, i: (d, 0, 0)),
            pl.BlockSpec((packed, tokens), lambda d, i: (i, 0)),
        ],
        out_specs=pl.BlockSpec((1, 1, rows, packed), lambda d, i: (d, i, 0, 0)),
        out_shape=jax.ShapeDtypeStruct((dps, blocks, rows, packed), BF16),
        compiler_params=pltpu.CompilerParams(vmem_limit_bytes=40 * 2**20),
        name="qkv_weight_part",
    )(rows_in, grads)


def qkv_back(halves, grads, inputs, mean, inverse, gain, row_devices):
    dps, blocks, rows, packed = halves[0].shape
    tokens = inputs.shape[2]
    few = rows // row_devices

    def body(first, second, g_ref, x_ref, mean_ref, inv_ref, gain_ref, part, with_norm, plain, stats):
        total = None
        for n, w_ref in enumerate((first, second)):
            for i in range(blocks):
                start = (n * blocks + i) * packed
                term = dot_nn(w_ref[0, i], g_ref[start : start + packed, :])
                total = term if total is None else total + term
        normed = (x_ref[0].astype(F32) - mean_ref[...]) * inv_ref[...]
        product = total * normed
        with_norm[0] = jnp.sum(product, axis=1, keepdims=True)
        plain[0] = jnp.sum(total, axis=1, keepdims=True)
        weight = gain_ref[0]
        now = jnp.concatenate(
            [
                jnp.sum(total * weight, axis=0, keepdims=True),
                jnp.sum(product * weight, axis=0, keepdims=True),
            ],
            axis=0,
        )

        @pl.when(pl.program_id(0) == 0)
        def _():
            stats[...] = now

        @pl.when(pl.program_id(0) > 0)
        def _():
            stats[...] += now

        for k in range(row_devices):
            part[k, 0] = total[k * few : (k + 1) * few].astype(BF16)

    weight_spec = pl.BlockSpec((1, blocks, rows, packed), lambda d: (d, 0, 0, 0))
    row_spec = pl.BlockSpec((1, tokens), lambda d: (0, 0))
    column = pl.BlockSpec((1, rows, 1), lambda d: (d, 0, 0))
    return pl.pallas_call(
        body,
        grid=(dps,),
        in_specs=[
            weight_spec,
            weight_spec,
            pl.BlockSpec((2 * blocks * packed, tokens), lambda d: (0, 0)),
            pl.BlockSpec((1, rows, tokens), lambda d: (d, 0, 0)),
            row_spec,
            row_spec,
            column,
        ],
        out_specs=[
            pl.BlockSpec((row_devices, 1, few, tokens), lambda d: (0, d, 0, 0)),
            column,
            column,
            pl.BlockSpec((2, tokens), lambda d: (0, 0)),
        ],
        out_shape=[
            jax.ShapeDtypeStruct((row_devices, dps, few, tokens), BF16),
            jax.ShapeDtypeStruct((dps, rows, 1), F32),
            jax.ShapeDtypeStruct((dps, rows, 1), F32),
            jax.ShapeDtypeStruct((2, tokens), F32),
        ],
        compiler_params=pltpu.CompilerParams(vmem_limit_bytes=48 * 2**20),
        name="qkv_back",
    )(*halves, grads, inputs, mean, inverse, gain)


def dot_tn(left, right):
    return lax.dot_general(left, right, (((0,), (0,)), ((), ())), preferred_element_type=F32)


def dot_nt(left, right):
    return lax.dot_general(left, right, (((1,), (1,)), ((), ())), preferred_element_type=F32)


def dot_nn(left, right):
    return lax.dot_general(left, right, (((1,), (0,)), ((), ())), preferred_element_type=F32)


def key_mask(block, me, start, keys, queries, diagonal):
    key_pos = block * keys + lax.broadcasted_iota(jnp.int32, (keys, queries), 0)
    mask = key_pos >= start
    if diagonal:
        query_pos = me * queries + lax.broadcasted_iota(jnp.int32, (keys, queries), 1)
        mask = mask & (key_pos <= query_pos)
    return mask


def attention_forward(me, start, query, key_values, offsets):
    rows, tokens = query.shape
    slots = rows // HEAD_DIM
    factor = 1.0 / math.sqrt(HEAD_DIM)
    n = len(offsets)

    def body(me_ref, start_ref, q_ref, *refs):
        kv, (o_ref, lse_ref), (top, total, acc) = refs[: 2 * n], refs[2 * n : 2 * n + 2], refs[2 * n + 2 :]
        my = me_ref[0]
        start_row = start_ref[...]
        q = q_ref[...] * jnp.asarray(factor, BF16)
        for i, off in enumerate(offsets):
            block = my ^ off
            k_ref, v_ref = kv[2 * i], kv[2 * i + 1]

            def run(first=(i == 0), off=off, block=block, k_ref=k_ref, v_ref=v_ref):
                s = dot_tn(k_ref[...], q)
                mask = key_mask(block, my, start_row, tokens, tokens, off == 0)
                s = jnp.where(mask, s, NEG_FILL)
                high = jnp.max(s, axis=0, keepdims=True)
                if not first:
                    high = jnp.maximum(high, top[...])
                p = jnp.exp(s - high)
                part = jnp.sum(p, axis=0, keepdims=True)
                mixed = dot_nn(v_ref[...], p.astype(BF16))
                if first:
                    total[...] = part
                    acc[...] = mixed
                else:
                    scale = jnp.exp(top[...] - high)
                    total[...] = total[...] * scale + part
                    acc[...] = acc[...] * scale + mixed
                top[...] = high

            if off == 0:
                run()
            else:
                pl.when(block < my)(run)
        o_ref[...] = (acc[...] / total[...]).astype(BF16)
        lse_ref[0] = top[...] + jnp.log(total[...])

    piece = (HEAD_DIM, tokens)
    specs = [
        pl.BlockSpec(memory_space=pltpu.SMEM),
        pl.BlockSpec((1, tokens), lambda j: (0, 0)),
        pl.BlockSpec(piece, lambda j: (j, 0)),
    ]
    args = [me, start, query]
    for array in key_values:
        specs += [pl.BlockSpec(piece, lambda j: (j, 0)), pl.BlockSpec(piece, lambda j: (slots + j, 0))]
        args += [array, array]
    return pl.pallas_call(
        body,
        grid=(slots,),
        in_specs=specs,
        out_specs=[
            pl.BlockSpec(piece, lambda j: (j, 0)),
            pl.BlockSpec((1, 1, tokens), lambda j: (j, 0, 0)),
        ],
        out_shape=[
            jax.ShapeDtypeStruct((rows, tokens), BF16),
            jax.ShapeDtypeStruct((slots, 1, tokens), F32),
        ],
        scratch_shapes=[
            pltpu.VMEM((1, tokens), F32),
            pltpu.VMEM((1, tokens), F32),
            pltpu.VMEM((HEAD_DIM, tokens), F32),
        ],
        compiler_params=pltpu.CompilerParams(vmem_limit_bytes=32 * 2**20),
        name="attention_forward",
    )(*args)


def attention_backward(me, start, query, key_values, offsets, out_rows, lse, grad_rows):
    rows, tokens = query.shape
    slots = rows // HEAD_DIM
    factor = 1.0 / math.sqrt(HEAD_DIM)
    n = len(offsets)

    def body(me_ref, start_ref, q_ref, o_ref, lse_ref, g_ref, *refs):
        kv, outs, (acc,) = refs[: 2 * n], refs[2 * n : -1], refs[-1:]
        dq_ref, dq_sum, dv_sum = outs[:3]
        grads = outs[3:]
        my = me_ref[0]
        start_row = start_ref[...]
        q = q_ref[...] * jnp.asarray(factor, BF16)
        g = g_ref[...]
        log_total = lse_ref[0]
        row_dot = jnp.sum(g.astype(F32) * o_ref[...].astype(F32), axis=0, keepdims=True)
        for i, off in enumerate(offsets):
            block = my ^ off
            k_ref, v_ref = kv[2 * i], kv[2 * i + 1]
            dk_ref, dv_ref = grads[2 * i], grads[2 * i + 1]

            def run(first=(i == 0), off=off, block=block, k_ref=k_ref, v_ref=v_ref, dk_ref=dk_ref, dv_ref=dv_ref):
                k = k_ref[...]
                s = dot_tn(k, q)
                mask = key_mask(block, my, start_row, tokens, tokens, off == 0)
                p = jnp.exp(jnp.where(mask, s, NEG_FILL) - log_total)
                dp = dot_tn(v_ref[...], g)
                ds = (p * (dp - row_dot)).astype(BF16)
                dv = dot_nt(g, p.astype(BF16))
                dv_ref[...] = dv.astype(BF16)
                dk_ref[...] = dot_nt(q, ds).astype(BF16)
                dq = dot_nn(k, ds)
                value_total = jnp.sum(dv, axis=1, keepdims=True)
                if first:
                    acc[...] = dq
                    dv_sum[...] = value_total
                else:
                    acc[...] += dq
                    dv_sum[...] += value_total

            def skip(dk_ref=dk_ref, dv_ref=dv_ref):
                dk_ref[...] = jnp.zeros_like(dk_ref)
                dv_ref[...] = jnp.zeros_like(dv_ref)

            if off == 0:
                run()
            else:
                pl.when(block < my)(run)
                pl.when(block >= my)(skip)
        dq = acc[...] * factor
        dq_ref[...] = dq.astype(BF16)
        dq_sum[...] = jnp.sum(dq, axis=1, keepdims=True)

    piece = (HEAD_DIM, tokens)
    head_spec = pl.BlockSpec(piece, lambda j: (j, 0))
    column = pl.BlockSpec((HEAD_DIM, 1), lambda j: (j, 0))
    specs = [
        pl.BlockSpec(memory_space=pltpu.SMEM),
        pl.BlockSpec((1, tokens), lambda j: (0, 0)),
        head_spec,
        head_spec,
        pl.BlockSpec((1, 1, tokens), lambda j: (j, 0, 0)),
        head_spec,
    ]
    args = [me, start, query, out_rows, lse, grad_rows]
    for array in key_values:
        specs += [head_spec, pl.BlockSpec(piece, lambda j: (slots + j, 0))]
        args += [array, array]
    full = jax.ShapeDtypeStruct((rows, tokens), BF16)
    thin = jax.ShapeDtypeStruct((rows, 1), F32)
    return pl.pallas_call(
        body,
        grid=(slots,),
        in_specs=specs,
        out_specs=[head_spec, column, column] + [head_spec] * (2 * n),
        out_shape=[full, thin, thin] + [full] * (2 * n),
        scratch_shapes=[pltpu.VMEM(piece, F32)],
        compiler_params=pltpu.CompilerParams(vmem_limit_bytes=32 * 2**20),
        name="attention_backward",
    )(*args)


def make_block(mesh):
    rows, dps, cols = mesh.shape["row"], mesh.shape["dp"], mesh.shape["col"]
    slots, width, source, unpack_block, unpack_rank, pack_final = head_tables(rows, cols)
    packed = width * UNIT
    offsets = list(range(0, cols, 2)) + list(range(1, cols, 2))
    even = [(d, b) for d in range(dps) for b in range(0, cols, 2)]
    plane = even + [(d, b + 1) for d, b in even]

    def to_row(values, k):
        return lax.ppermute(values, "row", [(i, (i + k) % rows) for i in range(rows)])

    def row_gather(values):
        return [values] + [to_row(values, rows - k) for k in range(1, rows)]

    def row_exchange(chunks):
        return [chunks[0]] + [to_row(chunks[rows - k], rows - k) for k in range(1, rows)]

    def row_reduce(chunks):
        total = chunks[0].astype(F32)
        for k in range(1, rows):
            total = total + to_row(chunks[k], k).astype(F32)
        return total

    def to_plane(values, d, b):
        return lax.ppermute(
            values,
            ("dp", "col"),
            [(y * cols + c, (y ^ d) * cols + (c ^ b)) for y in range(dps) for c in range(cols)],
        )

    def plane_direct(values, axis):
        return jnp.concatenate([values] + [to_plane(values, d, b) for d, b in even[1:]], axis=axis)

    def plane_gather(values, axis):
        first = plane_direct(values, axis)
        return jnp.concatenate([first, to_plane(first, 0, 1)], axis=axis)

    def plane_reduce(near, far, axis):
        sums = near.astype(F32) + to_plane(far, 0, 1).astype(F32)
        size = sums.shape[axis] // len(even)
        parts = [lax.slice_in_dim(sums, i * size, (i + 1) * size, axis=axis) for i in range(len(even))]
        total = parts[0]
        for (d, b), item in list(zip(even, parts))[1:]:
            total = total + to_plane(item.astype(BF16), d, b).astype(F32)
        return total

    def dp_exchange(chunks):
        return [chunks[0]] + [
            lax.ppermute(chunks[d], "dp", [(y, y ^ d) for y in range(dps)]) for d in range(1, dps)
        ]

    def sum_rows(values):
        step = 1
        while step < rows:
            values = values + lax.ppermute(values, "row", [(i, i ^ step) for i in range(rows)])
            step *= 2
        return values

    def at(array, index, axis=0):
        return lax.dynamic_index_in_dim(array, index, axis, keepdims=False)

    def per_device(
        hidden_in,
        upstream,
        segment_ids,
        qkv_weight,
        proj_weight,
        up_weight,
        down_weight,
        vectors,
        up_bias,
        qkv_moments,
        proj_moments,
        up_moments,
        down_moments,
        vector_moments,
        bias_moments,
    ):
        z, y, c = lax.axis_index("row"), lax.axis_index("dp"), lax.axis_index("col")
        tokens, feats = hidden_in.shape
        few = tokens // rows
        half = feats // dps
        hidden = down_weight.shape[0]
        group = segment_ids.shape[0]

        def swapped(blocks, axis):
            return jnp.stack([at(blocks, y ^ d, axis) for d in range(dps)], axis=axis)

        def rolled(array, axis):
            return jnp.stack([at(array, (z + k) % rows, axis) for k in range(rows)], axis=axis)

        def unrolled(pieces, axis):
            stacked = jnp.stack(pieces)
            return jnp.concatenate([at(stacked, (t - z) % rows) for t in range(rows)], axis=axis)

        def token_chunks(array):
            return [
                lax.dynamic_slice_in_dim(array, ((z + k) % rows) * few, few, array.ndim - 1)
                for k in range(rows)
            ]

        vec_swap = swapped(rolled(vectors.reshape(8, rows, feats), 1).reshape(8, rows, dps, half), 2)
        vec_swap = vec_swap.transpose(0, 2, 1, 3).reshape(8, D)

        columns = rolled(at(jnp.asarray(source), c), 0).reshape(rows * packed)
        local_cols = qkv_weight.shape[1]
        select = (
            lax.broadcasted_iota(jnp.int32, (local_cols, rows * packed), 0) == columns[None, :]
        ).astype(BF16)
        sorted_cols = mm("fn,nm->fm", qkv_weight.astype(BF16), select).astype(BF16)
        arrived = row_exchange([sorted_cols[:, k * packed : (k + 1) * packed] for k in range(rows)])
        qkv_first = plane_direct(jnp.stack(arrived).reshape(1, rows * half, packed), 0)

        x_own = swapped(hidden_in.T.reshape(dps, half, tokens), 0)
        x_all = jnp.stack(row_gather(x_own), axis=1).reshape(dps, rows * half, tokens)
        up_parts = up_weight.astype(BF16).reshape(half, dps, hidden).transpose(1, 0, 2)
        up_arrived = dp_exchange([at(up_parts, y ^ d) for d in range(dps)])
        up_rows = swapped(jnp.stack(up_arrived), 0).reshape(feats, hidden)
        down_rows = down_weight.astype(BF16).T
        proj_own = proj_weight.astype(BF16)
        qkv_first, x_all, up_rows, down_rows, proj_own = lax.optimization_barrier(
            (qkv_first, x_all, up_rows, down_rows, proj_own)
        )
        qkv_second = to_plane(qkv_first, 0, 1)
        halves = [item.reshape(dps, cols // 2, rows * half, packed) for item in (qkv_first, qkv_second)]
        w_up = lax.all_gather(up_rows, "row", axis=0, tiled=True)
        w_down = lax.all_gather(down_rows, "row", axis=0, tiled=True)

        x_f = x_all.astype(F32).reshape(D, tokens)
        mean_one = jnp.mean(x_f, axis=0, keepdims=True)
        spread_one = jnp.mean(x_f * x_f, axis=0, keepdims=True) - mean_one * mean_one
        inverse_one = lax.rsqrt(spread_one + EPS_NORM)
        normed_one = (x_f - mean_one) * inverse_one
        h1 = (normed_one * vec_swap[0][:, None] + vec_swap[1][:, None]).astype(BF16)
        h1 = h1.reshape(dps, rows * half, tokens)
        qkv_packed = [qkv_product(item, h1) for item in halves]

        order = np.argsort(np.asarray(offsets)).astype(np.int32)
        where_block = at(jnp.asarray(unpack_block), z)
        unpack = jnp.where(
            where_block >= 0,
            jnp.asarray(order)[c ^ jnp.maximum(where_block, 0)] * width + at(jnp.asarray(unpack_rank), z),
            -1,
        )

        def own_heads(vector):
            padded = jnp.pad(vector, (0, (rows * slots - HEADS) * HEAD_DIM))
            return at(padded.reshape(slots, rows, HEAD_DIM), z, 1).reshape(slots * HEAD_DIM)

        wide = slots * HEAD_DIM
        shift = jnp.concatenate([own_heads(vectors[2]), jnp.zeros((wide,), F32), own_heads(vectors[3])])
        qkv_rows = move_units(unpack, qkv_packed, shift[:, None], 3 * wide, BF16)
        query = qkv_rows[:wide]
        own_kv = qkv_rows[wide:]

        held = [own_kv]
        for b in offsets[1 : cols // 2]:
            held.append(lax.ppermute(own_kv, "col", [(i, i ^ b) for i in range(cols) if (i ^ b) > i]))
        key_values = held + [
            lax.ppermute(item, "col", [(i, i ^ 1) for i in range(cols)]) for item in held
        ]
        key_values, upstream_late, proj_own = lax.optimization_barrier((key_values, upstream, proj_own))
        w_proj = plane_gather(unrolled(row_gather(proj_own), 1), 0)
        top_few = unrolled(row_exchange(token_chunks(upstream_late.T)), 0)
        top_all = plane_gather(top_few, 1)
        me = c.astype(jnp.int32).reshape(1)
        query_ids = lax.dynamic_slice_in_dim(segment_ids, c * tokens, tokens)
        start = jnp.sum((segment_ids[:, None] < query_ids[None, :]).astype(jnp.int32), axis=0)[None, :]
        attn, lse = attention_forward(me, start, query, key_values, offsets)


        n_rows = D // cols // dps
        attn_pieces = row_exchange(token_chunks(attn))
        attn_abs = unrolled([item.reshape(slots, 1, HEAD_DIM, few) for item in attn_pieces], 1)
        attn_abs = attn_abs.reshape(rows * wide, few)[:D]
        blocks = attn_abs.reshape(cols, dps, n_rows, few)
        attn_few = jnp.concatenate([at(at(blocks, c ^ b), y ^ d) for d, b in plane], axis=0)
        x_few = lax.dynamic_slice_in_dim(x_all, z * few, few, 2).reshape(dps, rows, half, few)
        x_few = swapped(x_few, 0).transpose(1, 0, 2, 3).reshape(rows, feats, few)
        x_few = unrolled([x_few[k] for k in range(rows)], 0).astype(F32)
        mid = x_few + mm("rf,rt->ft", w_proj, attn_few) + vectors[4][:, None]
        mean_two = jnp.mean(mid, axis=0, keepdims=True)
        spread_two = jnp.mean(mid * mid, axis=0, keepdims=True) - mean_two * mean_two
        inverse_two = lax.rsqrt(spread_two + EPS_NORM)
        normed_two = (mid - mean_two) * inverse_two
        h2 = (normed_two * vectors[5][:, None] + vectors[6][:, None]).astype(BF16)
        h2_all = plane_gather(h2, 1)

        up_shift = lax.dynamic_slice_in_dim(up_bias, (c * dps + y) * hidden, hidden)
        pre = mm("fh,ft->ht", w_up, h2_all) + up_shift[:, None]
        inside = GELU_COEF * (pre + GELU_CUBE * pre * pre * pre)
        tanh_val = jnp.tanh(inside)
        act = (0.5 * pre * (1.0 + tanh_val)).astype(BF16)
        slope = 0.5 * (1.0 + tanh_val) + 0.5 * pre * (1.0 - tanh_val * tanh_val) * GELU_COEF * (
            1.0 + 3.0 * GELU_CUBE * pre * pre
        )
        grad_pre = mm("fh,ft->ht", w_down, top_all) * slope
        grad_pre_half = grad_pre.astype(BF16)
        bias_part = jnp.sum(grad_pre, axis=1)

        middle = len(even) * few

        def features_back(weight, values):
            far = mm("fh,ht->ft", weight, values[:, middle:]).astype(BF16)
            near = mm("fh,ht->ft", weight, values[:, :middle]).astype(BF16)
            return plane_reduce(near, far, 1), (near, far)

        def row_chunks(array):
            return [lax.dynamic_slice_in_dim(array, ((z + k) % rows) * feats, feats, 0) for k in range(rows)]

        grad_ln_two, partial = features_back(w_up, grad_pre_half)

        scaled = grad_ln_two * vectors[5][:, None]
        first_mean = jnp.mean(scaled, axis=0, keepdims=True)
        second_mean = jnp.mean(scaled * normed_two, axis=0, keepdims=True)
        grad_mid = top_few.astype(F32) + inverse_two * (scaled - first_mean - normed_two * second_mean)
        grad_mid_half = grad_mid.astype(BF16)
        grad_attn = mm("rf,ft->rt", w_proj, grad_mid_half).astype(BF16)
        natural = grad_attn.reshape(2, dps, cols // 2, n_rows, few).transpose(2, 0, 1, 3, 4)
        natural = swapped(natural.reshape(cols, dps, n_rows, few), 1)
        grad_abs = jnp.stack([at(natural, c ^ b) for b in range(cols)]).reshape(D, few)
        grad_abs = jnp.pad(grad_abs, ((0, rows * wide - D), (0, 0))).reshape(slots, rows, HEAD_DIM, few)
        grad_heads = unrolled(
            row_exchange([at(grad_abs, (z + k) % rows, 1).reshape(wide, few) for k in range(rows)]), 1
        )

        act_late, pre_late, _ = lax.optimization_barrier((act, grad_pre_half, partial))
        down_part = mm("ft,ht->fh", top_all, act_late).astype(BF16)
        up_part = mm("ft,ht->fh", h2_all, pre_late).astype(BF16)
        act_late, _ = lax.optimization_barrier((act, grad_ln_two))
        down_sum, _ = features_back(w_down, act_late)
        out_few = (mid + down_sum + vectors[7][:, None]).astype(BF16)
        block_out = unrolled(row_exchange(row_chunks(out_few)), 1).T

        middle_rows = len(even) * n_rows
        proj_far = mm("rt,ft->rf", attn_few[middle_rows:], grad_mid_half).astype(BF16)
        proj_near = mm("rt,ft->rf", attn_few[:middle_rows], grad_mid_half).astype(BF16)
        grad_heads, proj_far, proj_near, down_part, up_part = lax.optimization_barrier(
            (grad_heads, proj_far, proj_near, down_part, up_part)
        )
        down_sum_part = lax.psum_scatter(down_part, "row", scatter_dimension=0, tiled=True)
        up_sum = lax.psum_scatter(up_part, "row", scatter_dimension=0, tiled=True)
        proj_sum = plane_reduce(proj_near, proj_far, 0).astype(BF16)
        proj_cols = proj_sum.reshape(n_rows, rows, feats).transpose(1, 0, 2)
        proj_grad = row_reduce([at(proj_cols, (z + k) % rows) for k in range(rows)])
        grad_mid_own = unrolled(row_exchange(row_chunks(grad_mid_half)), 1)

        results = attention_backward(me, start, query, key_values, offsets, attn, lse, grad_heads)
        grad_query, query_total, value_total = results[:3]
        kv_grads = [jnp.concatenate(results[3 + 2 * i : 5 + 2 * i], axis=0) for i in range(cols)]
        half_cols = cols // 2
        kv_sums = [
            kv_grads[i].astype(F32)
            + lax.ppermute(kv_grads[half_cols + i], "col", [(j, j ^ 1) for j in range(cols)]).astype(F32)
            for i in range(half_cols)
        ]
        own_sum = kv_sums[0]
        for i in range(1, half_cols):
            b = offsets[i]
            own_sum = own_sum + lax.ppermute(
                kv_sums[i].astype(BF16), "col", [(j, j ^ b) for j in range(cols) if (j ^ b) < j]
            ).astype(F32)
        grad_qkv = jnp.concatenate([grad_query, own_sum.astype(BF16)], axis=0)
        finals = at(jnp.asarray(pack_final), z)
        finals = jnp.concatenate([at(finals, c ^ b) for b in offsets])
        grad_packed = move_units(finals, [grad_qkv], None, cols * packed, BF16)

        gain_one = vec_swap[0].reshape(dps, rows * half, 1)
        part_half, sum_norm, sum_plain, stats = qkv_back(
            halves, grad_packed, x_all, mean_one, inverse_one, gain_one, rows
        )
        near_cols = cols // 2 * packed
        qkv_far = qkv_weight_part(h1, grad_packed[near_cols:], cols // 2, packed)
        qkv_near = qkv_weight_part(h1, grad_packed[:near_cols], cols // 2, packed)
        stats = sum_rows(stats)
        grad_ln_own = row_reduce([part_half[k] for k in range(rows)])
        first_row, second_row = stats[0:1] / D, stats[1:2] / D
        own_normed = normed_one.reshape(dps, rows, half, tokens)[:, 0]
        own_gain = gain_one.reshape(dps, rows, half, 1)[:, 0]
        inner = inverse_one * (grad_ln_own * own_gain - first_row - own_normed * second_row)
        inner = swapped(inner, 0).reshape(feats, tokens)
        input_grad = (grad_mid_own.astype(F32) + inner).astype(BF16).T

        flat = (dps * (cols // 2), rows * half, packed)
        qkv_sum = plane_reduce(qkv_near.reshape(flat), qkv_far.reshape(flat), 0)[0].astype(BF16)
        qkv_sum = qkv_sum.reshape(rows, half, packed)
        qkv_home = jnp.concatenate(row_exchange([qkv_sum[k] for k in range(rows)]), axis=1)
        qkv_grad = mm("fm,nm->fn", qkv_home, select)

        up_sum, down_sum_part, _ = lax.optimization_barrier((up_sum, down_sum_part, part_half))
        down_grad = down_sum_part.T.astype(F32)
        up_blocks = up_sum.reshape(dps, half, hidden)
        up_back = dp_exchange([at(up_blocks, y ^ d) for d in range(dps)])
        up_grad = swapped(jnp.stack(up_back), 0).transpose(1, 0, 2).reshape(half, dps * hidden).astype(F32)

        def back_from_rel(vector):
            blocks = vector.reshape(rows, feats)
            return jnp.concatenate([at(blocks, (t - z) % rows) for t in range(rows)])

        def back_from_swap(vector):
            return back_from_rel(swapped(vector.reshape(dps, rows, half), 0).transpose(1, 0, 2).reshape(D))

        def from_heads(vector):
            blocks = vector.reshape(slots, 1, HEAD_DIM)
            mine = (jnp.arange(rows) == z)[None, :, None]
            return jnp.where(mine, blocks, 0.0).reshape(rows * wide)[:D]

        top_sum = jnp.sum(upstream.astype(F32), axis=0)
        parts = jnp.stack(
            [
                back_from_swap(sum_norm),
                back_from_swap(sum_plain),
                from_heads(query_total[:, 0]),
                from_heads(value_total[:, 0]),
                jnp.sum(grad_mid, axis=1),
                jnp.sum(grad_ln_two * normed_two, axis=1),
                jnp.sum(grad_ln_two, axis=1),
                lax.dynamic_update_slice_in_dim(jnp.zeros((D,), F32), top_sum, z * feats, 0),
            ]
        )
        bias_full = lax.dynamic_update_slice_in_dim(
            jnp.zeros((up_bias.shape[0],), F32), bias_part, (c * dps + y) * hidden, 0
        )
        summed = lax.psum(jnp.concatenate([parts.reshape(-1), bias_full]), ("dp", "row", "col"))
        summed, _ = lax.optimization_barrier((summed, qkv_home))
        vector_grad = summed[: 8 * D].reshape(8, D)
        bias_grad = summed[8 * D :]

        new_qkv, qkv_state = adam_step(qkv_weight, qkv_grad, qkv_moments, LR_MATRIX)
        new_proj, proj_state = adam_step(proj_weight, proj_grad, proj_moments, LR_MATRIX)
        new_up, up_state = adam_step(up_weight, up_grad, up_moments, LR_MATRIX)
        new_down, down_state = adam_step(down_weight, down_grad, down_moments, LR_MATRIX)
        new_vectors, vector_state = adam_step(vectors, vector_grad, vector_moments, LR_VECTOR)
        new_bias, bias_state = adam_step(up_bias, bias_grad, bias_moments, LR_VECTOR)
        return (
            block_out,
            input_grad,
            qkv_grad,
            proj_grad,
            up_grad,
            down_grad,
            vector_grad,
            bias_grad,
            new_qkv,
            new_proj,
            new_up,
            new_down,
            new_vectors,
            new_bias,
            qkv_state,
            proj_state,
            up_state,
            down_state,
            vector_state,
            bias_state,
        )

    return per_device


def solution(mesh):
    acts = P(("dp", "col"), "row")
    wide = P(("row", "dp"), "col")
    tall = P(("col", "dp"), "row")
    wide_pair = P(None, ("row", "dp"), "col")
    tall_pair = P(None, ("col", "dp"), "row")
    return jax.shard_map(
        make_block(mesh),
        mesh=mesh,
        in_specs=(
            acts,
            acts,
            P("dp"),
            wide,
            tall,
            wide,
            tall,
            P(),
            P(),
            wide_pair,
            tall_pair,
            wide_pair,
            tall_pair,
            P(),
            P(),
        ),
        out_specs=(
            acts,
            acts,
            wide,
            tall,
            wide,
            tall,
            P(),
            P(),
            wide,
            tall,
            wide,
            tall,
            P(),
            P(),
            wide_pair,
            tall_pair,
            wide_pair,
            tall_pair,
            P(),
            P(),
        ),
        check_vma=False,
    )
```

```python
import math

import jax
import jax.numpy as jnp
import numpy as np
from jax import lax
from jax.experimental import pallas as pl
from jax.experimental.pallas import tpu as pltpu
from jax.sharding import PartitionSpec as P

D = 1600
HEADS = 25
HEAD_DIM = 64
STEP = 3

EPS_NORM = 1e-05
BETA_ONE = 0.9
BETA_TWO = 0.95
EPS_ADAM = 1e-08
LR_MATRIX = 0.08
LR_VECTOR = 0.3
DECAY = 0.1
NEG_FILL = -1e30
GELU_COEF = 0.7978845608028654
GELU_CUBE = 0.044715
UNIT = 16

F32 = jnp.float32
BF16 = jnp.bfloat16


def cost(micros):
    return pl.CostEstimate(
        flops=int(micros * 1.15e9), bytes_accessed=int(micros * 3.6e6), transcendentals=0
    )


def after(values, event):
    return lax.optimization_barrier((values, event))[0]


def mm(spec, left, right):
    return jnp.einsum(spec, left, right, preferred_element_type=F32)


def adam_terms(weight, gradient, first, second, rate):
    first_moment = BETA_ONE * first + (1.0 - BETA_ONE) * gradient
    second = BETA_TWO * second + (1.0 - BETA_TWO) * gradient * gradient
    first_fix = 1.0 - BETA_ONE**STEP
    second_fix = 1.0 - BETA_TWO**STEP
    stepped = weight - rate * (
        first_moment / first_fix / (jnp.sqrt(second / second_fix) + EPS_ADAM) + DECAY * weight
    )
    return stepped, first_moment, second


def adam_step(weight, gradient, moments, rate):
    stepped, first, second = adam_terms(weight, gradient, moments[0], moments[1], rate)
    return (stepped, jnp.stack([first, second]))


def adam_matrix(weight, gradient, moments):
    n, m = weight.shape
    step = next(size for size in (160, 80, 40, n) if n % size == 0 and size * m <= 160 * 512)

    def body(w_ref, g_ref, m_ref, new_ref, state_ref):
        new, first, second = adam_terms(w_ref[...], g_ref[...], m_ref[0], m_ref[1], LR_MATRIX)
        new_ref[...] = new
        state_ref[0] = first
        state_ref[1] = second

    block = pl.BlockSpec((step, m), lambda i: (i, 0))
    pair = pl.BlockSpec((2, step, m), lambda i: (0, i, 0))
    return pl.pallas_call(
        body,
        grid=(n // step,),
        in_specs=[block, block, pair],
        out_specs=[block, pair],
        out_shape=[jax.ShapeDtypeStruct((n, m), F32), jax.ShapeDtypeStruct((2, n, m), F32)],
        compiler_params=pltpu.CompilerParams(vmem_limit_bytes=32 * 2**20),
        cost_estimate=cost(3),
        name="adam_matrix",
    )(weight, gradient, moments)


def head_tables(rows, cols):
    slots = -(-HEADS // rows)
    per_block = 3 * D // cols // UNIT
    per_head = HEAD_DIM // UNIT
    lists = [[[] for _ in range(rows)] for _ in range(cols)]
    for g in range(3 * D // UNIT):
        head = (g // per_head) % HEADS
        lists[g // per_block][head % rows].append(g)
    longest = max(len(entry) for block in lists for entry in block)
    width = -(-longest // 8) * 8
    source = np.full((cols, rows, width * UNIT), -1, np.int32)
    unpack_block = np.full((rows, 3 * slots * per_head), -1, np.int32)
    unpack_rank = np.zeros((rows, 3 * slots * per_head), np.int32)
    pack_final = np.full((rows, cols, width), -1, np.int32)
    for c in range(cols):
        for z in range(rows):
            for rank, g in enumerate(lists[c][z]):
                local = g - c * per_block
                source[c, z, rank * UNIT : (rank + 1) * UNIT] = local * UNIT + np.arange(UNIT)
                part, head = g // per_head // HEADS, (g // per_head) % HEADS
                final = (part * slots + head // rows) * per_head + g % per_head
                unpack_block[z, final] = c
                unpack_rank[z, final] = rank
                pack_final[z, c, rank] = final
    return slots, width, source, unpack_block, unpack_rank, pack_final


def move_units(table, sources, bias, out_rows, out_dtype):
    width = sources[0].shape[1]
    units = sources[0].shape[0] // UNIT
    count = out_rows // UNIT

    def body(tab, *refs):
        vals, out = refs[: len(sources)], refs[-1]
        for i in range(count):
            src = tab[i]
            rows = pl.ds(i * UNIT, UNIT)
            block = jnp.zeros((UNIT, width), F32)
            for n, val in enumerate(vals):
                own = src - n * units
                safe = pl.multiple_of(jnp.clip(own, 0, units - 1) * UNIT, UNIT)
                inside = jnp.logical_and(own >= 0, own < units)
                block = jnp.where(inside, val[pl.ds(safe, UNIT), :].astype(F32), block)
            if bias is not None:
                block = block + refs[len(sources)][rows, :]
            out[rows, :] = block.astype(out_dtype)

    extra = [] if bias is None else [bias]
    return pl.pallas_call(
        body,
        out_shape=jax.ShapeDtypeStruct((out_rows, width), out_dtype),
        in_specs=[pl.BlockSpec(memory_space=pltpu.SMEM)]
        + [pl.BlockSpec(memory_space=pltpu.VMEM)] * (len(sources) + len(extra)),
        out_specs=pl.BlockSpec(memory_space=pltpu.VMEM),
        compiler_params=pltpu.CompilerParams(vmem_limit_bytes=32 * 2**20),
        cost_estimate=cost(3),
        name="move_units",
    )(table, *sources, *extra)


def qkv_product(weight, rows_in):
    dps, blocks, rows, packed = weight.shape
    tokens = rows_in.shape[2]

    def body(w_ref, h_ref, out):
        total = dot_tn(w_ref[0, 0], h_ref[0])
        for d in range(1, dps):
            total = total + dot_tn(w_ref[d, 0], h_ref[d])
        out[...] = total

    return pl.pallas_call(
        body,
        grid=(blocks,),
        in_specs=[
            pl.BlockSpec((dps, 1, rows, packed), lambda i: (0, i, 0, 0)),
            pl.BlockSpec((dps, rows, tokens), lambda i: (0, 0, 0)),
        ],
        out_specs=pl.BlockSpec((packed, tokens), lambda i: (i, 0)),
        out_shape=jax.ShapeDtypeStruct((blocks * packed, tokens), F32),
        compiler_params=pltpu.CompilerParams(vmem_limit_bytes=40 * 2**20),
        cost_estimate=cost(4),
        name="qkv_product",
    )(weight, rows_in)


def qkv_weight_part(rows_in, grads, blocks, packed):
    dps, rows, tokens = rows_in.shape

    def body(h_ref, g_ref, out):
        out[0, 0] = dot_nt(h_ref[0], g_ref[...]).astype(BF16)

    return pl.pallas_call(
        body,
        grid=(dps, blocks),
        in_specs=[
            pl.BlockSpec((1, rows, tokens), lambda d, i: (d, 0, 0)),
            pl.BlockSpec((packed, tokens), lambda d, i: (i, 0)),
        ],
        out_specs=pl.BlockSpec((1, 1, rows, packed), lambda d, i: (d, i, 0, 0)),
        out_shape=jax.ShapeDtypeStruct((dps, blocks, rows, packed), BF16),
        compiler_params=pltpu.CompilerParams(vmem_limit_bytes=40 * 2**20),
        cost_estimate=cost(4),
        name="qkv_weight_part",
    )(rows_in, grads)


def qkv_back(halves, grads, inputs, mean, inverse, gain, row_devices):
    dps, blocks, rows, packed = halves[0].shape
    tokens = inputs.shape[2]
    few = rows // row_devices

    def body(first, second, g_ref, x_ref, mean_ref, inv_ref, gain_ref, part, with_norm, plain, stats):
        total = None
        for n, w_ref in enumerate((first, second)):
            for i in range(blocks):
                start = (n * blocks + i) * packed
                term = dot_nn(w_ref[0, i], g_ref[start : start + packed, :])
                total = term if total is None else total + term
        normed = (x_ref[0].astype(F32) - mean_ref[...]) * inv_ref[...]
        product = total * normed
        with_norm[0] = jnp.sum(product, axis=1, keepdims=True)
        plain[0] = jnp.sum(total, axis=1, keepdims=True)
        weight = gain_ref[0]
        now = jnp.concatenate(
            [
                jnp.sum(total * weight, axis=0, keepdims=True),
                jnp.sum(product * weight, axis=0, keepdims=True),
            ],
            axis=0,
        )

        @pl.when(pl.program_id(0) == 0)
        def _():
            stats[...] = now

        @pl.when(pl.program_id(0) > 0)
        def _():
            stats[...] += now

        for k in range(row_devices):
            part[k, 0] = total[k * few : (k + 1) * few].astype(BF16)

    weight_spec = pl.BlockSpec((1, blocks, rows, packed), lambda d: (d, 0, 0, 0))
    row_spec = pl.BlockSpec((1, tokens), lambda d: (0, 0))
    column = pl.BlockSpec((1, rows, 1), lambda d: (d, 0, 0))
    return pl.pallas_call(
        body,
        grid=(dps,),
        in_specs=[
            weight_spec,
            weight_spec,
            pl.BlockSpec((2 * blocks * packed, tokens), lambda d: (0, 0)),
            pl.BlockSpec((1, rows, tokens), lambda d: (d, 0, 0)),
            row_spec,
            row_spec,
            column,
        ],
        out_specs=[
            pl.BlockSpec((row_devices, 1, few, tokens), lambda d: (0, d, 0, 0)),
            column,
            column,
            pl.BlockSpec((2, tokens), lambda d: (0, 0)),
        ],
        out_shape=[
            jax.ShapeDtypeStruct((row_devices, dps, few, tokens), BF16),
            jax.ShapeDtypeStruct((dps, rows, 1), F32),
            jax.ShapeDtypeStruct((dps, rows, 1), F32),
            jax.ShapeDtypeStruct((2, tokens), F32),
        ],
        compiler_params=pltpu.CompilerParams(vmem_limit_bytes=48 * 2**20),
        cost_estimate=cost(7),
        name="qkv_back",
    )(*halves, grads, inputs, mean, inverse, gain)


def dot_tn(left, right):
    return lax.dot_general(left, right, (((0,), (0,)), ((), ())), preferred_element_type=F32)


def dot_nt(left, right):
    return lax.dot_general(left, right, (((1,), (1,)), ((), ())), preferred_element_type=F32)


def dot_nn(left, right):
    return lax.dot_general(left, right, (((1,), (0,)), ((), ())), preferred_element_type=F32)


def key_mask(block, me, start, keys, queries, diagonal):
    key_pos = block * keys + lax.broadcasted_iota(jnp.int32, (keys, queries), 0)
    mask = key_pos >= start
    if diagonal:
        query_pos = me * queries + lax.broadcasted_iota(jnp.int32, (keys, queries), 1)
        mask = mask & (key_pos <= query_pos)
    return mask


def attention_forward(me, start, query, key_values, offsets, carried=None):
    rows, tokens = query.shape
    slots = rows // HEAD_DIM
    factor = 1.0 / math.sqrt(HEAD_DIM)
    n = len(offsets)
    fresh = carried is None

    def body(me_ref, start_ref, q_ref, *refs):
        kv, refs = refs[: 2 * n], refs[2 * n :]
        top, total, acc = refs[-3:]
        if not fresh:
            top[...] = refs[0][0]
            total[...] = refs[1][0]
            acc[...] = refs[2][...]
            refs = refs[3:]
        my = me_ref[0]
        start_row = start_ref[...]
        q = q_ref[...] * jnp.asarray(factor, BF16)
        for i, off in enumerate(offsets):
            block = my ^ off
            k_ref, v_ref = kv[2 * i], kv[2 * i + 1]

            def run(off=off, block=block, k_ref=k_ref, v_ref=v_ref):
                first = off == 0
                s = dot_tn(k_ref[...], q)
                mask = key_mask(block, my, start_row, tokens, tokens, off == 0)
                s = jnp.where(mask, s, NEG_FILL)
                high = jnp.max(s, axis=0, keepdims=True)
                if not first:
                    high = jnp.maximum(high, top[...])
                p = jnp.exp(s - high)
                part = jnp.sum(p, axis=0, keepdims=True)
                mixed = dot_nn(v_ref[...], p.astype(BF16))
                if first:
                    total[...] = part
                    acc[...] = mixed
                else:
                    scale = jnp.exp(top[...] - high)
                    total[...] = total[...] * scale + part
                    acc[...] = acc[...] * scale + mixed
                top[...] = high

            if off == 0:
                run()
            else:
                pl.when(block < my)(run)
        if fresh:
            refs[0][0] = top[...]
            refs[1][0] = total[...]
            refs[2][...] = acc[...]
        else:
            refs[0][...] = (acc[...] / total[...]).astype(BF16)
            refs[1][0] = top[...] + jnp.log(total[...])

    piece = (HEAD_DIM, tokens)
    head_spec = pl.BlockSpec(piece, lambda j: (j, 0))
    row_spec = pl.BlockSpec((1, 1, tokens), lambda j: (j, 0, 0))
    specs = [
        pl.BlockSpec(memory_space=pltpu.SMEM),
        pl.BlockSpec((1, tokens), lambda j: (0, 0)),
        head_spec,
    ]
    args = [me, start, query]
    for array in key_values:
        specs += [head_spec, pl.BlockSpec(piece, lambda j: (slots + j, 0))]
        args += [array, array]
    row_shape = jax.ShapeDtypeStruct((slots, 1, tokens), F32)
    if fresh:
        out_specs = [row_spec, row_spec, head_spec]
        out_shape = [row_shape, row_shape, jax.ShapeDtypeStruct((rows, tokens), F32)]
    else:
        specs += [row_spec, row_spec, head_spec]
        args += list(carried)
        out_specs = [head_spec, row_spec]
        out_shape = [jax.ShapeDtypeStruct((rows, tokens), BF16), row_shape]
    return pl.pallas_call(
        body,
        grid=(slots,),
        in_specs=specs,
        out_specs=out_specs,
        out_shape=out_shape,
        scratch_shapes=[
            pltpu.VMEM((1, tokens), F32),
            pltpu.VMEM((1, tokens), F32),
            pltpu.VMEM((HEAD_DIM, tokens), F32),
        ],
        compiler_params=pltpu.CompilerParams(vmem_limit_bytes=32 * 2**20),
        cost_estimate=cost(11),
        name="attention_forward",
    )(*args)


def attention_backward(me, start, query, key_values, offsets, out_rows, lse, grad_rows, carried=None):
    rows, tokens = query.shape
    slots = rows // HEAD_DIM
    factor = 1.0 / math.sqrt(HEAD_DIM)
    n = len(offsets)
    fresh = carried is None

    def body(me_ref, start_ref, q_ref, o_ref, lse_ref, g_ref, *refs):
        kv, refs = refs[: 2 * n], refs[2 * n :]
        acc, value_acc = refs[-2:]
        if fresh:
            acc[...] = jnp.zeros_like(acc)
        else:
            acc[...] = refs[0][...]
            refs = refs[1:]
        grads, (dv_sum, dq_ref), rest = refs[: 2 * n], refs[2 * n : 2 * n + 2], refs[2 * n + 2 : -2]
        value_acc[...] = jnp.zeros_like(value_acc)
        my = me_ref[0]
        start_row = start_ref[...]
        q = q_ref[...] * jnp.asarray(factor, BF16)
        g = g_ref[...]
        log_total = lse_ref[0]
        row_dot = jnp.sum(g.astype(F32) * o_ref[...].astype(F32), axis=0, keepdims=True)
        for i, off in enumerate(offsets):
            block = my ^ off
            k_ref, v_ref = kv[2 * i], kv[2 * i + 1]
            dk_ref, dv_ref = grads[2 * i], grads[2 * i + 1]

            def run(off=off, block=block, k_ref=k_ref, v_ref=v_ref, dk_ref=dk_ref, dv_ref=dv_ref):
                k = k_ref[...]
                s = dot_tn(k, q)
                mask = key_mask(block, my, start_row, tokens, tokens, off == 0)
                p = jnp.exp(jnp.where(mask, s, NEG_FILL) - log_total)
                dp = dot_tn(v_ref[...], g)
                ds = (p * (dp - row_dot)).astype(BF16)
                dv = dot_nt(g, p.astype(BF16))
                dv_ref[...] = dv.astype(BF16)
                dk_ref[...] = dot_nt(q, ds).astype(BF16)
                acc[...] += dot_nn(k, ds)
                value_acc[...] += jnp.sum(dv, axis=1, keepdims=True)

            def skip(dk_ref=dk_ref, dv_ref=dv_ref):
                dk_ref[...] = jnp.zeros_like(dk_ref)
                dv_ref[...] = jnp.zeros_like(dv_ref)

            if off == 0:
                run()
            else:
                pl.when(block < my)(run)
                pl.when(block >= my)(skip)
        dv_sum[...] = value_acc[...]
        if fresh:
            dq_ref[...] = acc[...]
        else:
            dq = acc[...] * factor
            dq_ref[...] = dq.astype(BF16)
            rest[0][...] = jnp.sum(dq, axis=1, keepdims=True)

    piece = (HEAD_DIM, tokens)
    head_spec = pl.BlockSpec(piece, lambda j: (j, 0))
    column = pl.BlockSpec((HEAD_DIM, 1), lambda j: (j, 0))
    specs = [
        pl.BlockSpec(memory_space=pltpu.SMEM),
        pl.BlockSpec((1, tokens), lambda j: (0, 0)),
        head_spec,
        head_spec,
        pl.BlockSpec((1, 1, tokens), lambda j: (j, 0, 0)),
        head_spec,
    ]
    args = [me, start, query, out_rows, lse, grad_rows]
    for array in key_values:
        specs += [head_spec, pl.BlockSpec(piece, lambda j: (slots + j, 0))]
        args += [array, array]
    full = jax.ShapeDtypeStruct((rows, tokens), BF16)
    thin = jax.ShapeDtypeStruct((rows, 1), F32)
    if fresh:
        out_specs, out_shape = [column, head_spec], [thin, jax.ShapeDtypeStruct((rows, tokens), F32)]
    else:
        specs += [head_spec]
        args += [carried]
        out_specs, out_shape = [column, head_spec, column], [thin, full, thin]
    return pl.pallas_call(
        body,
        grid=(slots,),
        in_specs=specs,
        out_specs=[head_spec] * (2 * n) + out_specs,
        out_shape=[full] * (2 * n) + out_shape,
        scratch_shapes=[pltpu.VMEM(piece, F32), pltpu.VMEM((HEAD_DIM, 1), F32)],
        compiler_params=pltpu.CompilerParams(vmem_limit_bytes=32 * 2**20),
        cost_estimate=cost(14),
        name="attention_backward",
    )(*args)


def make_block(mesh):
    rows, dps, cols = mesh.shape["row"], mesh.shape["dp"], mesh.shape["col"]
    slots, width, source, unpack_block, unpack_rank, pack_final = head_tables(rows, cols)
    packed = width * UNIT
    offsets = list(range(0, cols, 2)) + list(range(1, cols, 2))
    even = [(d, b) for d in range(dps) for b in range(0, cols, 2)]
    plane = even + [(d, b + 1) for d, b in even]

    def to_row(values, k):
        return lax.ppermute(values, "row", [(i, (i + k) % rows) for i in range(rows)])

    def row_gather(values):
        return [values] + [to_row(values, rows - k) for k in range(1, rows)]

    def row_exchange(chunks):
        return [chunks[0]] + [to_row(chunks[rows - k], rows - k) for k in range(1, rows)]

    def row_reduce(chunks):
        total = chunks[0].astype(F32)
        for k in range(1, rows):
            total = total + to_row(chunks[k], k).astype(F32)
        return total

    def to_plane(values, d, b):
        return lax.ppermute(
            values,
            ("dp", "col"),
            [(y * cols + c, (y ^ d) * cols + (c ^ b)) for y in range(dps) for c in range(cols)],
        )

    def plane_send(values):
        return [values] + [to_plane(values, d, b) for d, b in even[1:]]

    def core_send(far):
        return to_plane(far, 0, 1)

    def plane_scatter(near, far_received, axis):
        sums = near.astype(F32) + far_received.astype(F32)
        size = sums.shape[axis] // len(even)
        parts = [lax.slice_in_dim(sums, i * size, (i + 1) * size, axis=axis) for i in range(len(even))]
        return [parts[0]] + [to_plane(item.astype(BF16), d, b) for (d, b), item in list(zip(even, parts))[1:]]

    def total_of(terms):
        total = terms[0].astype(F32)
        for item in terms[1:]:
            total = total + item.astype(F32)
        return total

    def dp_exchange(chunks):
        return [chunks[0]] + [
            lax.ppermute(chunks[d], "dp", [(y, y ^ d) for y in range(dps)]) for d in range(1, dps)
        ]

    def sum_everywhere(values):
        for axis, size in (("row", rows), ("dp", dps), ("col", cols)):
            step = 1
            while step < size:
                values = values + lax.ppermute(values, axis, [(i, i ^ step) for i in range(size)])
                step *= 2
        return values

    def sum_rows(values):
        step = 1
        while step < rows:
            values = values + lax.ppermute(values, "row", [(i, i ^ step) for i in range(rows)])
            step *= 2
        return values

    def at(array, index, axis=0):
        return lax.dynamic_index_in_dim(array, index, axis, keepdims=False)

    def per_device(
        hidden_in,
        upstream,
        segment_ids,
        qkv_weight,
        proj_weight,
        up_weight,
        down_weight,
        vectors,
        up_bias,
        qkv_moments,
        proj_moments,
        up_moments,
        down_moments,
        vector_moments,
        bias_moments,
    ):
        z, y, c = lax.axis_index("row"), lax.axis_index("dp"), lax.axis_index("col")
        tokens, feats = hidden_in.shape
        few = tokens // rows
        half = feats // dps
        hidden = down_weight.shape[0]
        group = segment_ids.shape[0]

        def swapped(blocks, axis):
            return jnp.stack([at(blocks, y ^ d, axis) for d in range(dps)], axis=axis)

        def rolled(array, axis):
            return jnp.stack([at(array, (z + k) % rows, axis) for k in range(rows)], axis=axis)

        def unrolled(pieces, axis):
            stacked = jnp.stack(pieces)
            return jnp.concatenate([at(stacked, (t - z) % rows) for t in range(rows)], axis=axis)

        def chunks_of(array, axis):
            size = array.shape[axis] // rows
            return [
                lax.dynamic_slice_in_dim(array, ((z + k) % rows) * size, size, axis) for k in range(rows)
            ]

        vec_swap = swapped(rolled(vectors.reshape(8, rows, feats), 1).reshape(8, rows, dps, half), 2)
        vec_swap = vec_swap.transpose(0, 2, 1, 3).reshape(8, D)

        columns = rolled(at(jnp.asarray(source), c), 0).reshape(rows * packed)
        local_cols = qkv_weight.shape[1]
        select = (
            lax.broadcasted_iota(jnp.int32, (local_cols, rows * packed), 0) == columns[None, :]
        ).astype(BF16)
        sorted_cols = mm("fn,nm->fm", qkv_weight.astype(BF16), select).astype(BF16)
        arrived = row_exchange([sorted_cols[:, k * packed : (k + 1) * packed] for k in range(rows)])

        x_own = swapped(hidden_in.T.reshape(dps, half, tokens), 0)
        x_all = jnp.stack(row_gather(x_own), axis=1).reshape(dps, rows * half, tokens)
        up_parts = up_weight.astype(BF16).reshape(half, dps, hidden).transpose(1, 0, 2)
        up_arrived = dp_exchange([at(up_parts, y ^ d) for d in range(dps)])
        up_rows = swapped(jnp.stack(up_arrived), 0).reshape(feats, hidden)
        down_rows = down_weight.astype(BF16).T
        up_rows, down_rows, arrived = lax.optimization_barrier((up_rows, down_rows, arrived))
        qkv_first = jnp.concatenate(plane_send(jnp.stack(arrived).reshape(1, rows * half, packed)), axis=0)
        qkv_first, x_all = lax.optimization_barrier((qkv_first, x_all))
        qkv_second = core_send(qkv_first)
        halves = [item.reshape(dps, cols // 2, rows * half, packed) for item in (qkv_first, qkv_second)]
        w_up = lax.all_gather(up_rows, "row", axis=0, tiled=True)
        w_down = lax.all_gather(down_rows, "row", axis=0, tiled=True)
        proj_pieces = row_gather(after(proj_weight.astype(BF16), x_all))
        top_pieces = row_exchange(chunks_of(after(upstream, x_all), 0))

        x_f = x_all.astype(F32).reshape(D, tokens)
        mean_one = jnp.mean(x_f, axis=0, keepdims=True)
        spread_one = jnp.mean(x_f * x_f, axis=0, keepdims=True) - mean_one * mean_one
        inverse_one = lax.rsqrt(spread_one + EPS_NORM)
        normed_one = (x_f - mean_one) * inverse_one
        h1 = (normed_one * vec_swap[0][:, None] + vec_swap[1][:, None]).astype(BF16)
        h1 = h1.reshape(dps, rows * half, tokens)
        qkv_packed = [qkv_product(item, h1) for item in halves]

        order = np.argsort(np.asarray(offsets)).astype(np.int32)
        where_block = at(jnp.asarray(unpack_block), z)
        unpack = jnp.where(
            where_block >= 0,
            jnp.asarray(order)[c ^ jnp.maximum(where_block, 0)] * width + at(jnp.asarray(unpack_rank), z),
            -1,
        )

        def own_heads(vector):
            padded = jnp.pad(vector, (0, (rows * slots - HEADS) * HEAD_DIM))
            return at(padded.reshape(slots, rows, HEAD_DIM), z, 1).reshape(slots * HEAD_DIM)

        wide = slots * HEAD_DIM
        shift = jnp.concatenate([own_heads(vectors[2]), jnp.zeros((wide,), F32), own_heads(vectors[3])])
        qkv_rows = move_units(unpack, qkv_packed, shift[:, None], 3 * wide, BF16)
        query = qkv_rows[:wide]
        own_kv = qkv_rows[wide:]

        swap_cores = [(i, i ^ 1) for i in range(cols)]
        far_near = [
            lax.ppermute(own_kv, "col", [(i, i ^ b) for i in range(cols) if (i ^ b) > i])
            for b in range(2, cols, 2)
        ]
        near_kv = [own_kv, lax.ppermute(own_kv, "col", swap_cores)]
        near_offsets = [0, 1]
        far_offsets = list(range(2, cols, 2)) + list(range(3, cols, 2))
        me = c.astype(jnp.int32).reshape(1)
        query_ids = lax.dynamic_slice_in_dim(segment_ids, c * tokens, tokens)
        start = jnp.sum((segment_ids[:, None] < query_ids[None, :]).astype(jnp.int32), axis=0)[None, :]
        carried = attention_forward(me, start, query, near_kv, near_offsets)
        carried, far_near, proj_pieces, top_pieces = lax.optimization_barrier(
            (carried, far_near, proj_pieces, top_pieces)
        )
        far_kv = far_near + [lax.ppermute(item, "col", swap_cores) for item in far_near]
        proj_sent = plane_send(unrolled(proj_pieces, 1))
        top_few = unrolled(top_pieces, 1)
        attn, lse = attention_forward(me, start, query, far_kv, far_offsets, carried)
        attn, proj_sent = lax.optimization_barrier((attn, proj_sent))
        proj_first = jnp.concatenate(proj_sent, axis=0)
        w_proj = jnp.concatenate([proj_first, core_send(proj_first)], axis=0)
        top_sent = plane_send(after(top_few, proj_first))

        n_rows = D // cols // dps
        attn_pieces = row_exchange(chunks_of(attn, 1))
        attn_abs = unrolled([item.reshape(slots, 1, HEAD_DIM, few) for item in attn_pieces], 1)
        attn_abs = attn_abs.reshape(rows * wide, few)[:D]
        blocks = attn_abs.reshape(cols, dps, n_rows, few)
        attn_few = jnp.concatenate([at(at(blocks, c ^ b), y ^ d) for d, b in plane], axis=0)
        x_few = lax.dynamic_slice_in_dim(x_all, z * few, few, 2).reshape(dps, rows, half, few)
        x_few = swapped(x_few, 0).transpose(1, 0, 2, 3).reshape(rows, feats, few)
        x_few = unrolled([x_few[k] for k in range(rows)], 0).T.astype(F32)
        mid = x_few + mm("rt,rf->tf", attn_few, w_proj) + vectors[4]
        mean_two = jnp.mean(mid, axis=1, keepdims=True)
        spread_two = jnp.mean(mid * mid, axis=1, keepdims=True) - mean_two * mean_two
        inverse_two = lax.rsqrt(spread_two + EPS_NORM)
        normed_two = (mid - mean_two) * inverse_two
        h2 = (normed_two * vectors[5] + vectors[6]).astype(BF16)
        h2, top_sent = lax.optimization_barrier((h2, top_sent))
        top_first = jnp.concatenate(top_sent, axis=0)
        top_second = core_send(top_first)
        h2_first = jnp.concatenate(plane_send(h2), axis=0)
        h2_second = core_send(h2_first)

        up_shift = lax.dynamic_slice_in_dim(up_bias, (c * dps + y) * hidden, hidden)

        def hidden_part(h2_rows, top_rows):
            pre = mm("tf,fh->th", h2_rows, w_up) + up_shift
            inside = GELU_COEF * (pre + GELU_CUBE * pre * pre * pre)
            tanh_val = jnp.tanh(inside)
            act = (0.5 * pre * (1.0 + tanh_val)).astype(BF16)
            slope = 0.5 * (1.0 + tanh_val) + 0.5 * pre * (1.0 - tanh_val * tanh_val) * GELU_COEF * (
                1.0 + 3.0 * GELU_CUBE * pre * pre
            )
            grad_pre = mm("tf,fh->th", top_rows, w_down) * slope
            return act, grad_pre.astype(BF16), jnp.sum(grad_pre, axis=0)

        act_near, pre_near, bias_near = hidden_part(h2_first, top_first)
        act_far, pre_far, bias_far = hidden_part(h2_second, top_second)
        bias_part = bias_near + bias_far
        back_far = mm("th,fh->tf", pre_far, w_up).astype(BF16)
        back_near = mm("th,fh->tf", pre_near, w_up).astype(BF16)
        grad_ln_two = total_of(plane_scatter(back_near, core_send(back_far), 0))

        act_near, act_far, pre_near, pre_far, _ = lax.optimization_barrier(
            (act_near, act_far, pre_near, pre_far, back_near)
        )
        up_part = (mm("tf,th->fh", h2_first, pre_near) + mm("tf,th->fh", h2_second, pre_far)).astype(BF16)
        down_part = (mm("tf,th->fh", top_first, act_near) + mm("tf,th->fh", top_second, act_far)).astype(BF16)

        scaled = grad_ln_two * vectors[5]
        first_mean = jnp.mean(scaled, axis=1, keepdims=True)
        second_mean = jnp.mean(scaled * normed_two, axis=1, keepdims=True)
        grad_mid = top_few.astype(F32) + inverse_two * (scaled - first_mean - normed_two * second_mean)
        grad_mid_half = grad_mid.astype(BF16)
        grad_attn = mm("rf,tf->rt", w_proj, grad_mid_half).astype(BF16)
        natural = grad_attn.reshape(2, dps, cols // 2, n_rows, few).transpose(2, 0, 1, 3, 4)
        natural = swapped(natural.reshape(cols, dps, n_rows, few), 1)
        grad_abs = jnp.stack([at(natural, c ^ b) for b in range(cols)]).reshape(D, few)
        grad_abs = jnp.pad(grad_abs, ((0, rows * wide - D), (0, 0))).reshape(slots, rows, HEAD_DIM, few)
        grad_heads = unrolled(
            row_exchange([at(grad_abs, (z + k) % rows, 1).reshape(wide, few) for k in range(rows)]), 1
        )

        act_near, act_far = after((act_near, act_far), up_part)
        down_far = mm("th,fh->tf", act_far, w_down).astype(BF16)
        down_near = mm("th,fh->tf", act_near, w_down).astype(BF16)
        down_received = core_send(down_far)
        down_terms = plane_scatter(after(down_near, grad_ln_two), down_received, 0)
        middle_rows = len(even) * n_rows
        proj_far = mm("rt,tf->rf", attn_few[middle_rows:], grad_mid_half).astype(BF16)
        proj_near = mm("rt,tf->rf", attn_few[:middle_rows], grad_mid_half).astype(BF16)
        proj_received = core_send(proj_far)
        grad_heads, proj_received, proj_near, down_part, up_part, down_terms = lax.optimization_barrier(
            (grad_heads, proj_received, proj_near, down_part, up_part, down_terms)
        )
        up_sum = lax.psum_scatter(up_part, "row", scatter_dimension=0, tiled=True)
        down_sum_part = lax.psum_scatter(down_part, "row", scatter_dimension=0, tiled=True)
        out_few = (mid + total_of(down_terms) + vectors[7]).astype(BF16)
        proj_terms = plane_scatter(proj_near, proj_received, 0)
        mid_pieces = row_exchange(chunks_of(grad_mid_half, 1))

        far = attention_backward(me, start, query, far_kv, far_offsets, attn, lse, grad_heads)
        half_far = len(far_offsets) // 2
        far_grads = [jnp.concatenate(far[2 * i : 2 * i + 2], axis=0) for i in range(len(far_offsets))]
        far_value_total, carried_query = far[-2:]
        far_sent = []
        for i in range(half_far):
            b = far_offsets[i]
            both = far_grads[i].astype(F32) + lax.ppermute(far_grads[half_far + i], "col", swap_cores).astype(F32)
            far_sent.append(
                lax.ppermute(both.astype(BF16), "col", [(j, j ^ b) for j in range(cols) if (j ^ b) < j])
            )
        carried_query, mid_pieces = lax.optimization_barrier((carried_query, mid_pieces))
        grad_mid_own = unrolled(mid_pieces, 0)
        out_pieces = row_exchange(chunks_of(out_few, 1))
        near = attention_backward(
            me, start, query, near_kv, near_offsets, attn, lse, grad_heads, carried_query
        )
        near, far_sent, proj_terms, out_pieces = lax.optimization_barrier(
            (near, far_sent, proj_terms, out_pieces)
        )
        block_out = unrolled(out_pieces, 0)
        near_value_total, grad_query, query_total = near[-3:]
        value_total = near_value_total + far_value_total
        own_sum = jnp.concatenate(near[0:2], axis=0).astype(F32)
        own_sum = own_sum + lax.ppermute(jnp.concatenate(near[2:4], axis=0), "col", swap_cores).astype(F32)
        for item in far_sent:
            own_sum = own_sum + item.astype(F32)
        proj_sum = total_of(proj_terms).astype(BF16)
        grad_qkv = jnp.concatenate([grad_query, own_sum.astype(BF16)], axis=0)
        finals = at(jnp.asarray(pack_final), z)
        finals = jnp.concatenate([at(finals, c ^ b) for b in offsets])
        grad_packed = move_units(finals, [grad_qkv], None, cols * packed, BF16)
        proj_grad = row_reduce(chunks_of(proj_sum, 1))

        gain_one = vec_swap[0].reshape(dps, rows * half, 1)
        part_half, sum_norm, sum_plain, stats = qkv_back(
            halves, grad_packed, x_all, mean_one, inverse_one, gain_one, rows
        )
        near_cols = cols // 2 * packed
        qkv_far = qkv_weight_part(h1, grad_packed[near_cols:], cols // 2, packed)
        qkv_near = qkv_weight_part(h1, grad_packed[:near_cols], cols // 2, packed)
        stats = sum_rows(stats)
        grad_ln_own = row_reduce([part_half[k] for k in range(rows)])
        first_row, second_row = stats[0:1] / D, stats[1:2] / D
        own_normed = normed_one.reshape(dps, rows, half, tokens)[:, 0]
        own_gain = gain_one.reshape(dps, rows, half, 1)[:, 0]
        inner = inverse_one * (grad_ln_own * own_gain - first_row - own_normed * second_row)
        inner = swapped(inner, 0).reshape(feats, tokens).T
        input_grad = (grad_mid_own.astype(F32) + inner).astype(BF16)

        flat = (dps * (cols // 2), rows * half, packed)
        qkv_sum = total_of(plane_scatter(qkv_near.reshape(flat), core_send(qkv_far.reshape(flat)), 0))
        qkv_sum = qkv_sum[0].astype(BF16)
        qkv_sum = qkv_sum.reshape(rows, half, packed)
        qkv_home = jnp.concatenate(row_exchange([qkv_sum[k] for k in range(rows)]), axis=1)
        qkv_grad = mm("fm,nm->fn", qkv_home, select)

        up_sum, down_sum_part, _ = lax.optimization_barrier((up_sum, down_sum_part, part_half))
        up_blocks = up_sum.reshape(dps, half, hidden)
        up_back = dp_exchange([at(up_blocks, y ^ d) for d in range(dps)])
        up_grad = swapped(jnp.stack(up_back), 0).transpose(1, 0, 2).reshape(half, dps * hidden).astype(F32)

        def back_from_rel(vector):
            blocks = vector.reshape(rows, feats)
            return jnp.concatenate([at(blocks, (t - z) % rows) for t in range(rows)])

        def back_from_swap(vector):
            return back_from_rel(swapped(vector.reshape(dps, rows, half), 0).transpose(1, 0, 2).reshape(D))

        def from_heads(vector):
            blocks = vector.reshape(slots, 1, HEAD_DIM)
            mine = (jnp.arange(rows) == z)[None, :, None]
            return jnp.where(mine, blocks, 0.0).reshape(rows * wide)[:D]

        top_sum = jnp.sum(upstream.astype(F32), axis=0)
        parts = jnp.stack(
            [
                back_from_swap(sum_norm),
                back_from_swap(sum_plain),
                from_heads(query_total[:, 0]),
                from_heads(value_total[:, 0]),
                jnp.sum(grad_mid, axis=0),
                jnp.sum(grad_ln_two * normed_two, axis=0),
                jnp.sum(grad_ln_two, axis=0),
                lax.dynamic_update_slice_in_dim(jnp.zeros((D,), F32), top_sum, z * feats, 0),
            ]
        )
        bias_full = lax.dynamic_update_slice_in_dim(
            jnp.zeros((up_bias.shape[0],), F32), bias_part, (c * dps + y) * hidden, 0
        )
        summed = sum_everywhere(jnp.concatenate([parts.reshape(-1), bias_full]))
        vector_grad = summed[: 8 * D].reshape(8, D)
        bias_grad = summed[8 * D :]

        new_up, up_state = adam_matrix(up_weight, up_grad, up_moments)
        down_turned = down_sum_part.astype(F32)
        down_grad = down_turned.T
        new_down, down_state = adam_matrix(down_weight.T, down_turned, down_moments.transpose(0, 2, 1))
        new_down, down_state = new_down.T, down_state.transpose(0, 2, 1)
        new_proj, proj_state = adam_matrix(proj_weight, proj_grad, proj_moments)
        new_qkv, qkv_state = adam_matrix(qkv_weight, qkv_grad, qkv_moments)
        new_vectors, vector_state = adam_step(vectors, vector_grad, vector_moments, LR_VECTOR)
        new_bias, bias_state = adam_step(up_bias, bias_grad, bias_moments, LR_VECTOR)
        return (
            block_out,
            input_grad,
            qkv_grad,
            proj_grad,
            up_grad,
            down_grad,
            vector_grad,
            bias_grad,
            new_qkv,
            new_proj,
            new_up,
            new_down,
            new_vectors,
            new_bias,
            qkv_state,
            proj_state,
            up_state,
            down_state,
            vector_state,
            bias_state,
        )

    return per_device


def solution(mesh):
    acts = P(("dp", "col"), "row")
    wide = P(("row", "dp"), "col")
    tall = P(("col", "dp"), "row")
    wide_pair = P(None, ("row", "dp"), "col")
    tall_pair = P(None, ("col", "dp"), "row")
    return jax.shard_map(
        make_block(mesh),
        mesh=mesh,
        in_specs=(
            acts,
            acts,
            P("dp"),
            wide,
            tall,
            wide,
            tall,
            P(),
            P(),
            wide_pair,
            tall_pair,
            wide_pair,
            tall_pair,
            P(),
            P(),
        ),
        out_specs=(
            acts,
            acts,
            wide,
            tall,
            wide,
            tall,
            P(),
            P(),
            wide,
            tall,
            wide,
            tall,
            P(),
            P(),
            wide_pair,
            tall_pair,
            wide_pair,
            tall_pair,
            P(),
            P(),
        ),
        check_vma=False,
    )
```

```python
import math

import jax
import jax.numpy as jnp
import numpy as np
from jax import lax
from jax.experimental import pallas as pl
from jax.experimental.pallas import tpu as pltpu
from jax.sharding import PartitionSpec as P

D = 1600
HEADS = 25
HEAD_DIM = 64
STEP = 3

EPS_NORM = 1e-05
BETA_ONE = 0.9
BETA_TWO = 0.95
EPS_ADAM = 1e-08
LR_MATRIX = 0.08
LR_VECTOR = 0.3
DECAY = 0.1
NEG_FILL = -1e30
GELU_COEF = 0.7978845608028654
GELU_CUBE = 0.044715
UNIT = 16
WIDE = -(-D // 128) * 128

F32 = jnp.float32
BF16 = jnp.bfloat16


def cost(micros):
    return pl.CostEstimate(
        flops=int(micros * 0.35e9), bytes_accessed=int(micros * 1.1e6), transcendentals=0
    )


def after(values, event):
    return lax.optimization_barrier((values, event))[0]


def mm(spec, left, right):
    return jnp.einsum(spec, left, right, preferred_element_type=F32)


def adam_terms(weight, gradient, first, second, rate):
    first_moment = BETA_ONE * first + (1.0 - BETA_ONE) * gradient
    second = BETA_TWO * second + (1.0 - BETA_TWO) * gradient * gradient
    first_fix = 1.0 - BETA_ONE**STEP
    second_fix = 1.0 - BETA_TWO**STEP
    stepped = weight - rate * (
        first_moment / first_fix / (jnp.sqrt(second / second_fix) + EPS_ADAM) + DECAY * weight
    )
    return stepped, first_moment, second


def adam_step(weight, gradient, moments, rate):
    stepped, first, second = adam_terms(weight, gradient, moments[0], moments[1], rate)
    return (stepped, jnp.stack([first, second]))


def adam_matrix(weight, gradient, moments):
    n, m = weight.shape
    step = next(size for size in (160, 80, 40, n) if n % size == 0 and size * m <= 160 * 512)

    def body(w_ref, g_ref, m_ref, new_ref, state_ref):
        new, first, second = adam_terms(w_ref[...], g_ref[...], m_ref[0], m_ref[1], LR_MATRIX)
        new_ref[...] = new
        state_ref[0] = first
        state_ref[1] = second

    block = pl.BlockSpec((step, m), lambda i: (i, 0))
    pair = pl.BlockSpec((2, step, m), lambda i: (0, i, 0))
    return pl.pallas_call(
        body,
        grid=(n // step,),
        in_specs=[block, block, pair],
        out_specs=[block, pair],
        out_shape=[jax.ShapeDtypeStruct((n, m), F32), jax.ShapeDtypeStruct((2, n, m), F32)],
        compiler_params=pltpu.CompilerParams(vmem_limit_bytes=32 * 2**20),
        cost_estimate=cost(3),
        name="adam_matrix",
    )(weight, gradient, moments)


def head_tables(rows, cols):
    slots = -(-HEADS // rows)
    per_block = 3 * D // cols // UNIT
    per_head = HEAD_DIM // UNIT
    lists = [[[] for _ in range(rows)] for _ in range(cols)]
    for g in range(3 * D // UNIT):
        head = (g // per_head) % HEADS
        lists[g // per_block][head % rows].append(g)
    longest = max(len(entry) for block in lists for entry in block)
    width = -(-longest // 8) * 8
    source = np.full((cols, rows, width * UNIT), -1, np.int32)
    unpack_block = np.full((rows, 3 * slots * per_head), -1, np.int32)
    unpack_rank = np.zeros((rows, 3 * slots * per_head), np.int32)
    pack_final = np.full((rows, cols, width), -1, np.int32)
    for c in range(cols):
        for z in range(rows):
            for rank, g in enumerate(lists[c][z]):
                local = g - c * per_block
                source[c, z, rank * UNIT : (rank + 1) * UNIT] = local * UNIT + np.arange(UNIT)
                part, head = g // per_head // HEADS, (g // per_head) % HEADS
                final = (part * slots + head // rows) * per_head + g % per_head
                unpack_block[z, final] = c
                unpack_rank[z, final] = rank
                pack_final[z, c, rank] = final
    return slots, width, source, unpack_block, unpack_rank, pack_final


def row_tables(rows, dps, cols, slots, plane, n_rows, unit):
    per_head, per_block = HEAD_DIM // unit, n_rows // unit
    place = {entry: i for i, entry in enumerate(plane)}
    to_weight = np.zeros((rows, dps, cols, D // unit), np.int32)
    to_heads = np.full((rows, dps, cols, rows * slots * per_head), -1, np.int32)
    to_plain = np.zeros((rows, D // unit), np.int32)
    for z in range(rows):
        for y in range(dps):
            for c in range(cols):
                for a in range(D // unit):
                    head, q = a // per_head, a % per_head
                    k, j = (head - z) % rows, head // rows
                    n, i = a // per_block, a % per_block
                    in_heads = (k * slots + j) * per_head + q
                    in_weight = place[(y ^ (n % dps), c ^ (n // dps))] * per_block + i
                    to_weight[z, y, c, in_weight] = in_heads
                    to_heads[z, y, c, in_heads] = in_weight
                    to_plain[z, ((n % dps) * cols + n // dps) * per_block + i] = in_heads
    return to_weight, to_heads, to_plain


def move_units(table, sources, bias, out_rows, out_dtype):
    width = sources[0].shape[1]
    units = sources[0].shape[0] // UNIT
    count = out_rows // UNIT

    def body(tab, *refs):
        vals, out = refs[: len(sources)], refs[-1]
        for i in range(count):
            src = tab[i]
            rows = pl.ds(i * UNIT, UNIT)
            block = jnp.zeros((UNIT, width), F32)
            for n, val in enumerate(vals):
                own = src - n * units
                safe = pl.multiple_of(jnp.clip(own, 0, units - 1) * UNIT, UNIT)
                inside = jnp.logical_and(own >= 0, own < units)
                block = jnp.where(inside, val[pl.ds(safe, UNIT), :].astype(F32), block)
            if bias is not None:
                block = block + refs[len(sources)][rows, :]
            out[rows, :] = block.astype(out_dtype)

    extra = [] if bias is None else [bias]
    shape = jax.ShapeDtypeStruct((out_rows, width), out_dtype)
    return pl.pallas_call(
        body,
        grid=(1,),
        out_shape=shape,
        in_specs=[pl.BlockSpec(memory_space=pltpu.SMEM)] + [whole(item) for item in [*sources, *extra]],
        out_specs=whole(shape),
        compiler_params=pltpu.CompilerParams(vmem_limit_bytes=40 * 2**20),
        cost_estimate=cost(3),
        name="move_units",
    )(table, *sources, *extra)


def qkv_product(weight, rows_in):
    dps, blocks, rows, packed = weight.shape
    tokens = rows_in.shape[2]

    def body(w_ref, h_ref, out):
        total = dot_tn(w_ref[0, 0], h_ref[0])
        for d in range(1, dps):
            total = total + dot_tn(w_ref[d, 0], h_ref[d])
        out[...] = total

    return pl.pallas_call(
        body,
        grid=(blocks,),
        in_specs=[
            pl.BlockSpec((dps, 1, rows, packed), lambda i: (0, i, 0, 0)),
            pl.BlockSpec((dps, rows, tokens), lambda i: (0, 0, 0)),
        ],
        out_specs=pl.BlockSpec((packed, tokens), lambda i: (i, 0)),
        out_shape=jax.ShapeDtypeStruct((blocks * packed, tokens), F32),
        compiler_params=pltpu.CompilerParams(vmem_limit_bytes=40 * 2**20),
        cost_estimate=cost(4),
        name="qkv_product",
    )(weight, rows_in)


def qkv_weight_part(rows_in, grads, blocks, packed):
    dps, rows, tokens = rows_in.shape

    def body(h_ref, g_ref, out):
        out[0, 0] = dot_nt(h_ref[0], g_ref[...]).astype(BF16)

    return pl.pallas_call(
        body,
        grid=(dps, blocks),
        in_specs=[
            pl.BlockSpec((1, rows, tokens), lambda d, i: (d, 0, 0)),
            pl.BlockSpec((packed, tokens), lambda d, i: (i, 0)),
        ],
        out_specs=pl.BlockSpec((1, 1, rows, packed), lambda d, i: (d, i, 0, 0)),
        out_shape=jax.ShapeDtypeStruct((dps, blocks, rows, packed), BF16),
        compiler_params=pltpu.CompilerParams(vmem_limit_bytes=40 * 2**20),
        cost_estimate=cost(4),
        name="qkv_weight_part",
    )(rows_in, grads)


def qkv_back(halves, grads, inputs, mean, inverse, gain, row_devices):
    dps, blocks, rows, packed = halves[0].shape
    tokens = inputs.shape[2]
    few = rows // row_devices

    def body(first, second, g_ref, x_ref, mean_ref, inv_ref, gain_ref, part, with_norm, plain):
        total = None
        for n, w_ref in enumerate((first, second)):
            for i in range(blocks):
                start = (n * blocks + i) * packed
                term = dot_nn(w_ref[0, i], g_ref[start : start + packed, :])
                total = term if total is None else total + term
        normed = (x_ref[0].astype(F32) - mean_ref[...]) * inv_ref[...]
        product = total * normed
        with_norm[0] = jnp.sum(product, axis=1, keepdims=True)
        plain[0] = jnp.sum(total, axis=1, keepdims=True)
        weight = gain_ref[0]
        sums = []
        for item in (total, product):
            exact = jnp.sum(item * weight, axis=0, keepdims=True)
            rounded = exact.astype(BF16).astype(F32)
            sums += [rounded, exact - rounded]
        tail = jnp.concatenate(sums + [jnp.zeros((4, tokens), F32)], axis=0)
        for k in range(row_devices):
            block = jnp.concatenate([total[k * few : (k + 1) * few], tail], axis=0)
            part[k, 0] = block.astype(BF16)

    weight_spec = pl.BlockSpec((1, blocks, rows, packed), lambda d: (d, 0, 0, 0))
    row_spec = pl.BlockSpec((1, tokens), lambda d: (0, 0))
    column = pl.BlockSpec((1, rows, 1), lambda d: (d, 0, 0))
    return pl.pallas_call(
        body,
        grid=(dps,),
        in_specs=[
            weight_spec,
            weight_spec,
            pl.BlockSpec((2 * blocks * packed, tokens), lambda d: (0, 0)),
            pl.BlockSpec((1, rows, tokens), lambda d: (d, 0, 0)),
            row_spec,
            row_spec,
            column,
        ],
        out_specs=[
            pl.BlockSpec((row_devices, 1, few + 8, tokens), lambda d: (0, d, 0, 0)),
            column,
            column,
        ],
        out_shape=[
            jax.ShapeDtypeStruct((row_devices, dps, few + 8, tokens), BF16),
            jax.ShapeDtypeStruct((dps, rows, 1), F32),
            jax.ShapeDtypeStruct((dps, rows, 1), F32),
        ],
        compiler_params=pltpu.CompilerParams(vmem_limit_bytes=48 * 2**20),
        cost_estimate=cost(7),
        name="qkv_back",
    )(*halves, grads, inputs, mean, inverse, gain)


def whole(array):
    rank = len(array.shape)
    return pl.BlockSpec(tuple(array.shape), lambda i: (0,) * rank)


def dot_tn(left, right):
    return lax.dot_general(left, right, (((0,), (0,)), ((), ())), preferred_element_type=F32)


def dot_nt(left, right):
    return lax.dot_general(left, right, (((1,), (1,)), ((), ())), preferred_element_type=F32)


def dot_nn(left, right):
    return lax.dot_general(left, right, (((1,), (0,)), ((), ())), preferred_element_type=F32)


def rows_by_table(table, source, target, unit):
    def move(i, carry):
        src = table[i]
        block = source[pl.ds(pl.multiple_of(jnp.maximum(src, 0) * unit, unit), unit), :]
        target[pl.ds(pl.multiple_of(i * unit, unit), unit), :] = jnp.where(src >= 0, block, 0.0)
        return carry

    lax.fori_loop(0, target.shape[0] // unit, move, 0, unroll=8)


def project(table, plain_table, pieces, halves, x_rows, vecs, unit):
    few = pieces[0].shape[1]
    wide = pieces[0].shape[0]
    n, m = len(pieces), len(halves)

    def body(tab, plain_tab, *refs):
        parts, weights, refs = refs[:n], refs[n : n + m], refs[n + m :]
        (x_ref, vec), outs = refs[:2], refs[2:]
        rows_ref, mid_ref, h2_ref, mean_ref, inv_ref, source, target = outs
        for k in range(n):
            source[k * wide : (k + 1) * wide, :] = parts[k][...].astype(F32)
        rows_by_table(tab, source, target, unit)
        mid = x_ref[...].astype(F32) + vec[0:1, :]
        size = weights[0].shape[0]
        for i, weight in enumerate(weights):
            mid = mid + dot_tn(target[i * size : (i + 1) * size, :].astype(BF16), weight[...])
        mean = jnp.sum(mid, axis=1, keepdims=True) / D
        spread = jnp.sum(mid * mid, axis=1, keepdims=True) / D - mean * mean
        inverse = lax.rsqrt(spread + EPS_NORM)
        mid_ref[...] = mid
        h2_ref[...] = jnp.zeros_like(h2_ref)
        h2_ref[:, :D] = ((mid - mean) * inverse * vec[1:2, :] + vec[2:3, :]).astype(BF16)
        mean_ref[...] = mean
        inv_ref[...] = inverse
        rows_by_table(plain_tab, source, target, unit)
        rows_ref[...] = target[...].astype(BF16)

    args = [*pieces, *halves, x_rows, vecs]
    shapes = [
        jax.ShapeDtypeStruct((D, few), BF16),
        jax.ShapeDtypeStruct((few, D), F32),
        jax.ShapeDtypeStruct((few, WIDE), BF16),
        jax.ShapeDtypeStruct((few, 1), F32),
        jax.ShapeDtypeStruct((few, 1), F32),
    ]
    return pl.pallas_call(
        body,
        grid=(1,),
        in_specs=[pl.BlockSpec(memory_space=pltpu.SMEM)] * 2 + [whole(item) for item in args],
        out_specs=[whole(item) for item in shapes],
        out_shape=shapes,
        scratch_shapes=[pltpu.VMEM((n * wide, few), F32), pltpu.VMEM((D, few), F32)],
        compiler_params=pltpu.CompilerParams(vmem_limit_bytes=48 * 2**20),
        cost_estimate=cost(5),
        name="project",
    )(table, plain_table, *args)


def project_back(table, terms, top, mid, mean, inverse, gain, halves, out_rows, unit):
    few = top.shape[0]
    n, m = len(terms), len(halves)

    def body(tab, *refs):
        parts, (top_ref, mid_ref, mean_ref, inv_ref, gain_ref) = refs[:n], refs[n : n + 5]
        weights = refs[n + 5 : n + 5 + m]
        half_ref, heads_ref, sums_ref, source, target = refs[n + 5 + m :]
        grad = parts[0][:, :D].astype(F32)
        for part in parts[1:]:
            grad = grad + part[:, :D].astype(F32)
        inv = inv_ref[...]
        normed = (mid_ref[...] - mean_ref[...]) * inv
        scaled = grad * gain_ref[...]
        first_mean = jnp.sum(scaled, axis=1, keepdims=True) / D
        second_mean = jnp.sum(scaled * normed, axis=1, keepdims=True) / D
        out = top_ref[:, :D].astype(F32) + inv * (scaled - first_mean - normed * second_mean)
        half = out.astype(BF16)
        half_ref[...] = half
        sums_ref[0:1, :] = jnp.sum(out, axis=0, keepdims=True)
        sums_ref[1:2, :] = jnp.sum(grad * normed, axis=0, keepdims=True)
        sums_ref[2:3, :] = jnp.sum(grad, axis=0, keepdims=True)
        size = weights[0].shape[0]
        for i, weight in enumerate(weights):
            source[i * size : (i + 1) * size, :] = dot_nt(weight[...], half)
        rows_by_table(tab, source, target, unit)
        heads_ref[...] = target[...].astype(BF16)

    args = [*terms, top, mid, mean, inverse, gain, *halves]
    shapes = [
        jax.ShapeDtypeStruct((few, D), BF16),
        jax.ShapeDtypeStruct((out_rows, few), BF16),
        jax.ShapeDtypeStruct((3, D), F32),
    ]
    return pl.pallas_call(
        body,
        grid=(1,),
        in_specs=[pl.BlockSpec(memory_space=pltpu.SMEM)] + [whole(item) for item in args],
        out_specs=[whole(item) for item in shapes],
        out_shape=shapes,
        scratch_shapes=[pltpu.VMEM((D, few), F32), pltpu.VMEM((out_rows, few), F32)],
        compiler_params=pltpu.CompilerParams(vmem_limit_bytes=48 * 2**20),
        cost_estimate=cost(5),
        name="project_back",
    )(table, *args)


def hidden_units(h2_rows, top_rows, w_up, w_down, shift):
    tokens = h2_rows.shape[0]
    hidden = w_up.shape[1]
    step = min(tokens, 256)

    def body(h_ref, t_ref, up, down, shift_ref, act_ref, grad_ref, sum_ref):
        pre = dot_nn(h_ref[:, :D], up[...]) + shift_ref[...]
        square = pre * pre
        tanh_val = jnp.tanh(GELU_COEF * (pre + GELU_CUBE * pre * square))
        act_ref[...] = (0.5 * pre * (1.0 + tanh_val)).astype(BF16)
        slope = 0.5 * (1.0 + tanh_val) + 0.5 * pre * (1.0 - tanh_val * tanh_val) * GELU_COEF * (
            1.0 + 3.0 * GELU_CUBE * square
        )
        grad = dot_nn(t_ref[:, :D], down[...]) * slope
        grad_ref[...] = grad.astype(BF16)
        now = jnp.sum(grad, axis=0, keepdims=True)

        @pl.when(pl.program_id(0) == 0)
        def _():
            sum_ref[...] = now

        @pl.when(pl.program_id(0) > 0)
        def _():
            sum_ref[...] += now

    rows_in = pl.BlockSpec((step, WIDE), lambda i: (i, 0))
    weight = pl.BlockSpec((D, hidden), lambda i: (0, 0))
    rows_out = pl.BlockSpec((step, hidden), lambda i: (i, 0))
    line = pl.BlockSpec((1, hidden), lambda i: (0, 0))
    flat = jax.ShapeDtypeStruct((tokens, hidden), BF16)
    return pl.pallas_call(
        body,
        grid=(tokens // step,),
        in_specs=[rows_in, rows_in, weight, weight, line],
        out_specs=[rows_out, rows_out, line],
        out_shape=[flat, flat, jax.ShapeDtypeStruct((1, hidden), F32)],
        compiler_params=pltpu.CompilerParams(vmem_limit_bytes=44 * 2**20),
        cost_estimate=cost(6),
        name="hidden_units",
    )(h2_rows, top_rows, w_up, w_down, shift)


def features_back(grads, weight):
    tokens, hidden = grads.shape

    def body(g_ref, w_ref, out):
        out[...] = jnp.zeros_like(out)
        out[:, :D] = dot_nt(g_ref[...], w_ref[...]).astype(BF16)

    step = min(tokens, 256)
    return pl.pallas_call(
        body,
        grid=(tokens // step,),
        in_specs=[
            pl.BlockSpec((step, hidden), lambda i: (i, 0)),
            pl.BlockSpec((D, hidden), lambda i: (0, 0)),
        ],
        out_specs=pl.BlockSpec((step, WIDE), lambda i: (i, 0)),
        out_shape=jax.ShapeDtypeStruct((tokens, WIDE), BF16),
        compiler_params=pltpu.CompilerParams(vmem_limit_bytes=32 * 2**20),
        cost_estimate=cost(2),
        name="features_back",
    )(grads, weight)


def weight_part(rows_in, grads):
    n = len(rows_in)
    hidden = grads[0].shape[1]

    def body(*refs):
        parts, values, out = refs[:n], refs[n : 2 * n], refs[2 * n]
        for low in range(0, D, 256):
            lanes = slice(low, min(low + 256, D))
            total = dot_tn(parts[0][:, lanes], values[0][...])
            for part, value in zip(parts[1:], values[1:]):
                total = total + dot_tn(part[:, lanes], value[...])
            out[lanes, :] = total.astype(BF16)

    shape = jax.ShapeDtypeStruct((D, hidden), BF16)
    return pl.pallas_call(
        body,
        in_specs=[pl.BlockSpec(memory_space=pltpu.VMEM)] * (2 * n),
        out_specs=pl.BlockSpec(memory_space=pltpu.VMEM),
        out_shape=shape,
        compiler_params=pltpu.CompilerParams(vmem_limit_bytes=48 * 2**20),
        cost_estimate=cost(4),
        name="weight_part",
    )(*rows_in, *grads)


def finish(where, terms, x_own, mean, inverse, gain, sides):
    dps, half, tokens = x_own.shape
    feats = dps * half
    few = sides[0].shape[1]
    n = len(terms)

    def body(tab, *refs):
        parts, (x_ref, mean_ref, inv_ref, gain_ref) = refs[:n], refs[n : n + 4]
        side = refs[n + 4 : n + 4 + len(sides)]
        grad_ref, out_ref, held = refs[n + 4 + len(sides) :]
        for k, ref in enumerate(side):
            lanes = pl.ds(pl.multiple_of(tab[k], 128), few)
            held[:, lanes] = ref[:feats, :].astype(F32)
            out_ref[:, lanes] = ref[feats:, :]
        grads, stats = [], None
        for d in range(dps):
            total = parts[0][d].astype(F32)
            for part in parts[1:]:
                total = total + part[d].astype(F32)
            tail = total[half : half + 8]
            stats = tail if stats is None else stats + tail
            grads.append(total[:half])
        first_row = (stats[0:1] + stats[1:2]) / D
        second_row = (stats[2:3] + stats[3:4]) / D
        inv = inv_ref[...]
        inner = []
        for d in range(dps):
            normed = (x_ref[d].astype(F32) - mean_ref[...]) * inv
            inner.append(inv * (grads[d] * gain_ref[d] - first_row - normed * second_row))
        blocks = []
        for i in range(dps):
            block = inner[0]
            for d in range(1, dps):
                block = jnp.where((tab[len(sides)] ^ d) == i, inner[d], block)
            blocks.append(block)
        whole = jnp.concatenate(blocks, axis=0) if dps > 1 else blocks[0]
        grad_ref[...] = (held[...] + whole).astype(BF16)

    args = [*terms, x_own, mean, inverse, gain, *sides]
    flat = jax.ShapeDtypeStruct((feats, tokens), BF16)
    return pl.pallas_call(
        body,
        grid=(1,),
        in_specs=[pl.BlockSpec(memory_space=pltpu.SMEM)] + [whole(item) for item in args],
        out_specs=[whole(flat)] * 2,
        out_shape=[flat, flat],
        scratch_shapes=[pltpu.VMEM((feats, tokens), F32)],
        compiler_params=pltpu.CompilerParams(vmem_limit_bytes=40 * 2**20),
        cost_estimate=cost(4),
        name="finish",
    )(where, *args)


def key_mask(block, me, start, keys, queries, diagonal):
    key_pos = block * keys + lax.broadcasted_iota(jnp.int32, (keys, queries), 0)
    mask = key_pos >= start
    if diagonal:
        query_pos = me * queries + lax.broadcasted_iota(jnp.int32, (keys, queries), 1)
        mask = mask & (key_pos <= query_pos)
    return mask


def attention_forward(me, start, query, key_values, offsets, carried=None):
    rows, tokens = query.shape
    slots = rows // HEAD_DIM
    factor = 1.0 / math.sqrt(HEAD_DIM)
    n = len(offsets)
    fresh = carried is None

    def body(me_ref, start_ref, q_ref, *refs):
        kv, refs = refs[: 2 * n], refs[2 * n :]
        top, total, acc = refs[-3:]
        if not fresh:
            top[...] = refs[0][0]
            total[...] = refs[1][0]
            acc[...] = refs[2][...]
            refs = refs[3:]
        my = me_ref[0]
        start_row = start_ref[...]
        q = q_ref[...] * jnp.asarray(factor, BF16)
        for i, off in enumerate(offsets):
            block = my ^ off
            k_ref, v_ref = kv[2 * i], kv[2 * i + 1]

            def run(off=off, block=block, k_ref=k_ref, v_ref=v_ref):
                first = off == 0
                s = dot_tn(k_ref[...], q)
                mask = key_mask(block, my, start_row, tokens, tokens, off == 0)
                s = jnp.where(mask, s, NEG_FILL)
                high = jnp.max(s, axis=0, keepdims=True)
                if not first:
                    high = jnp.maximum(high, top[...])
                p = jnp.exp(s - high)
                part = jnp.sum(p, axis=0, keepdims=True)
                mixed = dot_nn(v_ref[...], p.astype(BF16))
                if first:
                    total[...] = part
                    acc[...] = mixed
                else:
                    scale = jnp.exp(top[...] - high)
                    total[...] = total[...] * scale + part
                    acc[...] = acc[...] * scale + mixed
                top[...] = high

            if off == 0:
                run()
            else:
                pl.when(block < my)(run)
        if fresh:
            refs[0][0] = top[...]
            refs[1][0] = total[...]
            refs[2][...] = acc[...]
        else:
            refs[0][...] = (acc[...] / total[...]).astype(BF16)
            refs[1][0] = top[...] + jnp.log(total[...])

    piece = (HEAD_DIM, tokens)
    head_spec = pl.BlockSpec(piece, lambda j: (j, 0))
    row_spec = pl.BlockSpec((1, 1, tokens), lambda j: (j, 0, 0))
    specs = [
        pl.BlockSpec(memory_space=pltpu.SMEM),
        pl.BlockSpec((1, tokens), lambda j: (0, 0)),
        head_spec,
    ]
    args = [me, start, query]
    for array in key_values:
        specs += [head_spec, pl.BlockSpec(piece, lambda j: (slots + j, 0))]
        args += [array, array]
    row_shape = jax.ShapeDtypeStruct((slots, 1, tokens), F32)
    if fresh:
        out_specs = [row_spec, row_spec, head_spec]
        out_shape = [row_shape, row_shape, jax.ShapeDtypeStruct((rows, tokens), F32)]
    else:
        specs += [row_spec, row_spec, head_spec]
        args += list(carried)
        out_specs = [head_spec, row_spec]
        out_shape = [jax.ShapeDtypeStruct((rows, tokens), BF16), row_shape]
    return pl.pallas_call(
        body,
        grid=(slots,),
        in_specs=specs,
        out_specs=out_specs,
        out_shape=out_shape,
        scratch_shapes=[
            pltpu.VMEM((1, tokens), F32),
            pltpu.VMEM((1, tokens), F32),
            pltpu.VMEM((HEAD_DIM, tokens), F32),
        ],
        compiler_params=pltpu.CompilerParams(vmem_limit_bytes=32 * 2**20),
        cost_estimate=cost(11),
        name="attention_forward",
    )(*args)


def attention_backward(me, start, query, key_values, offsets, out_rows, lse, grad_rows, carried=None):
    rows, tokens = query.shape
    slots = rows // HEAD_DIM
    factor = 1.0 / math.sqrt(HEAD_DIM)
    n = len(offsets)
    fresh = carried is None

    def body(me_ref, start_ref, q_ref, o_ref, lse_ref, g_ref, *refs):
        kv, refs = refs[: 2 * n], refs[2 * n :]
        acc, value_acc = refs[-2:]
        if fresh:
            acc[...] = jnp.zeros_like(acc)
        else:
            acc[...] = refs[0][...]
            refs = refs[1:]
        grads, (dv_sum, dq_ref), rest = refs[: 2 * n], refs[2 * n : 2 * n + 2], refs[2 * n + 2 : -2]
        value_acc[...] = jnp.zeros_like(value_acc)
        my = me_ref[0]
        start_row = start_ref[...]
        q = q_ref[...] * jnp.asarray(factor, BF16)
        g = g_ref[...]
        log_total = lse_ref[0]
        row_dot = jnp.sum(g.astype(F32) * o_ref[...].astype(F32), axis=0, keepdims=True)
        for i, off in enumerate(offsets):
            block = my ^ off
            k_ref, v_ref = kv[2 * i], kv[2 * i + 1]
            dk_ref, dv_ref = grads[2 * i], grads[2 * i + 1]

            def run(off=off, block=block, k_ref=k_ref, v_ref=v_ref, dk_ref=dk_ref, dv_ref=dv_ref):
                k = k_ref[...]
                s = dot_tn(k, q)
                mask = key_mask(block, my, start_row, tokens, tokens, off == 0)
                p = jnp.exp(jnp.where(mask, s, NEG_FILL) - log_total)
                dp = dot_tn(v_ref[...], g)
                ds = (p * (dp - row_dot)).astype(BF16)
                dv = dot_nt(g, p.astype(BF16))
                dv_ref[...] = dv.astype(BF16)
                dk_ref[...] = dot_nt(q, ds).astype(BF16)
                acc[...] += dot_nn(k, ds)
                value_acc[...] += jnp.sum(dv, axis=1, keepdims=True)

            def skip(dk_ref=dk_ref, dv_ref=dv_ref):
                dk_ref[...] = jnp.zeros_like(dk_ref)
                dv_ref[...] = jnp.zeros_like(dv_ref)

            if off == 0:
                run()
            else:
                pl.when(block < my)(run)
                pl.when(block >= my)(skip)
        dv_sum[...] = value_acc[...]
        if fresh:
            dq_ref[...] = acc[...]
        else:
            dq = acc[...] * factor
            dq_ref[...] = dq.astype(BF16)
            rest[0][...] = jnp.sum(dq, axis=1, keepdims=True)

    piece = (HEAD_DIM, tokens)
    head_spec = pl.BlockSpec(piece, lambda j: (j, 0))
    column = pl.BlockSpec((HEAD_DIM, 1), lambda j: (j, 0))
    specs = [
        pl.BlockSpec(memory_space=pltpu.SMEM),
        pl.BlockSpec((1, tokens), lambda j: (0, 0)),
        head_spec,
        head_spec,
        pl.BlockSpec((1, 1, tokens), lambda j: (j, 0, 0)),
        head_spec,
    ]
    args = [me, start, query, out_rows, lse, grad_rows]
    for array in key_values:
        specs += [head_spec, pl.BlockSpec(piece, lambda j: (slots + j, 0))]
        args += [array, array]
    full = jax.ShapeDtypeStruct((rows, tokens), BF16)
    thin = jax.ShapeDtypeStruct((rows, 1), F32)
    if fresh:
        out_specs, out_shape = [column, head_spec], [thin, jax.ShapeDtypeStruct((rows, tokens), F32)]
    else:
        specs += [head_spec]
        args += [carried]
        out_specs, out_shape = [column, head_spec, column], [thin, full, thin]
    return pl.pallas_call(
        body,
        grid=(slots,),
        in_specs=specs,
        out_specs=[head_spec] * (2 * n) + out_specs,
        out_shape=[full] * (2 * n) + out_shape,
        scratch_shapes=[pltpu.VMEM(piece, F32), pltpu.VMEM((HEAD_DIM, 1), F32)],
        compiler_params=pltpu.CompilerParams(vmem_limit_bytes=32 * 2**20),
        cost_estimate=cost(14),
        name="attention_backward",
    )(*args)


def make_block(mesh):
    rows, dps, cols = mesh.shape["row"], mesh.shape["dp"], mesh.shape["col"]
    slots, width, source, unpack_block, unpack_rank, pack_final = head_tables(rows, cols)
    packed = width * UNIT
    offsets = list(range(0, cols, 2)) + list(range(1, cols, 2))
    even = [(d, b) for d in range(dps) for b in range(0, cols, 2)]
    plane = even + [(d, b + 1) for d, b in even]

    n_rows = D // cols // dps
    wide = slots * HEAD_DIM
    unit = math.gcd(n_rows, 8)
    to_weight, to_heads, to_plain = row_tables(rows, dps, cols, slots, plane, n_rows, unit)

    def to_row(values, k):
        return lax.ppermute(values, "row", [(i, (i + k) % rows) for i in range(rows)])

    def row_gather(values):
        return [values] + [to_row(values, rows - k) for k in range(1, rows)]

    def row_exchange(chunks):
        return [chunks[0]] + [to_row(chunks[rows - k], rows - k) for k in range(1, rows)]

    def to_plane(values, d, b):
        return lax.ppermute(
            values,
            ("dp", "col"),
            [(y * cols + c, (y ^ d) * cols + (c ^ b)) for y in range(dps) for c in range(cols)],
        )

    def plane_send(values):
        return [values] + [to_plane(values, d, b) for d, b in even[1:]]

    def core_send(far):
        return to_plane(far, 0, 1)

    def plane_scatter(near, far_received, axis):
        sums = near.astype(F32) + far_received.astype(F32)
        size = sums.shape[axis] // len(even)
        parts = [lax.slice_in_dim(sums, i * size, (i + 1) * size, axis=axis) for i in range(len(even))]
        return [parts[0]] + [to_plane(item.astype(BF16), d, b) for (d, b), item in list(zip(even, parts))[1:]]

    def total_of(terms):
        total = terms[0].astype(F32)
        for item in terms[1:]:
            total = total + item.astype(F32)
        return total

    def dp_exchange(chunks):
        return [chunks[0]] + [
            lax.ppermute(chunks[d], "dp", [(y, y ^ d) for y in range(dps)]) for d in range(1, dps)
        ]

    def sum_everywhere(values):
        for axis, size in (("dp", dps), ("col", cols), ("row", rows)):
            step = 2 if axis == "col" else 1
            while step < size:
                values = values + lax.ppermute(values, axis, [(i, i ^ step) for i in range(size)])
                step *= 2
        return values

    def at(array, index, axis=0):
        return lax.dynamic_index_in_dim(array, index, axis, keepdims=False)

    def per_device(
        hidden_in,
        upstream,
        segment_ids,
        qkv_weight,
        proj_weight,
        up_weight,
        down_weight,
        vectors,
        up_bias,
        qkv_moments,
        proj_moments,
        up_moments,
        down_moments,
        vector_moments,
        bias_moments,
    ):
        z, y, c = lax.axis_index("row"), lax.axis_index("dp"), lax.axis_index("col")
        tokens, feats = hidden_in.shape
        few = tokens // rows
        half = feats // dps
        hidden = down_weight.shape[0]
        group = segment_ids.shape[0]

        def swapped(blocks, axis):
            return jnp.stack([at(blocks, y ^ d, axis) for d in range(dps)], axis=axis)

        def rolled(array, axis):
            return jnp.stack([at(array, (z + k) % rows, axis) for k in range(rows)], axis=axis)

        def unrolled(pieces, axis):
            stacked = jnp.stack(pieces)
            return jnp.concatenate([at(stacked, (t - z) % rows) for t in range(rows)], axis=axis)

        def chunks_of(array, axis):
            size = array.shape[axis] // rows
            return [
                lax.dynamic_slice_in_dim(array, ((z + k) % rows) * size, size, axis) for k in range(rows)
            ]

        me = c.astype(jnp.int32).reshape(1)
        weight_table = at(at(at(jnp.asarray(to_weight), z), y), c)
        heads_table = at(at(at(jnp.asarray(to_heads), z), y), c)

        vec_swap = swapped(rolled(vectors.reshape(8, rows, feats), 1).reshape(8, rows, dps, half), 2)
        vec_swap = vec_swap.transpose(0, 2, 1, 3).reshape(8, D)
        query_ids = lax.dynamic_slice_in_dim(segment_ids, c * tokens, tokens)
        start = jnp.sum((segment_ids[:, None] < query_ids[None, :]).astype(jnp.int32), axis=0)[None, :]

        columns = rolled(at(jnp.asarray(source), c), 0).reshape(rows * packed)
        local_cols = qkv_weight.shape[1]
        select = (
            lax.broadcasted_iota(jnp.int32, (local_cols, rows * packed), 0) == columns[None, :]
        ).astype(BF16)
        sorted_cols = mm("fn,nm->fm", qkv_weight.astype(BF16), select).astype(BF16)
        arrived = row_exchange([sorted_cols[:, k * packed : (k + 1) * packed] for k in range(rows)])
        up_parts = up_weight.astype(BF16).reshape(half, dps, hidden).transpose(1, 0, 2)
        up_arrived = dp_exchange([at(up_parts, y ^ d) for d in range(dps)])
        up_rows = swapped(jnp.stack(up_arrived), 0).reshape(feats, hidden)
        arrived, up_rows, down_rows = lax.optimization_barrier((arrived, up_rows, down_weight.astype(BF16).T))

        x_own = swapped(hidden_in.T.reshape(dps, half, tokens), 0)
        qkv_sent = plane_send(jnp.stack(arrived).reshape(1, rows * half, packed))
        x_pieces = row_gather(x_own)
        qkv_sent, x_pieces, proj_own, upstream_late, up_rows, down_rows = lax.optimization_barrier(
            (qkv_sent, x_pieces, proj_weight.astype(BF16), upstream, up_rows, down_rows)
        )
        w_up = lax.all_gather(up_rows, "row", axis=0, tiled=True)
        w_down = lax.all_gather(down_rows, "row", axis=0, tiled=True)

        proj_pieces = row_gather(proj_own)
        qkv_first = jnp.concatenate(qkv_sent, axis=0)
        qkv_second = core_send(qkv_first)
        halves = [item.reshape(dps, cols // 2, rows * half, packed) for item in (qkv_first, qkv_second)]
        x_all = jnp.stack(x_pieces, axis=1).reshape(dps, rows * half, tokens)
        x_f = x_all.astype(F32).reshape(D, tokens)
        mean_one = jnp.mean(x_f, axis=0, keepdims=True)
        spread_one = jnp.mean(x_f * x_f, axis=0, keepdims=True) - mean_one * mean_one
        inverse_one = lax.rsqrt(spread_one + EPS_NORM)
        h1 = ((x_f - mean_one) * inverse_one * vec_swap[0][:, None] + vec_swap[1][:, None]).astype(BF16)
        h1 = h1.reshape(dps, rows * half, tokens)
        qkv_packed = [qkv_product(item, h1) for item in halves]

        order = np.argsort(np.asarray(offsets)).astype(np.int32)
        where_block = at(jnp.asarray(unpack_block), z)
        unpack = jnp.where(
            where_block >= 0,
            jnp.asarray(order)[c ^ jnp.maximum(where_block, 0)] * width + at(jnp.asarray(unpack_rank), z),
            -1,
        )

        def own_heads(vector):
            padded = jnp.pad(vector, (0, (rows * slots - HEADS) * HEAD_DIM))
            return at(padded.reshape(slots, rows, HEAD_DIM), z, 1).reshape(wide)

        shift = jnp.concatenate([own_heads(vectors[2]), jnp.zeros((wide,), F32), own_heads(vectors[3])])
        qkv_rows = move_units(unpack, qkv_packed, shift[:, None], 3 * wide, BF16)
        qkv_rows, proj_pieces = lax.optimization_barrier((qkv_rows, proj_pieces))

        query, own_kv = qkv_rows[:wide], qkv_rows[wide:]
        swap_cores = [(i, i ^ 1) for i in range(cols)]
        near_offsets = [0, 1]
        far_offsets = list(range(2, cols, 2)) + list(range(3, cols, 2))
        far_near = [
            lax.ppermute(own_kv, "col", [(i, i ^ b) for i in range(cols) if (i ^ b) > i])
            for b in range(2, cols, 2)
        ]
        near_kv = [own_kv, lax.ppermute(own_kv, "col", swap_cores)]
        top_pieces = row_exchange(chunks_of(upstream_late.T, 1))
        carried = attention_forward(me, start, query, near_kv, near_offsets)
        proj_rows = unrolled(proj_pieces, 1)
        carried, far_near, top_pieces, proj_rows = lax.optimization_barrier(
            (carried, far_near, top_pieces, proj_rows)
        )

        far_kv = far_near + [lax.ppermute(item, "col", swap_cores) for item in far_near]
        proj_sent = plane_send(proj_rows)
        attn, lse = attention_forward(me, start, query, far_kv, far_offsets, carried)
        attn, w_up, top_pieces, x_late = lax.optimization_barrier((attn, w_up, top_pieces, x_all))

        attn_pieces = row_exchange(chunks_of(attn, 1))
        x_few = lax.dynamic_slice_in_dim(x_late, z * few, few, 2).reshape(dps, rows, half, few)
        x_few = swapped(x_few, 0).transpose(1, 0, 2, 3).reshape(rows, feats, few)
        x_few = unrolled([x_few[k] for k in range(rows)], 0).T
        top_turned = lax.optimization_barrier(unrolled(top_pieces, 0))
        top_few = jnp.pad(top_turned.T, ((0, 0), (0, WIDE - D)))
        attn_pieces, proj_sent, x_few, top_few = lax.optimization_barrier((attn_pieces, proj_sent, x_few, top_few))
        if n_rows % 8:
            proj_sent = [jnp.concatenate(proj_sent, axis=0)]
        proj_halves = proj_sent + [core_send(item) for item in proj_sent]
        top_sent = plane_send(top_few)

        attn_few, mid, h2, mean_two, inverse_two = project(
            weight_table, at(jnp.asarray(to_plain), z), attn_pieces, proj_halves, x_few, jnp.stack([vectors[4], vectors[5], vectors[6]]), unit
        )
        h2, top_sent, w_down = lax.optimization_barrier((h2, top_sent, w_down))

        top_first = jnp.concatenate(top_sent, axis=0)
        top_second = core_send(top_first)
        h2_sent, top_second = lax.optimization_barrier((plane_send(h2), top_second))

        h2_first = jnp.concatenate(h2_sent, axis=0)
        h2_second = core_send(h2_first)
        up_shift = lax.dynamic_slice_in_dim(up_bias, (c * dps + y) * hidden, hidden)[None, :]
        act_near, pre_near, bias_near = hidden_units(h2_first, top_first, w_up, w_down, up_shift)
        act_far, pre_far, bias_far = hidden_units(h2_second, top_second, w_up, w_down, up_shift)
        bias_part = (bias_near + bias_far)[0]
        back_far = features_back(pre_far, w_up)
        back_received = core_send(back_far)
        back_near = features_back(after(pre_near, back_far), w_up)
        act_near, act_far, pre_near, pre_far, back_near, back_received = lax.optimization_barrier(
            (act_near, act_far, pre_near, pre_far, back_near, back_received)
        )

        back_terms = plane_scatter(back_near, back_received, 0)
        down_far = features_back(act_far, w_down)
        down_received = core_send(down_far)
        down_near = features_back(act_near, w_down)
        up_part = weight_part([h2_first, h2_second], [pre_near, pre_far])
        down_part = weight_part([top_first, top_second], [act_near, act_far])
        back_terms, down_received, down_near, up_part, down_part = lax.optimization_barrier(
            (back_terms, down_received, down_near, up_part, down_part)
        )
        up_sum = lax.psum_scatter(up_part, "row", scatter_dimension=0, tiled=True)

        grad_mid_half, heads_out, mid_sums = project_back(
            heads_table,
            back_terms,
            top_few,
            mid,
            mean_two,
            inverse_two,
            vectors[5][None, :],
            proj_halves,
            rows * wide,
            unit,
        )
        down_terms = plane_scatter(after(down_near, grad_mid_half), down_received, 0)
        head_pieces = row_exchange([heads_out[k * wide : (k + 1) * wide] for k in range(rows)])
        proj_part = mm("rt,tf->rf", attn_few, grad_mid_half).astype(BF16)
        head_pieces, proj_part, down_part = lax.optimization_barrier((head_pieces, proj_part, down_part))
        proj_sum = lax.psum_scatter(proj_part, ("dp", "col"), scatter_dimension=0, tiled=True)
        down_sum_part = lax.psum_scatter(down_part, "row", scatter_dimension=0, tiled=True)
        grad_heads = unrolled(head_pieces, 1)

        far = attention_backward(me, start, query, far_kv, far_offsets, attn, lse, grad_heads)
        far, down_terms = lax.optimization_barrier((far, down_terms))
        half_far = len(far_offsets) // 2
        far_grads = [jnp.concatenate(far[2 * i : 2 * i + 2], axis=0) for i in range(len(far_offsets))]
        far_value_total, carried_query = far[-2:]
        far_received = [lax.ppermute(item, "col", swap_cores) for item in far_grads[half_far:]]
        far_sent = []
        for i in range(half_far):
            b = far_offsets[i]
            both = (far_grads[i].astype(F32) + far_received[i].astype(F32)).astype(BF16)
            far_sent.append(lax.ppermute(both, "col", [(j, j ^ b) for j in range(cols) if (j ^ b) < j]))
        out_few = (mid + total_of([item[:, :D] for item in down_terms]) + vectors[7]).astype(BF16)
        side_rows = jnp.concatenate(
            [grad_mid_half.T.reshape(rows, feats, few), out_few.T.reshape(rows, feats, few)], axis=1
        )
        sides = row_exchange([at(side_rows, (z + k) % rows) for k in range(rows)])

        carried_query, _ = lax.optimization_barrier((carried_query, far_received))
        near = attention_backward(
            me, start, query, near_kv, near_offsets, attn, lse, grad_heads, carried_query
        )
        near, far_sent, sides, up_sum = lax.optimization_barrier((near, far_sent, sides, up_sum))
        up_blocks = up_sum.reshape(dps, half, hidden)
        up_back = dp_exchange([at(up_blocks, y ^ d) for d in range(dps)])
        near_value_total, grad_query, query_total = near[-3:]
        value_total = near_value_total + far_value_total
        near_received = lax.ppermute(jnp.concatenate(near[2:4], axis=0), "col", swap_cores)
        own_sum = jnp.concatenate(near[0:2], axis=0).astype(F32) + near_received.astype(F32)
        for item in far_sent:
            own_sum = own_sum + item.astype(F32)
        grad_qkv = jnp.concatenate([grad_query, own_sum.astype(BF16)], axis=0)
        finals = at(jnp.asarray(pack_final), z)
        finals = jnp.concatenate([at(finals, c ^ b) for b in offsets])
        grad_packed = move_units(finals, [grad_qkv], None, cols * packed, BF16)
        grad_packed = lax.optimization_barrier(grad_packed)

        gain_one = vec_swap[0].reshape(dps, rows * half, 1)
        near_cols = cols // 2 * packed
        flat = (dps * (cols // 2), rows * half, packed)
        part_half, sum_norm, sum_plain = qkv_back(
            halves, grad_packed, x_all, mean_one, inverse_one, gain_one, rows
        )
        ln_terms = [part_half[0]] + [to_row(part_half[k], k) for k in range(1, rows)]
        grad_packed = after(grad_packed, part_half)
        qkv_far = qkv_weight_part(h1, grad_packed[near_cols:], cols // 2, packed)
        qkv_received = core_send(qkv_far.reshape(flat))
        grad_packed = after(grad_packed, qkv_far)
        qkv_near = qkv_weight_part(h1, grad_packed[:near_cols], cols // 2, packed)
        qkv_terms = plane_scatter(qkv_near.reshape(flat), qkv_received, 0)
        sum_norm, sum_plain, query_total, value_total, mid_sums, bias_part, top_own, up_back, _ = (
            lax.optimization_barrier(
                (sum_norm, sum_plain, query_total, value_total, mid_sums, bias_part, upstream, up_back, qkv_near)
            )
        )

        def back_from_rel(vector):
            blocks = vector.reshape(rows, feats)
            return jnp.concatenate([at(blocks, (t - z) % rows) for t in range(rows)])

        def back_from_swap(vector):
            return back_from_rel(swapped(vector.reshape(dps, rows, half), 0).transpose(1, 0, 2).reshape(D))

        def from_heads(vector):
            blocks = vector.reshape(slots, 1, HEAD_DIM)
            mine = (jnp.arange(rows) == z)[None, :, None]
            return jnp.where(mine, blocks, 0.0).reshape(rows * wide)[:D]

        def token_sums(sum_norm, sum_plain):
            top_sum = jnp.sum(top_own.astype(F32), axis=0)
            parts = jnp.stack(
                [
                    back_from_swap(sum_norm),
                    back_from_swap(sum_plain),
                    from_heads(query_total[:, 0]),
                    from_heads(value_total[:, 0]),
                    mid_sums[0],
                    mid_sums[1],
                    mid_sums[2],
                    lax.dynamic_update_slice_in_dim(jnp.zeros((D,), F32), top_sum, z * feats, 0),
                ]
            )
            bias_full = lax.dynamic_update_slice_in_dim(
                jnp.zeros((up_bias.shape[0],), F32), bias_part, (c * dps + y) * hidden, 0
            )
            return jnp.concatenate([parts.reshape(-1), bias_full])

        up_grad = swapped(jnp.stack(up_back), 0).transpose(1, 0, 2).reshape(half, dps * hidden).astype(F32)
        vector_sums = token_sums(sum_norm, sum_plain)
        qkv_terms, ln_terms, vector_sums, proj_sum = lax.optimization_barrier(
            (qkv_terms, ln_terms, vector_sums, proj_sum)
        )
        qkv_sum = total_of(qkv_terms)[0].astype(BF16).reshape(rows, half, packed)

        qkv_home = jnp.concatenate(row_exchange([qkv_sum[k] for k in range(rows)]), axis=1)
        qkv_home, down_sum_part = lax.optimization_barrier((qkv_home, down_sum_part))
        qkv_grad = mm("fm,nm->fn", qkv_home, select)
        proj_cols = proj_sum.reshape(n_rows, rows, feats).transpose(1, 0, 2)
        proj_grad = total_of(row_exchange([at(proj_cols, (z + k) % rows) for k in range(rows)]))
        own_gain = gain_one.reshape(dps, rows, half, 1)[:, 0]
        where = jnp.stack([((z + k) % rows) * few for k in range(rows)] + [y]).astype(jnp.int32)
        input_grad, block_out = finish(where, ln_terms, x_own, mean_one, inverse_one, own_gain, sides)
        input_grad, block_out = input_grad.T, block_out.T

        vector_sums = vector_sums + lax.ppermute(vector_sums, "col", swap_cores)
        summed = sum_everywhere(vector_sums)
        vector_grad = summed[: 8 * D].reshape(8, D)
        bias_grad = summed[8 * D :]

        new_up, up_state = adam_matrix(up_weight, up_grad, up_moments)
        down_turned = down_sum_part.astype(F32)
        down_grad = down_turned.T
        new_down, down_state = adam_matrix(down_weight.T, down_turned, down_moments.transpose(0, 2, 1))
        new_down, down_state = new_down.T, down_state.transpose(0, 2, 1)
        new_proj, proj_state = adam_matrix(proj_weight, proj_grad, proj_moments)
        new_qkv, qkv_state = adam_matrix(qkv_weight, qkv_grad, qkv_moments)
        new_vectors, vector_state = adam_step(vectors, vector_grad, vector_moments, LR_VECTOR)
        new_bias, bias_state = adam_step(up_bias, bias_grad, bias_moments, LR_VECTOR)
        return (
            block_out,
            input_grad,
            qkv_grad,
            proj_grad,
            up_grad,
            down_grad,
            vector_grad,
            bias_grad,
            new_qkv,
            new_proj,
            new_up,
            new_down,
            new_vectors,
            new_bias,
            qkv_state,
            proj_state,
            up_state,
            down_state,
            vector_state,
            bias_state,
        )

    return per_device


def solution(mesh):
    acts = P(("dp", "col"), "row")
    wide = P(("row", "dp"), "col")
    tall = P(("col", "dp"), "row")
    wide_pair = P(None, ("row", "dp"), "col")
    tall_pair = P(None, ("col", "dp"), "row")
    return jax.shard_map(
        make_block(mesh),
        mesh=mesh,
        in_specs=(
            acts,
            acts,
            P("dp"),
            wide,
            tall,
            wide,
            tall,
            P(),
            P(),
            wide_pair,
            tall_pair,
            wide_pair,
            tall_pair,
            P(),
            P(),
        ),
        out_specs=(
            acts,
            acts,
            wide,
            tall,
            wide,
            tall,
            P(),
            P(),
            wide,
            tall,
            wide,
            tall,
            P(),
            P(),
            wide_pair,
            tall_pair,
            wide_pair,
            tall_pair,
            P(),
            P(),
        ),
        check_vma=False,
    )
```

```python
import math

import jax
import jax.numpy as jnp
import numpy as np
from jax import lax
from jax.experimental import pallas as pl
from jax.experimental.pallas import tpu as pltpu
from jax.sharding import PartitionSpec as P

D = 1600
HEADS = 25
HEAD_DIM = 64
STEP = 3

EPS_NORM = 1e-05
BETA_ONE = 0.9
BETA_TWO = 0.95
EPS_ADAM = 1e-08
LR_MATRIX = 0.08
LR_VECTOR = 0.3
DECAY = 0.1
NEG_FILL = -1e30
GELU_COEF = 0.7978845608028654
GELU_CUBE = 0.044715
UNIT = 16
WIDE = -(-D // 128) * 128

F32 = jnp.float32
BF16 = jnp.bfloat16


def cost(micros):
    return pl.CostEstimate(
        flops=int(micros * 0.35e9), bytes_accessed=int(micros * 1.1e6), transcendentals=0
    )


def mm(spec, left, right):
    return jnp.einsum(spec, left, right, preferred_element_type=F32)


def adam_terms(weight, gradient, first, second, rate):
    first_moment = BETA_ONE * first + (1.0 - BETA_ONE) * gradient
    second = BETA_TWO * second + (1.0 - BETA_TWO) * gradient * gradient
    first_fix = 1.0 - BETA_ONE**STEP
    second_fix = 1.0 - BETA_TWO**STEP
    stepped = weight - rate * (
        first_moment / first_fix / (jnp.sqrt(second / second_fix) + EPS_ADAM) + DECAY * weight
    )
    return stepped, first_moment, second


def adam_step(weight, gradient, moments, rate):
    stepped, first, second = adam_terms(weight, gradient, moments[0], moments[1], rate)
    return (stepped, jnp.stack([first, second]))


def adam_matrix(weight, gradient, moments):
    n, m = weight.shape
    step = next(size for size in (160, 80, 40, n) if n % size == 0 and size * m <= 160 * 512)

    def body(w_ref, g_ref, m_ref, new_ref, state_ref):
        new, first, second = adam_terms(w_ref[...], g_ref[...], m_ref[0], m_ref[1], LR_MATRIX)
        new_ref[...] = new
        state_ref[0] = first
        state_ref[1] = second

    block = pl.BlockSpec((step, m), lambda i: (i, 0))
    pair = pl.BlockSpec((2, step, m), lambda i: (0, i, 0))
    return pl.pallas_call(
        body,
        grid=(n // step,),
        in_specs=[block, block, pair],
        out_specs=[block, pair],
        out_shape=[jax.ShapeDtypeStruct((n, m), F32), jax.ShapeDtypeStruct((2, n, m), F32)],
        compiler_params=pltpu.CompilerParams(vmem_limit_bytes=32 * 2**20),
        cost_estimate=cost(3),
        name="adam_matrix",
    )(weight, gradient, moments)


def head_tables(rows, cols):
    slots = -(-HEADS // rows)
    per_block = 3 * D // cols // UNIT
    per_head = HEAD_DIM // UNIT
    lists = [[[] for _ in range(rows)] for _ in range(cols)]
    for g in range(3 * D // UNIT):
        head = (g // per_head) % HEADS
        lists[g // per_block][head % rows].append(g)
    longest = max(len(entry) for block in lists for entry in block)
    width = -(-longest // 8) * 8
    source = np.full((cols, rows, width * UNIT), -1, np.int32)
    unpack_block = np.full((rows, 3 * slots * per_head), -1, np.int32)
    unpack_rank = np.zeros((rows, 3 * slots * per_head), np.int32)
    pack_final = np.full((rows, cols, width), -1, np.int32)
    for c in range(cols):
        for z in range(rows):
            for rank, g in enumerate(lists[c][z]):
                local = g - c * per_block
                source[c, z, rank * UNIT : (rank + 1) * UNIT] = local * UNIT + np.arange(UNIT)
                part, head = g // per_head // HEADS, (g // per_head) % HEADS
                final = (part * slots + head // rows) * per_head + g % per_head
                unpack_block[z, final] = c
                unpack_rank[z, final] = rank
                pack_final[z, c, rank] = final
    return slots, width, source, unpack_block, unpack_rank, pack_final


def row_tables(rows, dps, cols, slots, plane, n_rows, unit):
    per_head, per_block = HEAD_DIM // unit, n_rows // unit
    place = {entry: i for i, entry in enumerate(plane)}
    to_weight = np.zeros((rows, dps, cols, D // unit), np.int32)
    to_heads = np.full((rows, dps, cols, rows * slots * per_head), -1, np.int32)
    to_plain = np.zeros((rows, D // unit), np.int32)
    for z in range(rows):
        for y in range(dps):
            for c in range(cols):
                for a in range(D // unit):
                    head, q = a // per_head, a % per_head
                    k, j = (head - z) % rows, head // rows
                    n, i = a // per_block, a % per_block
                    in_heads = (k * slots + j) * per_head + q
                    in_weight = place[(y ^ (n % dps), c ^ (n // dps))] * per_block + i
                    to_weight[z, y, c, in_weight] = in_heads
                    to_heads[z, y, c, in_heads] = in_weight
                    to_plain[z, ((n % dps) * cols + n // dps) * per_block + i] = in_heads
    return to_weight, to_heads, to_plain


def move_units(table, sources, bias, out_rows, out_dtype):
    width = sources[0].shape[1]
    units = sources[0].shape[0] // UNIT
    count = out_rows // UNIT

    def body(tab, *refs):
        vals, out = refs[: len(sources)], refs[-1]
        for i in range(count):
            src = tab[i]
            rows = pl.ds(i * UNIT, UNIT)
            block = jnp.zeros((UNIT, width), F32)
            for n, val in enumerate(vals):
                own = src - n * units
                safe = pl.multiple_of(jnp.clip(own, 0, units - 1) * UNIT, UNIT)
                inside = jnp.logical_and(own >= 0, own < units)
                block = jnp.where(inside, val[pl.ds(safe, UNIT), :].astype(F32), block)
            if bias is not None:
                block = block + refs[len(sources)][rows, :]
            out[rows, :] = block.astype(out_dtype)

    extra = [] if bias is None else [bias]
    shape = jax.ShapeDtypeStruct((out_rows, width), out_dtype)
    return pl.pallas_call(
        body,
        grid=(1,),
        out_shape=shape,
        in_specs=[pl.BlockSpec(memory_space=pltpu.SMEM)] + [whole(item) for item in [*sources, *extra]],
        out_specs=whole(shape),
        compiler_params=pltpu.CompilerParams(vmem_limit_bytes=40 * 2**20),
        cost_estimate=cost(3),
        name="move_units",
    )(table, *sources, *extra)


def qkv_product(weight, rows_in):
    dps, blocks, rows, packed = weight.shape
    tokens = rows_in.shape[2]

    def body(w_ref, h_ref, out):
        total = dot_tn(w_ref[0, 0], h_ref[0])
        for d in range(1, dps):
            total = total + dot_tn(w_ref[d, 0], h_ref[d])
        out[...] = total

    return pl.pallas_call(
        body,
        grid=(blocks,),
        in_specs=[
            pl.BlockSpec((dps, 1, rows, packed), lambda i: (0, i, 0, 0)),
            pl.BlockSpec((dps, rows, tokens), lambda i: (0, 0, 0)),
        ],
        out_specs=pl.BlockSpec((packed, tokens), lambda i: (i, 0)),
        out_shape=jax.ShapeDtypeStruct((blocks * packed, tokens), F32),
        compiler_params=pltpu.CompilerParams(vmem_limit_bytes=40 * 2**20),
        cost_estimate=cost(4),
        name="qkv_product",
    )(weight, rows_in)


def qkv_weight_part(rows_in, grads, blocks, packed):
    dps, rows, tokens = rows_in.shape

    def body(h_ref, g_ref, out):
        out[0, 0] = dot_nt(h_ref[0], g_ref[...]).astype(BF16)

    return pl.pallas_call(
        body,
        grid=(dps, blocks),
        in_specs=[
            pl.BlockSpec((1, rows, tokens), lambda d, i: (d, 0, 0)),
            pl.BlockSpec((packed, tokens), lambda d, i: (i, 0)),
        ],
        out_specs=pl.BlockSpec((1, 1, rows, packed), lambda d, i: (d, i, 0, 0)),
        out_shape=jax.ShapeDtypeStruct((dps, blocks, rows, packed), BF16),
        compiler_params=pltpu.CompilerParams(vmem_limit_bytes=40 * 2**20),
        cost_estimate=cost(4),
        name="qkv_weight_part",
    )(rows_in, grads)


def qkv_back(halves, grads, inputs, mean, inverse, gain, row_devices):
    dps, blocks, rows, packed = halves[0].shape
    tokens = inputs.shape[2]
    few = rows // row_devices

    def body(first, second, g_ref, x_ref, mean_ref, inv_ref, gain_ref, part, with_norm, plain):
        total = None
        for n, w_ref in enumerate((first, second)):
            for i in range(blocks):
                start = (n * blocks + i) * packed
                term = dot_nn(w_ref[0, i], g_ref[start : start + packed, :])
                total = term if total is None else total + term
        normed = (x_ref[0].astype(F32) - mean_ref[...]) * inv_ref[...]
        product = total * normed
        with_norm[0] = jnp.sum(product, axis=1, keepdims=True)
        plain[0] = jnp.sum(total, axis=1, keepdims=True)
        weight = gain_ref[0]
        sums = []
        for item in (total, product):
            exact = jnp.sum(item * weight, axis=0, keepdims=True)
            rounded = exact.astype(BF16).astype(F32)
            sums += [rounded, exact - rounded]
        tail = jnp.concatenate(sums + [jnp.zeros((4, tokens), F32)], axis=0)
        for k in range(row_devices):
            block = jnp.concatenate([total[k * few : (k + 1) * few], tail], axis=0)
            part[k, 0] = block.astype(BF16)

    weight_spec = pl.BlockSpec((1, blocks, rows, packed), lambda d: (d, 0, 0, 0))
    row_spec = pl.BlockSpec((1, tokens), lambda d: (0, 0))
    column = pl.BlockSpec((1, rows, 1), lambda d: (d, 0, 0))
    return pl.pallas_call(
        body,
        grid=(dps,),
        in_specs=[
            weight_spec,
            weight_spec,
            pl.BlockSpec((2 * blocks * packed, tokens), lambda d: (0, 0)),
            pl.BlockSpec((1, rows, tokens), lambda d: (d, 0, 0)),
            row_spec,
            row_spec,
            column,
        ],
        out_specs=[
            pl.BlockSpec((row_devices, 1, few + 8, tokens), lambda d: (0, d, 0, 0)),
            column,
            column,
        ],
        out_shape=[
            jax.ShapeDtypeStruct((row_devices, dps, few + 8, tokens), BF16),
            jax.ShapeDtypeStruct((dps, rows, 1), F32),
            jax.ShapeDtypeStruct((dps, rows, 1), F32),
        ],
        compiler_params=pltpu.CompilerParams(vmem_limit_bytes=48 * 2**20),
        cost_estimate=cost(7),
        name="qkv_back",
    )(*halves, grads, inputs, mean, inverse, gain)


def whole(array):
    rank = len(array.shape)
    return pl.BlockSpec(tuple(array.shape), lambda i: (0,) * rank)


def dot_tn(left, right):
    return lax.dot_general(left, right, (((0,), (0,)), ((), ())), preferred_element_type=F32)


def dot_nt(left, right):
    return lax.dot_general(left, right, (((1,), (1,)), ((), ())), preferred_element_type=F32)


def dot_nn(left, right):
    return lax.dot_general(left, right, (((1,), (0,)), ((), ())), preferred_element_type=F32)


def rows_by_table(table, source, target, unit):
    def move(i, carry):
        src = table[i]
        block = source[pl.ds(pl.multiple_of(jnp.maximum(src, 0) * unit, unit), unit), :]
        target[pl.ds(pl.multiple_of(i * unit, unit), unit), :] = jnp.where(src >= 0, block, 0.0)
        return carry

    lax.fori_loop(0, target.shape[0] // unit, move, 0, unroll=8)


def project(table, plain_table, pieces, halves, x_rows, vecs, unit):
    few = pieces[0].shape[1]
    wide = pieces[0].shape[0]
    n, m = len(pieces), len(halves)

    def body(tab, plain_tab, *refs):
        parts, weights, refs = refs[:n], refs[n : n + m], refs[n + m :]
        (x_ref, vec), outs = refs[:2], refs[2:]
        rows_ref, mid_ref, h2_ref, mean_ref, inv_ref, source, target = outs
        for k in range(n):
            source[k * wide : (k + 1) * wide, :] = parts[k][...].astype(F32)
        rows_by_table(tab, source, target, unit)
        mid = x_ref[...].astype(F32) + vec[0:1, :]
        size = weights[0].shape[0]
        for i, weight in enumerate(weights):
            mid = mid + dot_tn(target[i * size : (i + 1) * size, :].astype(BF16), weight[...])
        mean = jnp.sum(mid, axis=1, keepdims=True) / D
        spread = jnp.sum(mid * mid, axis=1, keepdims=True) / D - mean * mean
        inverse = lax.rsqrt(spread + EPS_NORM)
        mid_ref[...] = mid
        h2_ref[...] = jnp.zeros_like(h2_ref)
        h2_ref[:, :D] = ((mid - mean) * inverse * vec[1:2, :] + vec[2:3, :]).astype(BF16)
        mean_ref[...] = mean
        inv_ref[...] = inverse
        rows_by_table(plain_tab, source, target, unit)
        rows_ref[...] = target[...].astype(BF16)

    args = [*pieces, *halves, x_rows, vecs]
    shapes = [
        jax.ShapeDtypeStruct((D, few), BF16),
        jax.ShapeDtypeStruct((few, D), F32),
        jax.ShapeDtypeStruct((few, WIDE), BF16),
        jax.ShapeDtypeStruct((few, 1), F32),
        jax.ShapeDtypeStruct((few, 1), F32),
    ]
    return pl.pallas_call(
        body,
        grid=(1,),
        in_specs=[pl.BlockSpec(memory_space=pltpu.SMEM)] * 2 + [whole(item) for item in args],
        out_specs=[whole(item) for item in shapes],
        out_shape=shapes,
        scratch_shapes=[pltpu.VMEM((n * wide, few), F32), pltpu.VMEM((D, few), F32)],
        compiler_params=pltpu.CompilerParams(vmem_limit_bytes=48 * 2**20),
        cost_estimate=cost(5),
        name="project",
    )(table, plain_table, *args)


def project_back(table, terms, top, mid, mean, inverse, gain, halves, out_rows, unit):
    few = top.shape[0]
    n, m = len(terms), len(halves)

    def body(tab, *refs):
        parts, (top_ref, mid_ref, mean_ref, inv_ref, gain_ref) = refs[:n], refs[n : n + 5]
        weights = refs[n + 5 : n + 5 + m]
        half_ref, heads_ref, sums_ref, source, target = refs[n + 5 + m :]
        grad = parts[0][:, :D].astype(F32)
        for part in parts[1:]:
            grad = grad + part[:, :D].astype(F32)
        inv = inv_ref[...]
        normed = (mid_ref[...] - mean_ref[...]) * inv
        scaled = grad * gain_ref[...]
        first_mean = jnp.sum(scaled, axis=1, keepdims=True) / D
        second_mean = jnp.sum(scaled * normed, axis=1, keepdims=True) / D
        out = top_ref[:, :D].astype(F32) + inv * (scaled - first_mean - normed * second_mean)
        half = out.astype(BF16)
        half_ref[...] = half
        sums_ref[0:1, :] = jnp.sum(out, axis=0, keepdims=True)
        sums_ref[1:2, :] = jnp.sum(grad * normed, axis=0, keepdims=True)
        sums_ref[2:3, :] = jnp.sum(grad, axis=0, keepdims=True)
        size = weights[0].shape[0]
        for i, weight in enumerate(weights):
            source[i * size : (i + 1) * size, :] = dot_nt(weight[...], half)
        rows_by_table(tab, source, target, unit)
        heads_ref[...] = target[...].astype(BF16)

    args = [*terms, top, mid, mean, inverse, gain, *halves]
    shapes = [
        jax.ShapeDtypeStruct((few, D), BF16),
        jax.ShapeDtypeStruct((out_rows, few), BF16),
        jax.ShapeDtypeStruct((3, D), F32),
    ]
    return pl.pallas_call(
        body,
        grid=(1,),
        in_specs=[pl.BlockSpec(memory_space=pltpu.SMEM)] + [whole(item) for item in args],
        out_specs=[whole(item) for item in shapes],
        out_shape=shapes,
        scratch_shapes=[pltpu.VMEM((D, few), F32), pltpu.VMEM((out_rows, few), F32)],
        compiler_params=pltpu.CompilerParams(vmem_limit_bytes=48 * 2**20),
        cost_estimate=cost(5),
        name="project_back",
    )(table, *args)


def hidden_units(h2_rows, top_rows, weights, shift):
    tokens = h2_rows.shape[0]
    row_devices, _, feats, hidden = weights.shape
    step = min(tokens, 256)

    def body(h_ref, t_ref, up, down, shift_ref, act_ref, grad_ref, sum_ref):
        pre = dot_nn(h_ref[:, :D], up[:, 0].reshape(D, hidden)) + shift_ref[...]
        square = pre * pre
        tanh_val = jnp.tanh(GELU_COEF * (pre + GELU_CUBE * pre * square))
        act_ref[...] = (0.5 * pre * (1.0 + tanh_val)).astype(BF16)
        slope = 0.5 * (1.0 + tanh_val) + 0.5 * pre * (1.0 - tanh_val * tanh_val) * GELU_COEF * (
            1.0 + 3.0 * GELU_CUBE * square
        )
        grad = dot_nn(t_ref[:, :D], down[:, 0].reshape(D, hidden)) * slope
        grad_ref[...] = grad.astype(BF16)
        now = jnp.sum(grad, axis=0, keepdims=True)

        @pl.when(pl.program_id(0) == 0)
        def _():
            sum_ref[...] = now

        @pl.when(pl.program_id(0) > 0)
        def _():
            sum_ref[...] += now

    rows_in = pl.BlockSpec((step, WIDE), lambda i: (i, 0))
    up_weight = pl.BlockSpec((row_devices, 1, feats, hidden), lambda i: (0, 0, 0, 0))
    down_weight = pl.BlockSpec((row_devices, 1, feats, hidden), lambda i: (0, 1, 0, 0))
    rows_out = pl.BlockSpec((step, hidden), lambda i: (i, 0))
    line = pl.BlockSpec((1, hidden), lambda i: (0, 0))
    flat = jax.ShapeDtypeStruct((tokens, hidden), BF16)
    return pl.pallas_call(
        body,
        grid=(tokens // step,),
        in_specs=[rows_in, rows_in, up_weight, down_weight, line],
        out_specs=[rows_out, rows_out, line],
        out_shape=[flat, flat, jax.ShapeDtypeStruct((1, hidden), F32)],
        compiler_params=pltpu.CompilerParams(vmem_limit_bytes=44 * 2**20),
        cost_estimate=cost(6),
        name="hidden_units",
    )(h2_rows, top_rows, weights, weights, shift)


def features_back(grads, weights, which):
    tokens, hidden = grads.shape
    row_devices, _, feats, _ = weights.shape

    def body(g_ref, w_ref, out):
        out[...] = jnp.zeros_like(out)
        out[:, :D] = dot_nt(g_ref[...], w_ref[:, 0].reshape(D, hidden)).astype(BF16)

    step = min(tokens, 256)
    return pl.pallas_call(
        body,
        grid=(tokens // step,),
        in_specs=[
            pl.BlockSpec((step, hidden), lambda i: (i, 0)),
            pl.BlockSpec((row_devices, 1, feats, hidden), lambda i: (0, which, 0, 0)),
        ],
        out_specs=pl.BlockSpec((step, WIDE), lambda i: (i, 0)),
        out_shape=jax.ShapeDtypeStruct((tokens, WIDE), BF16),
        compiler_params=pltpu.CompilerParams(vmem_limit_bytes=32 * 2**20),
        cost_estimate=cost(2),
        name="features_back",
    )(grads, weights)


def weight_parts(pairs, row_devices):
    n = len(pairs[0][0])
    hidden = pairs[0][1][0].shape[1]
    feats = D // row_devices

    def body(*refs):
        out = refs[-1]
        for which in range(2):
            parts = refs[2 * n * which : 2 * n * which + n]
            values = refs[2 * n * which + n : 2 * n * which + 2 * n]
            for low in range(0, D, 256):
                high = min(low + 256, D)
                total = dot_tn(parts[0][:, low:high], values[0][...])
                for part, value in zip(parts[1:], values[1:]):
                    total = total + dot_tn(part[:, low:high], value[...])
                place = low
                while place < high:
                    k = place // feats
                    end = min(high, (k + 1) * feats)
                    out[k, which, place - k * feats : end - k * feats, :] = total[place - low : end - low].astype(BF16)
                    place = end

    vmem = pl.BlockSpec(memory_space=pltpu.VMEM)
    return pl.pallas_call(
        body,
        in_specs=[vmem] * (4 * n),
        out_specs=vmem,
        out_shape=jax.ShapeDtypeStruct((row_devices, 2, feats, hidden), BF16),
        compiler_params=pltpu.CompilerParams(vmem_limit_bytes=48 * 2**20),
        cost_estimate=cost(9),
        name="weight_parts",
    )(*pairs[0][0], *pairs[0][1], *pairs[1][0], *pairs[1][1])


def finish(where, terms, x_own, mean, inverse, gain, sides):
    dps, half, tokens = x_own.shape
    feats = dps * half
    few = sides[0].shape[1]
    n = len(terms)

    def body(tab, *refs):
        parts, (x_ref, mean_ref, inv_ref, gain_ref) = refs[:n], refs[n : n + 4]
        side = refs[n + 4 : n + 4 + len(sides)]
        grad_ref, out_ref, held = refs[n + 4 + len(sides) :]
        for k, ref in enumerate(side):
            lanes = pl.ds(pl.multiple_of(tab[k], 128), few)
            held[:, lanes] = ref[:feats, :].astype(F32)
            out_ref[:, lanes] = ref[feats:, :]
        grads, stats = [], None
        for d in range(dps):
            total = parts[0][d].astype(F32)
            for part in parts[1:]:
                total = total + part[d].astype(F32)
            tail = total[half : half + 8]
            stats = tail if stats is None else stats + tail
            grads.append(total[:half])
        first_row = (stats[0:1] + stats[1:2]) / D
        second_row = (stats[2:3] + stats[3:4]) / D
        inv = inv_ref[...]
        inner = []
        for d in range(dps):
            normed = (x_ref[d].astype(F32) - mean_ref[...]) * inv
            inner.append(inv * (grads[d] * gain_ref[d] - first_row - normed * second_row))
        blocks = []
        for i in range(dps):
            block = inner[0]
            for d in range(1, dps):
                block = jnp.where((tab[len(sides)] ^ d) == i, inner[d], block)
            blocks.append(block)
        whole = jnp.concatenate(blocks, axis=0) if dps > 1 else blocks[0]
        grad_ref[...] = (held[...] + whole).astype(BF16)

    args = [*terms, x_own, mean, inverse, gain, *sides]
    flat = jax.ShapeDtypeStruct((feats, tokens), BF16)
    return pl.pallas_call(
        body,
        grid=(1,),
        in_specs=[pl.BlockSpec(memory_space=pltpu.SMEM)] + [whole(item) for item in args],
        out_specs=[whole(flat)] * 2,
        out_shape=[flat, flat],
        scratch_shapes=[pltpu.VMEM((feats, tokens), F32)],
        compiler_params=pltpu.CompilerParams(vmem_limit_bytes=40 * 2**20),
        cost_estimate=cost(4),
        name="finish",
    )(where, *args)


def key_mask(block, me, start, keys, queries, diagonal):
    key_pos = block * keys + lax.broadcasted_iota(jnp.int32, (keys, queries), 0)
    mask = key_pos >= start
    if diagonal:
        query_pos = me * queries + lax.broadcasted_iota(jnp.int32, (keys, queries), 1)
        mask = mask & (key_pos <= query_pos)
    return mask


def attention_forward(me, start, query, key_values, offsets, carried=None):
    rows, tokens = query.shape
    slots = rows // HEAD_DIM
    factor = 1.0 / math.sqrt(HEAD_DIM)
    n = len(offsets)
    fresh = carried is None

    def body(me_ref, start_ref, q_ref, *refs):
        kv, refs = refs[: 2 * n], refs[2 * n :]
        top, total, acc = refs[-3:]
        if not fresh:
            top[...] = refs[0][0]
            total[...] = refs[1][0]
            acc[...] = refs[2][...]
            refs = refs[3:]
        my = me_ref[0]
        start_row = start_ref[...]
        q = q_ref[...] * jnp.asarray(factor, BF16)
        for i, off in enumerate(offsets):
            block = my ^ off
            k_ref, v_ref = kv[2 * i], kv[2 * i + 1]

            def run(off=off, block=block, k_ref=k_ref, v_ref=v_ref):
                first = off == 0
                s = dot_tn(k_ref[...], q)
                mask = key_mask(block, my, start_row, tokens, tokens, off == 0)
                s = jnp.where(mask, s, NEG_FILL)
                high = jnp.max(s, axis=0, keepdims=True)
                if not first:
                    high = jnp.maximum(high, top[...])
                p = jnp.exp(s - high)
                part = jnp.sum(p, axis=0, keepdims=True)
                mixed = dot_nn(v_ref[...], p.astype(BF16))
                if first:
                    total[...] = part
                    acc[...] = mixed
                else:
                    scale = jnp.exp(top[...] - high)
                    total[...] = total[...] * scale + part
                    acc[...] = acc[...] * scale + mixed
                top[...] = high

            if off == 0:
                run()
            else:
                pl.when(block < my)(run)
        if fresh:
            refs[0][0] = top[...]
            refs[1][0] = total[...]
            refs[2][...] = acc[...]
        else:
            refs[0][...] = (acc[...] / total[...]).astype(BF16)
            refs[1][0] = top[...] + jnp.log(total[...])

    piece = (HEAD_DIM, tokens)
    head_spec = pl.BlockSpec(piece, lambda j: (j, 0))
    row_spec = pl.BlockSpec((1, 1, tokens), lambda j: (j, 0, 0))
    specs = [
        pl.BlockSpec(memory_space=pltpu.SMEM),
        pl.BlockSpec((1, tokens), lambda j: (0, 0)),
        head_spec,
    ]
    args = [me, start, query]
    for array in key_values:
        specs += [head_spec, pl.BlockSpec(piece, lambda j: (slots + j, 0))]
        args += [array, array]
    row_shape = jax.ShapeDtypeStruct((slots, 1, tokens), F32)
    if fresh:
        out_specs = [row_spec, row_spec, head_spec]
        out_shape = [row_shape, row_shape, jax.ShapeDtypeStruct((rows, tokens), F32)]
    else:
        specs += [row_spec, row_spec, head_spec]
        args += list(carried)
        out_specs = [head_spec, row_spec]
        out_shape = [jax.ShapeDtypeStruct((rows, tokens), BF16), row_shape]
    return pl.pallas_call(
        body,
        grid=(slots,),
        in_specs=specs,
        out_specs=out_specs,
        out_shape=out_shape,
        scratch_shapes=[
            pltpu.VMEM((1, tokens), F32),
            pltpu.VMEM((1, tokens), F32),
            pltpu.VMEM((HEAD_DIM, tokens), F32),
        ],
        compiler_params=pltpu.CompilerParams(vmem_limit_bytes=32 * 2**20),
        cost_estimate=cost(11),
        name="attention_forward",
    )(*args)


def attention_backward(me, start, query, key_values, offsets, out_rows, lse, grad_rows, carried=None):
    rows, tokens = query.shape
    slots = rows // HEAD_DIM
    factor = 1.0 / math.sqrt(HEAD_DIM)
    n = len(offsets)
    fresh = carried is None

    def body(me_ref, start_ref, q_ref, o_ref, lse_ref, g_ref, *refs):
        kv, refs = refs[: 2 * n], refs[2 * n :]
        acc, value_acc = refs[-2:]
        if fresh:
            acc[...] = jnp.zeros_like(acc)
        else:
            acc[...] = refs[0][...]
            refs = refs[1:]
        grads, (dv_sum, dq_ref), rest = refs[: 2 * n], refs[2 * n : 2 * n + 2], refs[2 * n + 2 : -2]
        value_acc[...] = jnp.zeros_like(value_acc)
        my = me_ref[0]
        start_row = start_ref[...]
        q = q_ref[...] * jnp.asarray(factor, BF16)
        g = g_ref[...]
        log_total = lse_ref[0]
        row_dot = jnp.sum(g.astype(F32) * o_ref[...].astype(F32), axis=0, keepdims=True)
        for i, off in enumerate(offsets):
            block = my ^ off
            k_ref, v_ref = kv[2 * i], kv[2 * i + 1]
            dk_ref, dv_ref = grads[2 * i], grads[2 * i + 1]

            def run(off=off, block=block, k_ref=k_ref, v_ref=v_ref, dk_ref=dk_ref, dv_ref=dv_ref):
                k = k_ref[...]
                s = dot_tn(k, q)
                mask = key_mask(block, my, start_row, tokens, tokens, off == 0)
                p = jnp.exp(jnp.where(mask, s, NEG_FILL) - log_total)
                dp = dot_tn(v_ref[...], g)
                ds = (p * (dp - row_dot)).astype(BF16)
                dv = dot_nt(g, p.astype(BF16))
                dv_ref[...] = dv.astype(BF16)
                dk_ref[...] = dot_nt(q, ds).astype(BF16)
                acc[...] += dot_nn(k, ds)
                value_acc[...] += jnp.sum(dv, axis=1, keepdims=True)

            def skip(dk_ref=dk_ref, dv_ref=dv_ref):
                dk_ref[...] = jnp.zeros_like(dk_ref)
                dv_ref[...] = jnp.zeros_like(dv_ref)

            if off == 0:
                run()
            else:
                pl.when(block < my)(run)
                pl.when(block >= my)(skip)
        dv_sum[...] = value_acc[...]
        if fresh:
            dq_ref[...] = acc[...]
        else:
            dq = acc[...] * factor
            dq_ref[...] = dq.astype(BF16)
            rest[0][...] = jnp.sum(dq, axis=1, keepdims=True)

    piece = (HEAD_DIM, tokens)
    head_spec = pl.BlockSpec(piece, lambda j: (j, 0))
    column = pl.BlockSpec((HEAD_DIM, 1), lambda j: (j, 0))
    specs = [
        pl.BlockSpec(memory_space=pltpu.SMEM),
        pl.BlockSpec((1, tokens), lambda j: (0, 0)),
        head_spec,
        head_spec,
        pl.BlockSpec((1, 1, tokens), lambda j: (j, 0, 0)),
        head_spec,
    ]
    args = [me, start, query, out_rows, lse, grad_rows]
    for array in key_values:
        specs += [head_spec, pl.BlockSpec(piece, lambda j: (slots + j, 0))]
        args += [array, array]
    full = jax.ShapeDtypeStruct((rows, tokens), BF16)
    thin = jax.ShapeDtypeStruct((rows, 1), F32)
    if fresh:
        out_specs, out_shape = [column, head_spec], [thin, jax.ShapeDtypeStruct((rows, tokens), F32)]
    else:
        specs += [head_spec]
        args += [carried]
        out_specs, out_shape = [column, head_spec, column], [thin, full, thin]
    return pl.pallas_call(
        body,
        grid=(slots,),
        in_specs=specs,
        out_specs=[head_spec] * (2 * n) + out_specs,
        out_shape=[full] * (2 * n) + out_shape,
        scratch_shapes=[pltpu.VMEM(piece, F32), pltpu.VMEM((HEAD_DIM, 1), F32)],
        compiler_params=pltpu.CompilerParams(vmem_limit_bytes=32 * 2**20),
        cost_estimate=cost(14),
        name="attention_backward",
    )(*args)


def make_block(mesh):
    rows, dps, cols = mesh.shape["row"], mesh.shape["dp"], mesh.shape["col"]
    slots, width, source, unpack_block, unpack_rank, pack_final = head_tables(rows, cols)
    packed = width * UNIT
    offsets = list(range(0, cols, 2)) + list(range(1, cols, 2))
    even = [(d, b) for d in range(dps) for b in range(0, cols, 2)]
    plane = even + [(d, b + 1) for d, b in even]

    n_rows = D // cols // dps
    wide = slots * HEAD_DIM
    unit = math.gcd(n_rows, 8)
    to_weight, to_heads, to_plain = row_tables(rows, dps, cols, slots, plane, n_rows, unit)

    def to_row(values, k):
        return lax.ppermute(values, "row", [(i, (i + k) % rows) for i in range(rows)])

    def row_gather(values):
        return [values] + [to_row(values, rows - k) for k in range(1, rows)]

    def row_exchange(chunks):
        return [chunks[0]] + [to_row(chunks[rows - k], rows - k) for k in range(1, rows)]

    def to_plane(values, d, b):
        return lax.ppermute(
            values,
            ("dp", "col"),
            [(y * cols + c, (y ^ d) * cols + (c ^ b)) for y in range(dps) for c in range(cols)],
        )

    def plane_send(values):
        return [values] + [to_plane(values, d, b) for d, b in even[1:]]

    def core_send(far):
        return to_plane(far, 0, 1)

    def plane_scatter(near, far_received, axis):
        sums = near.astype(F32) + far_received.astype(F32)
        size = sums.shape[axis] // len(even)
        parts = [lax.slice_in_dim(sums, i * size, (i + 1) * size, axis=axis) for i in range(len(even))]
        return [parts[0]] + [to_plane(item.astype(BF16), d, b) for (d, b), item in list(zip(even, parts))[1:]]

    def total_of(terms):
        total = terms[0].astype(F32)
        for item in terms[1:]:
            total = total + item.astype(F32)
        return total

    def dp_exchange(chunks):
        return [chunks[0]] + [
            lax.ppermute(chunks[d], "dp", [(y, y ^ d) for y in range(dps)]) for d in range(1, dps)
        ]

    def sum_everywhere(values):
        for axis, size in (("dp", dps), ("col", cols), ("row", rows)):
            step = 2 if axis == "col" else 1
            while step < size:
                values = values + lax.ppermute(values, axis, [(i, i ^ step) for i in range(size)])
                step *= 2
        return values

    def at(array, index, axis=0):
        return lax.dynamic_index_in_dim(array, index, axis, keepdims=False)

    def per_device(
        hidden_in,
        upstream,
        segment_ids,
        qkv_weight,
        proj_weight,
        up_weight,
        down_weight,
        vectors,
        up_bias,
        qkv_moments,
        proj_moments,
        up_moments,
        down_moments,
        vector_moments,
        bias_moments,
    ):
        z, y, c = lax.axis_index("row"), lax.axis_index("dp"), lax.axis_index("col")
        tokens, feats = hidden_in.shape
        few = tokens // rows
        half = feats // dps
        hidden = down_weight.shape[0]
        group = segment_ids.shape[0]

        def swapped(blocks, axis):
            return jnp.stack([at(blocks, y ^ d, axis) for d in range(dps)], axis=axis)

        def rolled(array, axis):
            return jnp.stack([at(array, (z + k) % rows, axis) for k in range(rows)], axis=axis)

        def unrolled(pieces, axis):
            stacked = jnp.stack(pieces)
            return jnp.concatenate([at(stacked, (t - z) % rows) for t in range(rows)], axis=axis)

        def chunks_of(array, axis):
            size = array.shape[axis] // rows
            return [
                lax.dynamic_slice_in_dim(array, ((z + k) % rows) * size, size, axis) for k in range(rows)
            ]

        me = c.astype(jnp.int32).reshape(1)
        weight_table = at(at(at(jnp.asarray(to_weight), z), y), c)
        heads_table = at(at(at(jnp.asarray(to_heads), z), y), c)

        vec_swap = swapped(rolled(vectors.reshape(8, rows, feats), 1).reshape(8, rows, dps, half), 2)
        vec_swap = vec_swap.transpose(0, 2, 1, 3).reshape(8, D)
        query_ids = lax.dynamic_slice_in_dim(segment_ids, c * tokens, tokens)
        start = jnp.sum((segment_ids[:, None] < query_ids[None, :]).astype(jnp.int32), axis=0)[None, :]

        columns = rolled(at(jnp.asarray(source), c), 0).reshape(rows * packed)
        local_cols = qkv_weight.shape[1]
        select = (
            lax.broadcasted_iota(jnp.int32, (local_cols, rows * packed), 0) == columns[None, :]
        ).astype(BF16)
        sorted_cols = mm("fn,nm->fm", qkv_weight.astype(BF16), select).astype(BF16)
        arrived = row_exchange([sorted_cols[:, k * packed : (k + 1) * packed] for k in range(rows)])
        top_pieces = row_exchange(chunks_of(upstream.T, 1))
        up_parts = up_weight.astype(BF16).reshape(half, dps, hidden).transpose(1, 0, 2)
        up_arrived = dp_exchange([at(up_parts, y ^ d) for d in range(dps)])
        up_rows = swapped(jnp.stack(up_arrived), 0).reshape(feats, hidden)
        arrived, up_rows, down_rows, top_pieces = lax.optimization_barrier(
            (arrived, up_rows, down_weight.astype(BF16).T, top_pieces)
        )

        x_own = swapped(hidden_in.T.reshape(dps, half, tokens), 0)
        qkv_sent = plane_send(jnp.stack(arrived).reshape(1, rows * half, packed))
        x_pieces = row_gather(x_own)
        both_rows = jnp.concatenate([up_rows, down_rows], axis=0)
        qkv_sent, x_pieces, proj_own, both_rows = lax.optimization_barrier(
            (qkv_sent, x_pieces, proj_weight.astype(BF16), both_rows)
        )
        w_both = lax.all_gather(both_rows, "row", axis=0, tiled=True).reshape(rows, 2, feats, hidden)

        proj_pieces = row_gather(proj_own)
        qkv_first = jnp.concatenate(qkv_sent, axis=0)
        qkv_second = core_send(qkv_first)
        halves = [item.reshape(dps, cols // 2, rows * half, packed) for item in (qkv_first, qkv_second)]
        x_all = jnp.stack(x_pieces, axis=1).reshape(dps, rows * half, tokens)
        x_f = x_all.astype(F32).reshape(D, tokens)
        mean_one = jnp.mean(x_f, axis=0, keepdims=True)
        spread_one = jnp.mean(x_f * x_f, axis=0, keepdims=True) - mean_one * mean_one
        inverse_one = lax.rsqrt(spread_one + EPS_NORM)
        h1 = ((x_f - mean_one) * inverse_one * vec_swap[0][:, None] + vec_swap[1][:, None]).astype(BF16)
        h1 = h1.reshape(dps, rows * half, tokens)
        qkv_packed = [qkv_product(item, h1) for item in halves]

        order = np.argsort(np.asarray(offsets)).astype(np.int32)
        where_block = at(jnp.asarray(unpack_block), z)
        unpack = jnp.where(
            where_block >= 0,
            jnp.asarray(order)[c ^ jnp.maximum(where_block, 0)] * width + at(jnp.asarray(unpack_rank), z),
            -1,
        )

        def own_heads(vector):
            padded = jnp.pad(vector, (0, (rows * slots - HEADS) * HEAD_DIM))
            return at(padded.reshape(slots, rows, HEAD_DIM), z, 1).reshape(wide)

        shift = jnp.concatenate([own_heads(vectors[2]), jnp.zeros((wide,), F32), own_heads(vectors[3])])
        qkv_rows = move_units(unpack, qkv_packed, shift[:, None], 3 * wide, BF16)
        qkv_rows, proj_pieces = lax.optimization_barrier((qkv_rows, proj_pieces))

        query, own_kv = qkv_rows[:wide], qkv_rows[wide:]
        swap_cores = [(i, i ^ 1) for i in range(cols)]
        near_offsets = [0, 1]
        far_offsets = list(range(2, cols, 2)) + list(range(3, cols, 2))
        far_near = [
            lax.ppermute(own_kv, "col", [(i, i ^ b) for i in range(cols) if (i ^ b) > i])
            for b in range(2, cols, 2)
        ]
        near_kv = [own_kv, lax.ppermute(own_kv, "col", swap_cores)]
        carried = attention_forward(me, start, query, near_kv, near_offsets)
        proj_rows = unrolled(proj_pieces, 1)
        carried, far_near, top_pieces, proj_rows = lax.optimization_barrier(
            (carried, far_near, top_pieces, proj_rows)
        )

        far_kv = far_near + [lax.ppermute(item, "col", swap_cores) for item in far_near]
        proj_sent = plane_send(proj_rows)
        attn, lse = attention_forward(me, start, query, far_kv, far_offsets, carried)
        attn, top_pieces, x_late = lax.optimization_barrier((attn, top_pieces, x_all))

        attn_pieces = row_exchange(chunks_of(attn, 1))
        x_few = lax.dynamic_slice_in_dim(x_late, z * few, few, 2).reshape(dps, rows, half, few)
        x_few = swapped(x_few, 0).transpose(1, 0, 2, 3).reshape(rows, feats, few)
        x_few = unrolled([x_few[k] for k in range(rows)], 0).T
        top_turned = lax.optimization_barrier(unrolled(top_pieces, 0))
        top_few = jnp.pad(top_turned.T, ((0, 0), (0, WIDE - D)))
        attn_pieces, proj_sent, x_few, top_few = lax.optimization_barrier((attn_pieces, proj_sent, x_few, top_few))
        if n_rows % 8:
            proj_sent = [jnp.concatenate(proj_sent, axis=0)]
        proj_halves = proj_sent + [core_send(item) for item in proj_sent]
        top_sent = plane_send(top_few)

        attn_few, mid, h2, mean_two, inverse_two = project(
            weight_table, at(jnp.asarray(to_plain), z), attn_pieces, proj_halves, x_few, jnp.stack([vectors[4], vectors[5], vectors[6]]), unit
        )
        h2, top_sent = lax.optimization_barrier((h2, top_sent))

        top_first = jnp.concatenate(top_sent, axis=0)
        top_second = core_send(top_first)
        h2_sent, top_second, w_both = lax.optimization_barrier((plane_send(h2), top_second, w_both))

        h2_first = jnp.concatenate(h2_sent, axis=0)
        h2_second = core_send(h2_first)
        up_shift = lax.dynamic_slice_in_dim(up_bias, (c * dps + y) * hidden, hidden)[None, :]
        act_near, pre_near, bias_near = hidden_units(h2_first, top_first, w_both, up_shift)
        act_far, pre_far, bias_far = hidden_units(h2_second, top_second, w_both, up_shift)
        bias_part = (bias_near + bias_far)[0]
        back_far = features_back(pre_far, w_both, 0)
        back_received = core_send(back_far)
        back_near = features_back(pre_near, w_both, 0)
        act_near, act_far, pre_near, pre_far, back_near, back_received = lax.optimization_barrier(
            (act_near, act_far, pre_near, pre_far, back_near, back_received)
        )

        back_terms = plane_scatter(back_near, back_received, 0)
        down_far = features_back(act_far, w_both, 1)
        down_received = core_send(down_far)
        down_near = features_back(act_near, w_both, 1)
        both_part = weight_parts(
            [([h2_first, h2_second], [pre_near, pre_far]), ([top_first, top_second], [act_near, act_far])], rows
        )
        back_terms, down_received, down_near, both_part = lax.optimization_barrier(
            (back_terms, down_received, down_near, both_part)
        )
        both_sum = lax.psum_scatter(
            both_part.reshape(rows * 2 * feats, hidden), "row", scatter_dimension=0, tiled=True
        )

        grad_mid_half, heads_out, mid_sums = project_back(
            heads_table,
            back_terms,
            top_few,
            mid,
            mean_two,
            inverse_two,
            vectors[5][None, :],
            proj_halves,
            rows * wide,
            unit,
        )
        down_terms = plane_scatter(down_near, down_received, 0)
        head_pieces = row_exchange([heads_out[k * wide : (k + 1) * wide] for k in range(rows)])
        proj_part = mm("rt,tf->rf", attn_few, grad_mid_half).astype(BF16)
        head_pieces, proj_part = lax.optimization_barrier((head_pieces, proj_part))
        proj_sum = lax.psum_scatter(proj_part, ("dp", "col"), scatter_dimension=0, tiled=True)
        grad_heads = unrolled(head_pieces, 1)

        far = attention_backward(me, start, query, far_kv, far_offsets, attn, lse, grad_heads)
        far, down_terms = lax.optimization_barrier((far, down_terms))
        half_far = len(far_offsets) // 2
        far_grads = [jnp.concatenate(far[2 * i : 2 * i + 2], axis=0) for i in range(len(far_offsets))]
        far_value_total, carried_query = far[-2:]
        far_received = [lax.ppermute(item, "col", swap_cores) for item in far_grads[half_far:]]
        far_sent = []
        for i in range(half_far):
            b = far_offsets[i]
            both = (far_grads[i].astype(F32) + far_received[i].astype(F32)).astype(BF16)
            far_sent.append(lax.ppermute(both, "col", [(j, j ^ b) for j in range(cols) if (j ^ b) < j]))
        out_few = (mid + total_of([item[:, :D] for item in down_terms]) + vectors[7]).astype(BF16)
        side_rows = jnp.concatenate(
            [grad_mid_half.T.reshape(rows, feats, few), out_few.T.reshape(rows, feats, few)], axis=1
        )
        sides = row_exchange([at(side_rows, (z + k) % rows) for k in range(rows)])

        carried_query, _ = lax.optimization_barrier((carried_query, far_received))
        near = attention_backward(
            me, start, query, near_kv, near_offsets, attn, lse, grad_heads, carried_query
        )
        near, far_sent, sides = lax.optimization_barrier((near, far_sent, sides))
        near_value_total, grad_query, query_total = near[-3:]
        value_total = near_value_total + far_value_total
        near_received = lax.ppermute(jnp.concatenate(near[2:4], axis=0), "col", swap_cores)
        own_sum = jnp.concatenate(near[0:2], axis=0).astype(F32) + near_received.astype(F32)
        for item in far_sent:
            own_sum = own_sum + item.astype(F32)
        grad_qkv = jnp.concatenate([grad_query, own_sum.astype(BF16)], axis=0)
        finals = at(jnp.asarray(pack_final), z)
        finals = jnp.concatenate([at(finals, c ^ b) for b in offsets])
        grad_packed = move_units(finals, [grad_qkv], None, cols * packed, BF16)
        grad_packed = lax.optimization_barrier(grad_packed)

        gain_one = vec_swap[0].reshape(dps, rows * half, 1)
        near_cols = cols // 2 * packed
        flat = (dps * (cols // 2), rows * half, packed)
        part_half, sum_norm, sum_plain = qkv_back(
            halves, grad_packed, x_all, mean_one, inverse_one, gain_one, rows
        )
        part_half, grad_packed = lax.optimization_barrier((part_half, grad_packed))
        ln_terms = [part_half[0]] + [to_row(part_half[k], k) for k in range(1, rows)]
        qkv_far = qkv_weight_part(h1, grad_packed[near_cols:], cols // 2, packed)
        qkv_received = core_send(qkv_far.reshape(flat))
        qkv_near = qkv_weight_part(h1, grad_packed[:near_cols], cols // 2, packed)
        sum_norm, sum_plain, query_total, value_total, mid_sums, bias_part, top_own, qkv_near = (
            lax.optimization_barrier(
                (sum_norm, sum_plain, query_total, value_total, mid_sums, bias_part, upstream, qkv_near)
            )
        )
        qkv_terms = plane_scatter(qkv_near.reshape(flat), qkv_received, 0)
        up_home, down_sum_part = both_sum[:feats], both_sum[feats:]

        def back_from_rel(vector):
            blocks = vector.reshape(rows, feats)
            return jnp.concatenate([at(blocks, (t - z) % rows) for t in range(rows)])

        def back_from_swap(vector):
            return back_from_rel(swapped(vector.reshape(dps, rows, half), 0).transpose(1, 0, 2).reshape(D))

        def from_heads(vector):
            blocks = vector.reshape(slots, 1, HEAD_DIM)
            mine = (jnp.arange(rows) == z)[None, :, None]
            return jnp.where(mine, blocks, 0.0).reshape(rows * wide)[:D]

        def token_sums(sum_norm, sum_plain):
            top_sum = jnp.sum(top_own.astype(F32), axis=0)
            parts = jnp.stack(
                [
                    back_from_swap(sum_norm),
                    back_from_swap(sum_plain),
                    from_heads(query_total[:, 0]),
                    from_heads(value_total[:, 0]),
                    mid_sums[0],
                    mid_sums[1],
                    mid_sums[2],
                    lax.dynamic_update_slice_in_dim(jnp.zeros((D,), F32), top_sum, z * feats, 0),
                ]
            )
            bias_full = lax.dynamic_update_slice_in_dim(
                jnp.zeros((up_bias.shape[0],), F32), bias_part, (c * dps + y) * hidden, 0
            )
            return jnp.concatenate([parts.reshape(-1), bias_full])

        vector_sums = token_sums(sum_norm, sum_plain)
        qkv_terms, ln_terms, vector_sums, up_home = lax.optimization_barrier(
            (qkv_terms, ln_terms, vector_sums, up_home)
        )
        up_blocks = up_home.reshape(dps, half, hidden)
        up_back = dp_exchange([at(up_blocks, y ^ d) for d in range(dps)])
        up_grad = swapped(jnp.stack(up_back), 0).transpose(1, 0, 2).reshape(half, dps * hidden).astype(F32)
        qkv_sum = total_of(qkv_terms)[0].astype(BF16).reshape(rows, half, packed)

        qkv_home = jnp.concatenate(row_exchange([qkv_sum[k] for k in range(rows)]), axis=1)
        qkv_grad = mm("fm,nm->fn", qkv_home, select)
        new_up, up_state = adam_matrix(up_weight, up_grad, up_moments)
        new_up, up_state, proj_sum = lax.optimization_barrier((new_up, up_state, proj_sum))
        proj_cols = proj_sum.reshape(n_rows, rows, feats).transpose(1, 0, 2)
        proj_grad = total_of(row_exchange([at(proj_cols, (z + k) % rows) for k in range(rows)]))
        own_gain = gain_one.reshape(dps, rows, half, 1)[:, 0]
        where = jnp.stack([((z + k) % rows) * few for k in range(rows)] + [y]).astype(jnp.int32)
        input_grad, block_out = finish(where, ln_terms, x_own, mean_one, inverse_one, own_gain, sides)
        input_grad, block_out = input_grad.T, block_out.T

        vector_sums = vector_sums + lax.ppermute(vector_sums, "col", swap_cores)
        summed = sum_everywhere(vector_sums)
        vector_grad = summed[: 8 * D].reshape(8, D)
        bias_grad = summed[8 * D :]

        down_turned = down_sum_part.astype(F32)
        down_grad = down_turned.T
        new_down, down_state = adam_matrix(down_weight.T, down_turned, down_moments.transpose(0, 2, 1))
        new_down, down_state = new_down.T, down_state.transpose(0, 2, 1)
        new_proj, proj_state = adam_matrix(proj_weight, proj_grad, proj_moments)
        new_qkv, qkv_state = adam_matrix(qkv_weight, qkv_grad, qkv_moments)
        new_vectors, vector_state = adam_step(vectors, vector_grad, vector_moments, LR_VECTOR)
        new_bias, bias_state = adam_step(up_bias, bias_grad, bias_moments, LR_VECTOR)
        return (
            block_out,
            input_grad,
            qkv_grad,
            proj_grad,
            up_grad,
            down_grad,
            vector_grad,
            bias_grad,
            new_qkv,
            new_proj,
            new_up,
            new_down,
            new_vectors,
            new_bias,
            qkv_state,
            proj_state,
            up_state,
            down_state,
            vector_state,
            bias_state,
        )

    return per_device


def solution(mesh):
    acts = P(("dp", "col"), "row")
    wide = P(("row", "dp"), "col")
    tall = P(("col", "dp"), "row")
    wide_pair = P(None, ("row", "dp"), "col")
    tall_pair = P(None, ("col", "dp"), "row")
    return jax.shard_map(
        make_block(mesh),
        mesh=mesh,
        in_specs=(
            acts,
            acts,
            P("dp"),
            wide,
            tall,
            wide,
            tall,
            P(),
            P(),
            wide_pair,
            tall_pair,
            wide_pair,
            tall_pair,
            P(),
            P(),
        ),
        out_specs=(
            acts,
            acts,
            wide,
            tall,
            wide,
            tall,
            P(),
            P(),
            wide,
            tall,
            wide,
            tall,
            P(),
            P(),
            wide_pair,
            tall_pair,
            wide_pair,
            tall_pair,
            P(),
            P(),
        ),
        check_vma=False,
    )
```

```python
import math

import jax
import jax.numpy as jnp
import numpy as np
from jax import lax
from jax.experimental import pallas as pl
from jax.experimental.pallas import tpu as pltpu
from jax.sharding import PartitionSpec as P

D = 1600
HEADS = 25
HEAD_DIM = 64
STEP = 3

EPS_NORM = 1e-05
BETA_ONE = 0.9
BETA_TWO = 0.95
EPS_ADAM = 1e-08
LR_MATRIX = 0.08
LR_VECTOR = 0.3
DECAY = 0.1
NEG_FILL = -1e30
GELU_COEF = 0.7978845608028654
GELU_CUBE = 0.044715
UNIT = 16
WIDE = -(-D // 128) * 128

F32 = jnp.float32
BF16 = jnp.bfloat16


def cost(micros):
    return pl.CostEstimate(
        flops=int(micros * 1.1e9), bytes_accessed=int(micros * 3.4e6), transcendentals=0
    )


def mm(spec, left, right):
    return jnp.einsum(spec, left, right, preferred_element_type=F32)


def adam_terms(weight, gradient, first, second, rate):
    first_moment = BETA_ONE * first + (1.0 - BETA_ONE) * gradient
    second = BETA_TWO * second + (1.0 - BETA_TWO) * gradient * gradient
    first_fix = 1.0 - BETA_ONE**STEP
    second_fix = 1.0 - BETA_TWO**STEP
    stepped = weight - rate * (
        first_moment / first_fix / (jnp.sqrt(second / second_fix) + EPS_ADAM) + DECAY * weight
    )
    return stepped, first_moment, second


def adam_step(weight, gradient, moments, rate):
    stepped, first, second = adam_terms(weight, gradient, moments[0], moments[1], rate)
    return (stepped, jnp.stack([first, second]))


def adam_matrix(weight, gradient, moments):
    n, m = weight.shape
    step = next(size for size in (160, 80, 40, n) if n % size == 0 and size * m <= 160 * 512)

    def body(w_ref, g_ref, m_ref, new_ref, state_ref):
        new, first, second = adam_terms(w_ref[...], g_ref[...], m_ref[0], m_ref[1], LR_MATRIX)
        new_ref[...] = new
        state_ref[0] = first
        state_ref[1] = second

    block = pl.BlockSpec((step, m), lambda i: (i, 0))
    pair = pl.BlockSpec((2, step, m), lambda i: (0, i, 0))
    return pl.pallas_call(
        body,
        grid=(n // step,),
        in_specs=[block, block, pair],
        out_specs=[block, pair],
        out_shape=[jax.ShapeDtypeStruct((n, m), F32), jax.ShapeDtypeStruct((2, n, m), F32)],
        compiler_params=pltpu.CompilerParams(vmem_limit_bytes=32 * 2**20),
        cost_estimate=cost(3),
        name="adam_matrix",
    )(weight, gradient, moments)


def head_tables(rows, cols):
    slots = -(-HEADS // rows)
    per_block = 3 * D // cols // UNIT
    per_head = HEAD_DIM // UNIT
    lists = [[[] for _ in range(rows)] for _ in range(cols)]
    for g in range(3 * D // UNIT):
        head = (g // per_head) % HEADS
        lists[g // per_block][head % rows].append(g)
    longest = max(len(entry) for block in lists for entry in block)
    width = -(-longest // 8) * 8
    source = np.full((cols, rows, width * UNIT), -1, np.int32)
    unpack_block = np.full((rows, 3 * slots * per_head), -1, np.int32)
    unpack_rank = np.zeros((rows, 3 * slots * per_head), np.int32)
    pack_final = np.full((rows, cols, width), -1, np.int32)
    for c in range(cols):
        for z in range(rows):
            for rank, g in enumerate(lists[c][z]):
                local = g - c * per_block
                source[c, z, rank * UNIT : (rank + 1) * UNIT] = local * UNIT + np.arange(UNIT)
                part, head = g // per_head // HEADS, (g // per_head) % HEADS
                final = (part * slots + head // rows) * per_head + g % per_head
                unpack_block[z, final] = c
                unpack_rank[z, final] = rank
                pack_final[z, c, rank] = final
    return slots, width, source, unpack_block, unpack_rank, pack_final


def row_tables(rows, dps, cols, slots, plane, n_rows, unit):
    per_head, per_block = HEAD_DIM // unit, n_rows // unit
    place = {entry: i for i, entry in enumerate(plane)}
    to_weight = np.zeros((rows, dps, cols, D // unit), np.int32)
    to_heads = np.full((rows, dps, cols, rows * slots * per_head), -1, np.int32)
    to_plain = np.zeros((rows, D // unit), np.int32)
    for z in range(rows):
        for y in range(dps):
            for c in range(cols):
                for a in range(D // unit):
                    head, q = a // per_head, a % per_head
                    k, j = (head - z) % rows, head // rows
                    n, i = a // per_block, a % per_block
                    in_heads = (k * slots + j) * per_head + q
                    in_weight = place[(y ^ (n % dps), c ^ (n // dps))] * per_block + i
                    to_weight[z, y, c, in_weight] = in_heads
                    to_heads[z, y, c, in_heads] = in_weight
                    to_plain[z, ((n % dps) * cols + n // dps) * per_block + i] = in_heads
    return to_weight, to_heads, to_plain


def move_units(table, sources, bias, out_rows, out_dtype):
    width = sources[0].shape[1]
    units = sources[0].shape[0] // UNIT
    count = out_rows // UNIT

    def body(tab, *refs):
        vals, out = refs[: len(sources)], refs[-1]
        for i in range(count):
            src = tab[i]
            rows = pl.ds(i * UNIT, UNIT)
            block = jnp.zeros((UNIT, width), F32)
            for n, val in enumerate(vals):
                own = src - n * units
                safe = pl.multiple_of(jnp.clip(own, 0, units - 1) * UNIT, UNIT)
                inside = jnp.logical_and(own >= 0, own < units)
                block = jnp.where(inside, val[pl.ds(safe, UNIT), :].astype(F32), block)
            if bias is not None:
                block = block + refs[len(sources)][rows, :]
            out[rows, :] = block.astype(out_dtype)

    extra = [] if bias is None else [bias]
    shape = jax.ShapeDtypeStruct((out_rows, width), out_dtype)
    return pl.pallas_call(
        body,
        grid=(1,),
        out_shape=shape,
        in_specs=[pl.BlockSpec(memory_space=pltpu.SMEM)] + [whole(item) for item in [*sources, *extra]],
        out_specs=whole(shape),
        compiler_params=pltpu.CompilerParams(vmem_limit_bytes=40 * 2**20),
        cost_estimate=cost(3),
        name="move_units",
    )(table, *sources, *extra)


def qkv_product(weight, rows_in):
    dps, blocks, rows, packed = weight.shape
    tokens = rows_in.shape[2]

    def body(w_ref, h_ref, out):
        total = dot_tn(w_ref[0, 0], h_ref[0])
        for d in range(1, dps):
            total = total + dot_tn(w_ref[d, 0], h_ref[d])
        out[...] = total

    return pl.pallas_call(
        body,
        grid=(blocks,),
        in_specs=[
            pl.BlockSpec((dps, 1, rows, packed), lambda i: (0, i, 0, 0)),
            pl.BlockSpec((dps, rows, tokens), lambda i: (0, 0, 0)),
        ],
        out_specs=pl.BlockSpec((packed, tokens), lambda i: (i, 0)),
        out_shape=jax.ShapeDtypeStruct((blocks * packed, tokens), F32),
        compiler_params=pltpu.CompilerParams(vmem_limit_bytes=40 * 2**20),
        cost_estimate=cost(4),
        name="qkv_product",
    )(weight, rows_in)


def qkv_weight_part(rows_in, grads, blocks, packed):
    dps, rows, tokens = rows_in.shape

    def body(h_ref, g_ref, out):
        out[0, 0] = dot_nt(h_ref[0], g_ref[...]).astype(BF16)

    return pl.pallas_call(
        body,
        grid=(dps, blocks),
        in_specs=[
            pl.BlockSpec((1, rows, tokens), lambda d, i: (d, 0, 0)),
            pl.BlockSpec((packed, tokens), lambda d, i: (i, 0)),
        ],
        out_specs=pl.BlockSpec((1, 1, rows, packed), lambda d, i: (d, i, 0, 0)),
        out_shape=jax.ShapeDtypeStruct((dps, blocks, rows, packed), BF16),
        compiler_params=pltpu.CompilerParams(vmem_limit_bytes=40 * 2**20),
        cost_estimate=cost(4),
        name="qkv_weight_part",
    )(rows_in, grads)


def qkv_back(halves, grads, inputs, mean, inverse, gain, row_devices):
    dps, blocks, rows, packed = halves[0].shape
    tokens = inputs.shape[2]
    few = rows // row_devices

    def body(first, second, g_ref, x_ref, mean_ref, inv_ref, gain_ref, part, with_norm, plain):
        total = None
        for n, w_ref in enumerate((first, second)):
            for i in range(blocks):
                start = (n * blocks + i) * packed
                term = dot_nn(w_ref[0, i], g_ref[start : start + packed, :])
                total = term if total is None else total + term
        normed = (x_ref[0].astype(F32) - mean_ref[...]) * inv_ref[...]
        product = total * normed
        with_norm[0] = jnp.sum(product, axis=1, keepdims=True)
        plain[0] = jnp.sum(total, axis=1, keepdims=True)
        weight = gain_ref[0]
        sums = []
        for item in (total, product):
            exact = jnp.sum(item * weight, axis=0, keepdims=True)
            rounded = exact.astype(BF16).astype(F32)
            sums += [rounded, exact - rounded]
        tail = jnp.concatenate(sums + [jnp.zeros((4, tokens), F32)], axis=0)
        for k in range(row_devices):
            block = jnp.concatenate([total[k * few : (k + 1) * few], tail], axis=0)
            part[k, 0] = block.astype(BF16)

    weight_spec = pl.BlockSpec((1, blocks, rows, packed), lambda d: (d, 0, 0, 0))
    row_spec = pl.BlockSpec((1, tokens), lambda d: (0, 0))
    column = pl.BlockSpec((1, rows, 1), lambda d: (d, 0, 0))
    return pl.pallas_call(
        body,
        grid=(dps,),
        in_specs=[
            weight_spec,
            weight_spec,
            pl.BlockSpec((2 * blocks * packed, tokens), lambda d: (0, 0)),
            pl.BlockSpec((1, rows, tokens), lambda d: (d, 0, 0)),
            row_spec,
            row_spec,
            column,
        ],
        out_specs=[
            pl.BlockSpec((row_devices, 1, few + 8, tokens), lambda d: (0, d, 0, 0)),
            column,
            column,
        ],
        out_shape=[
            jax.ShapeDtypeStruct((row_devices, dps, few + 8, tokens), BF16),
            jax.ShapeDtypeStruct((dps, rows, 1), F32),
            jax.ShapeDtypeStruct((dps, rows, 1), F32),
        ],
        compiler_params=pltpu.CompilerParams(vmem_limit_bytes=48 * 2**20),
        cost_estimate=cost(7),
        name="qkv_back",
    )(*halves, grads, inputs, mean, inverse, gain)


def whole(array):
    rank = len(array.shape)
    return pl.BlockSpec(tuple(array.shape), lambda i: (0,) * rank)


def dot_tn(left, right):
    return lax.dot_general(left, right, (((0,), (0,)), ((), ())), preferred_element_type=F32)


def dot_nt(left, right):
    return lax.dot_general(left, right, (((1,), (1,)), ((), ())), preferred_element_type=F32)


def dot_nn(left, right):
    return lax.dot_general(left, right, (((1,), (0,)), ((), ())), preferred_element_type=F32)


def rows_by_table(table, source, target, unit):
    def move(i, carry):
        src = table[i]
        block = source[pl.ds(pl.multiple_of(jnp.maximum(src, 0) * unit, unit), unit), :]
        target[pl.ds(pl.multiple_of(i * unit, unit), unit), :] = jnp.where(src >= 0, block, 0.0)
        return carry

    lax.fori_loop(0, target.shape[0] // unit, move, 0, unroll=8)


def project(table, plain_table, pieces, halves, x_rows, vecs, unit):
    few = pieces[0].shape[1]
    wide = pieces[0].shape[0]
    n, m = len(pieces), len(halves)

    def body(tab, plain_tab, *refs):
        parts, weights, refs = refs[:n], refs[n : n + m], refs[n + m :]
        (x_ref, vec), outs = refs[:2], refs[2:]
        rows_ref, mid_ref, h2_ref, mean_ref, inv_ref, source, target = outs
        for k in range(n):
            source[k * wide : (k + 1) * wide, :] = parts[k][...].astype(F32)
        rows_by_table(tab, source, target, unit)
        mid = x_ref[...].astype(F32) + vec[0:1, :]
        size = weights[0].shape[0]
        for i, weight in enumerate(weights):
            mid = mid + dot_tn(target[i * size : (i + 1) * size, :].astype(BF16), weight[...])
        mean = jnp.sum(mid, axis=1, keepdims=True) / D
        spread = jnp.sum(mid * mid, axis=1, keepdims=True) / D - mean * mean
        inverse = lax.rsqrt(spread + EPS_NORM)
        mid_ref[...] = mid
        h2_ref[...] = jnp.zeros_like(h2_ref)
        h2_ref[:, :D] = ((mid - mean) * inverse * vec[1:2, :] + vec[2:3, :]).astype(BF16)
        mean_ref[...] = mean
        inv_ref[...] = inverse
        rows_by_table(plain_tab, source, target, unit)
        rows_ref[...] = target[...].astype(BF16)

    args = [*pieces, *halves, x_rows, vecs]
    shapes = [
        jax.ShapeDtypeStruct((D, few), BF16),
        jax.ShapeDtypeStruct((few, D), F32),
        jax.ShapeDtypeStruct((few, WIDE), BF16),
        jax.ShapeDtypeStruct((few, 1), F32),
        jax.ShapeDtypeStruct((few, 1), F32),
    ]
    return pl.pallas_call(
        body,
        grid=(1,),
        in_specs=[pl.BlockSpec(memory_space=pltpu.SMEM)] * 2 + [whole(item) for item in args],
        out_specs=[whole(item) for item in shapes],
        out_shape=shapes,
        scratch_shapes=[pltpu.VMEM((n * wide, few), F32), pltpu.VMEM((D, few), F32)],
        compiler_params=pltpu.CompilerParams(vmem_limit_bytes=48 * 2**20),
        cost_estimate=cost(5),
        name="project",
    )(table, plain_table, *args)


def project_back(table, terms, top, mid, mean, inverse, gain, halves, out_rows, unit):
    few = top.shape[0]
    n, m = len(terms), len(halves)

    def body(tab, *refs):
        parts, (top_ref, mid_ref, mean_ref, inv_ref, gain_ref) = refs[:n], refs[n : n + 5]
        weights = refs[n + 5 : n + 5 + m]
        half_ref, heads_ref, sums_ref, source, target = refs[n + 5 + m :]
        grad = parts[0][:, :D].astype(F32)
        for part in parts[1:]:
            grad = grad + part[:, :D].astype(F32)
        inv = inv_ref[...]
        normed = (mid_ref[...] - mean_ref[...]) * inv
        scaled = grad * gain_ref[...]
        first_mean = jnp.sum(scaled, axis=1, keepdims=True) / D
        second_mean = jnp.sum(scaled * normed, axis=1, keepdims=True) / D
        out = top_ref[:, :D].astype(F32) + inv * (scaled - first_mean - normed * second_mean)
        half = out.astype(BF16)
        half_ref[...] = half
        sums_ref[0:1, :] = jnp.sum(out, axis=0, keepdims=True)
        sums_ref[1:2, :] = jnp.sum(grad * normed, axis=0, keepdims=True)
        sums_ref[2:3, :] = jnp.sum(grad, axis=0, keepdims=True)
        size = weights[0].shape[0]
        for i, weight in enumerate(weights):
            source[i * size : (i + 1) * size, :] = dot_nt(weight[...], half)
        rows_by_table(tab, source, target, unit)
        heads_ref[...] = target[...].astype(BF16)

    args = [*terms, top, mid, mean, inverse, gain, *halves]
    shapes = [
        jax.ShapeDtypeStruct((few, D), BF16),
        jax.ShapeDtypeStruct((out_rows, few), BF16),
        jax.ShapeDtypeStruct((3, D), F32),
    ]
    return pl.pallas_call(
        body,
        grid=(1,),
        in_specs=[pl.BlockSpec(memory_space=pltpu.SMEM)] + [whole(item) for item in args],
        out_specs=[whole(item) for item in shapes],
        out_shape=shapes,
        scratch_shapes=[pltpu.VMEM((D, few), F32), pltpu.VMEM((out_rows, few), F32)],
        compiler_params=pltpu.CompilerParams(vmem_limit_bytes=48 * 2**20),
        cost_estimate=cost(5),
        name="project_back",
    )(table, *args)


def hidden_units(h2_rows, top_rows, weights, shift):
    tokens = h2_rows.shape[0]
    row_devices, _, feats, hidden = weights.shape
    step = min(tokens, 256)

    def body(h_ref, t_ref, up, down, shift_ref, act_ref, grad_ref, sum_ref):
        pre = dot_nn(h_ref[:, :D], up[:, 0].reshape(D, hidden)) + shift_ref[...]
        square = pre * pre
        tanh_val = jnp.tanh(GELU_COEF * (pre + GELU_CUBE * pre * square))
        act_ref[...] = (0.5 * pre * (1.0 + tanh_val)).astype(BF16)
        slope = 0.5 * (1.0 + tanh_val) + 0.5 * pre * (1.0 - tanh_val * tanh_val) * GELU_COEF * (
            1.0 + 3.0 * GELU_CUBE * square
        )
        grad = dot_nn(t_ref[:, :D], down[:, 0].reshape(D, hidden)) * slope
        grad_ref[...] = grad.astype(BF16)
        now = jnp.sum(grad, axis=0, keepdims=True)

        @pl.when(pl.program_id(0) == 0)
        def _():
            sum_ref[...] = now

        @pl.when(pl.program_id(0) > 0)
        def _():
            sum_ref[...] += now

    rows_in = pl.BlockSpec((step, WIDE), lambda i: (i, 0))
    up_weight = pl.BlockSpec((row_devices, 1, feats, hidden), lambda i: (0, 0, 0, 0))
    down_weight = pl.BlockSpec((row_devices, 1, feats, hidden), lambda i: (0, 1, 0, 0))
    rows_out = pl.BlockSpec((step, hidden), lambda i: (i, 0))
    line = pl.BlockSpec((1, hidden), lambda i: (0, 0))
    flat = jax.ShapeDtypeStruct((tokens, hidden), BF16)
    return pl.pallas_call(
        body,
        grid=(tokens // step,),
        in_specs=[rows_in, rows_in, up_weight, down_weight, line],
        out_specs=[rows_out, rows_out, line],
        out_shape=[flat, flat, jax.ShapeDtypeStruct((1, hidden), F32)],
        compiler_params=pltpu.CompilerParams(vmem_limit_bytes=44 * 2**20),
        cost_estimate=cost(6),
        name="hidden_units",
    )(h2_rows, top_rows, weights, weights, shift)


def features_back(grads, weights, which):
    tokens, hidden = grads.shape
    row_devices, _, feats, _ = weights.shape

    def body(g_ref, w_ref, out):
        out[...] = jnp.zeros_like(out)
        out[:, :D] = dot_nt(g_ref[...], w_ref[:, 0].reshape(D, hidden)).astype(BF16)

    step = min(tokens, 256)
    return pl.pallas_call(
        body,
        grid=(tokens // step,),
        in_specs=[
            pl.BlockSpec((step, hidden), lambda i: (i, 0)),
            pl.BlockSpec((row_devices, 1, feats, hidden), lambda i: (0, which, 0, 0)),
        ],
        out_specs=pl.BlockSpec((step, WIDE), lambda i: (i, 0)),
        out_shape=jax.ShapeDtypeStruct((tokens, WIDE), BF16),
        compiler_params=pltpu.CompilerParams(vmem_limit_bytes=32 * 2**20),
        cost_estimate=cost(2),
        name="features_back",
    )(grads, weights)


def weight_parts(pairs, row_devices):
    n = len(pairs[0][0])
    hidden = pairs[0][1][0].shape[1]
    feats = D // row_devices

    def body(*refs):
        out = refs[-1]
        for which in range(2):
            parts = refs[2 * n * which : 2 * n * which + n]
            values = refs[2 * n * which + n : 2 * n * which + 2 * n]
            for low in range(0, D, 256):
                high = min(low + 256, D)
                total = dot_tn(parts[0][:, low:high], values[0][...])
                for part, value in zip(parts[1:], values[1:]):
                    total = total + dot_tn(part[:, low:high], value[...])
                place = low
                while place < high:
                    k = place // feats
                    end = min(high, (k + 1) * feats)
                    out[k, which, place - k * feats : end - k * feats, :] = total[place - low : end - low].astype(BF16)
                    place = end

    vmem = pl.BlockSpec(memory_space=pltpu.VMEM)
    return pl.pallas_call(
        body,
        in_specs=[vmem] * (4 * n),
        out_specs=vmem,
        out_shape=jax.ShapeDtypeStruct((row_devices, 2, feats, hidden), BF16),
        compiler_params=pltpu.CompilerParams(vmem_limit_bytes=48 * 2**20),
        cost_estimate=cost(9),
        name="weight_parts",
    )(*pairs[0][0], *pairs[0][1], *pairs[1][0], *pairs[1][1])


def finish(where, terms, x_own, mean, inverse, gain, sides):
    dps, half, tokens = x_own.shape
    feats = dps * half
    few = sides[0].shape[1]
    n = len(terms)

    def body(tab, *refs):
        parts, (x_ref, mean_ref, inv_ref, gain_ref) = refs[:n], refs[n : n + 4]
        side = refs[n + 4 : n + 4 + len(sides)]
        grad_ref, out_ref, held = refs[n + 4 + len(sides) :]
        for k, ref in enumerate(side):
            lanes = pl.ds(pl.multiple_of(tab[k], 128), few)
            held[:, lanes] = ref[:feats, :].astype(F32)
            out_ref[:, lanes] = ref[feats:, :]
        grads, stats = [], None
        for d in range(dps):
            total = parts[0][d].astype(F32)
            for part in parts[1:]:
                total = total + part[d].astype(F32)
            tail = total[half : half + 8]
            stats = tail if stats is None else stats + tail
            grads.append(total[:half])
        first_row = (stats[0:1] + stats[1:2]) / D
        second_row = (stats[2:3] + stats[3:4]) / D
        inv = inv_ref[...]
        inner = []
        for d in range(dps):
            normed = (x_ref[d].astype(F32) - mean_ref[...]) * inv
            inner.append(inv * (grads[d] * gain_ref[d] - first_row - normed * second_row))
        blocks = []
        for i in range(dps):
            block = inner[0]
            for d in range(1, dps):
                block = jnp.where((tab[len(sides)] ^ d) == i, inner[d], block)
            blocks.append(block)
        whole = jnp.concatenate(blocks, axis=0) if dps > 1 else blocks[0]
        grad_ref[...] = (held[...] + whole).astype(BF16)

    args = [*terms, x_own, mean, inverse, gain, *sides]
    flat = jax.ShapeDtypeStruct((feats, tokens), BF16)
    return pl.pallas_call(
        body,
        grid=(1,),
        in_specs=[pl.BlockSpec(memory_space=pltpu.SMEM)] + [whole(item) for item in args],
        out_specs=[whole(flat)] * 2,
        out_shape=[flat, flat],
        scratch_shapes=[pltpu.VMEM((feats, tokens), F32)],
        compiler_params=pltpu.CompilerParams(vmem_limit_bytes=40 * 2**20),
        cost_estimate=cost(4),
        name="finish",
    )(where, *args)


def key_mask(block, me, start, keys, queries, diagonal):
    key_pos = block * keys + lax.broadcasted_iota(jnp.int32, (keys, queries), 0)
    mask = key_pos >= start
    if diagonal:
        query_pos = me * queries + lax.broadcasted_iota(jnp.int32, (keys, queries), 1)
        mask = mask & (key_pos <= query_pos)
    return mask


def attention_forward(me, start, query, key_values, offsets, carried=None):
    rows, tokens = query.shape
    slots = rows // HEAD_DIM
    factor = 1.0 / math.sqrt(HEAD_DIM)
    n = len(offsets)
    fresh = carried is None

    def body(me_ref, start_ref, q_ref, *refs):
        kv, refs = refs[: 2 * n], refs[2 * n :]
        top, total, acc = refs[-3:]
        if not fresh:
            top[...] = refs[0][0]
            total[...] = refs[1][0]
            acc[...] = refs[2][...]
            refs = refs[3:]
        my = me_ref[0]
        start_row = start_ref[...]
        q = q_ref[...] * jnp.asarray(factor, BF16)
        for i, off in enumerate(offsets):
            block = my ^ off
            k_ref, v_ref = kv[2 * i], kv[2 * i + 1]

            def run(off=off, block=block, k_ref=k_ref, v_ref=v_ref):
                first = off == 0
                s = dot_tn(k_ref[...], q)
                mask = key_mask(block, my, start_row, tokens, tokens, off == 0)
                s = jnp.where(mask, s, NEG_FILL)
                high = jnp.max(s, axis=0, keepdims=True)
                if not first:
                    high = jnp.maximum(high, top[...])
                p = jnp.exp(s - high)
                part = jnp.sum(p, axis=0, keepdims=True)
                mixed = dot_nn(v_ref[...], p.astype(BF16))
                if first:
                    total[...] = part
                    acc[...] = mixed
                else:
                    scale = jnp.exp(top[...] - high)
                    total[...] = total[...] * scale + part
                    acc[...] = acc[...] * scale + mixed
                top[...] = high

            if off == 0:
                run()
            else:
                pl.when(block < my)(run)
        if fresh:
            refs[0][0] = top[...]
            refs[1][0] = total[...]
            refs[2][...] = acc[...]
        else:
            refs[0][...] = (acc[...] / total[...]).astype(BF16)
            refs[1][0] = top[...] + jnp.log(total[...])

    piece = (HEAD_DIM, tokens)
    head_spec = pl.BlockSpec(piece, lambda j: (j, 0))
    row_spec = pl.BlockSpec((1, 1, tokens), lambda j: (j, 0, 0))
    specs = [
        pl.BlockSpec(memory_space=pltpu.SMEM),
        pl.BlockSpec((1, tokens), lambda j: (0, 0)),
        head_spec,
    ]
    args = [me, start, query]
    for array in key_values:
        specs += [head_spec, pl.BlockSpec(piece, lambda j: (slots + j, 0))]
        args += [array, array]
    row_shape = jax.ShapeDtypeStruct((slots, 1, tokens), F32)
    if fresh:
        out_specs = [row_spec, row_spec, head_spec]
        out_shape = [row_shape, row_shape, jax.ShapeDtypeStruct((rows, tokens), F32)]
    else:
        specs += [row_spec, row_spec, head_spec]
        args += list(carried)
        out_specs = [head_spec, row_spec]
        out_shape = [jax.ShapeDtypeStruct((rows, tokens), BF16), row_shape]
    return pl.pallas_call(
        body,
        grid=(slots,),
        in_specs=specs,
        out_specs=out_specs,
        out_shape=out_shape,
        scratch_shapes=[
            pltpu.VMEM((1, tokens), F32),
            pltpu.VMEM((1, tokens), F32),
            pltpu.VMEM((HEAD_DIM, tokens), F32),
        ],
        compiler_params=pltpu.CompilerParams(vmem_limit_bytes=32 * 2**20),
        cost_estimate=cost(11),
        name="attention_forward",
    )(*args)


def attention_backward(me, start, query, key_values, offsets, out_rows, lse, grad_rows, carried=None):
    rows, tokens = query.shape
    slots = rows // HEAD_DIM
    factor = 1.0 / math.sqrt(HEAD_DIM)
    n = len(offsets)
    fresh = carried is None

    def body(me_ref, start_ref, q_ref, o_ref, lse_ref, g_ref, *refs):
        kv, refs = refs[: 2 * n], refs[2 * n :]
        acc, value_acc = refs[-2:]
        if fresh:
            acc[...] = jnp.zeros_like(acc)
        else:
            acc[...] = refs[0][...]
            refs = refs[1:]
        grads, (dv_sum, dq_ref), rest = refs[: 2 * n], refs[2 * n : 2 * n + 2], refs[2 * n + 2 : -2]
        value_acc[...] = jnp.zeros_like(value_acc)
        my = me_ref[0]
        start_row = start_ref[...]
        q = q_ref[...] * jnp.asarray(factor, BF16)
        g = g_ref[...]
        log_total = lse_ref[0]
        row_dot = jnp.sum(g.astype(F32) * o_ref[...].astype(F32), axis=0, keepdims=True)
        for i, off in enumerate(offsets):
            block = my ^ off
            k_ref, v_ref = kv[2 * i], kv[2 * i + 1]
            dk_ref, dv_ref = grads[2 * i], grads[2 * i + 1]

            def run(off=off, block=block, k_ref=k_ref, v_ref=v_ref, dk_ref=dk_ref, dv_ref=dv_ref):
                k = k_ref[...]
                s = dot_tn(k, q)
                mask = key_mask(block, my, start_row, tokens, tokens, off == 0)
                p = jnp.exp(jnp.where(mask, s, NEG_FILL) - log_total)
                dp = dot_tn(v_ref[...], g)
                ds = (p * (dp - row_dot)).astype(BF16)
                dv = dot_nt(g, p.astype(BF16))
                dv_ref[...] = dv.astype(BF16)
                dk_ref[...] = dot_nt(q, ds).astype(BF16)
                acc[...] += dot_nn(k, ds)
                value_acc[...] += jnp.sum(dv, axis=1, keepdims=True)

            def skip(dk_ref=dk_ref, dv_ref=dv_ref):
                dk_ref[...] = jnp.zeros_like(dk_ref)
                dv_ref[...] = jnp.zeros_like(dv_ref)

            if off == 0:
                run()
            else:
                pl.when(block < my)(run)
                pl.when(block >= my)(skip)
        dv_sum[...] = value_acc[...]
        if fresh:
            dq_ref[...] = acc[...]
        else:
            dq = acc[...] * factor
            dq_ref[...] = dq.astype(BF16)
            rest[0][...] = jnp.sum(dq, axis=1, keepdims=True)

    piece = (HEAD_DIM, tokens)
    head_spec = pl.BlockSpec(piece, lambda j: (j, 0))
    column = pl.BlockSpec((HEAD_DIM, 1), lambda j: (j, 0))
    specs = [
        pl.BlockSpec(memory_space=pltpu.SMEM),
        pl.BlockSpec((1, tokens), lambda j: (0, 0)),
        head_spec,
        head_spec,
        pl.BlockSpec((1, 1, tokens), lambda j: (j, 0, 0)),
        head_spec,
    ]
    args = [me, start, query, out_rows, lse, grad_rows]
    for array in key_values:
        specs += [head_spec, pl.BlockSpec(piece, lambda j: (slots + j, 0))]
        args += [array, array]
    full = jax.ShapeDtypeStruct((rows, tokens), BF16)
    thin = jax.ShapeDtypeStruct((rows, 1), F32)
    if fresh:
        out_specs, out_shape = [column, head_spec], [thin, jax.ShapeDtypeStruct((rows, tokens), F32)]
    else:
        specs += [head_spec]
        args += [carried]
        out_specs, out_shape = [column, head_spec, column], [thin, full, thin]
    return pl.pallas_call(
        body,
        grid=(slots,),
        in_specs=specs,
        out_specs=[head_spec] * (2 * n) + out_specs,
        out_shape=[full] * (2 * n) + out_shape,
        scratch_shapes=[pltpu.VMEM(piece, F32), pltpu.VMEM((HEAD_DIM, 1), F32)],
        compiler_params=pltpu.CompilerParams(vmem_limit_bytes=32 * 2**20),
        cost_estimate=cost(14),
        name="attention_backward",
    )(*args)


def make_block(mesh):
    rows, dps, cols = mesh.shape["row"], mesh.shape["dp"], mesh.shape["col"]
    slots, width, source, unpack_block, unpack_rank, pack_final = head_tables(rows, cols)
    packed = width * UNIT
    offsets = list(range(0, cols, 2)) + list(range(1, cols, 2))
    even = [(d, b) for d in range(dps) for b in range(0, cols, 2)]
    plane = even + [(d, b + 1) for d, b in even]

    n_rows = D // cols // dps
    wide = slots * HEAD_DIM
    unit = math.gcd(n_rows, 8)
    to_weight, to_heads, to_plain = row_tables(rows, dps, cols, slots, plane, n_rows, unit)

    def to_row(values, k):
        return lax.ppermute(values, "row", [(i, (i + k) % rows) for i in range(rows)])

    def row_gather(values):
        return [values] + [to_row(values, rows - k) for k in range(1, rows)]

    def row_exchange(chunks):
        return [chunks[0]] + [to_row(chunks[rows - k], rows - k) for k in range(1, rows)]

    def to_plane(values, d, b):
        return lax.ppermute(
            values,
            ("dp", "col"),
            [(y * cols + c, (y ^ d) * cols + (c ^ b)) for y in range(dps) for c in range(cols)],
        )

    def plane_send(values):
        return [values] + [to_plane(values, d, b) for d, b in even[1:]]

    def core_send(far):
        return to_plane(far, 0, 1)

    def plane_scatter(near, far_received, axis):
        sums = near.astype(F32) + far_received.astype(F32)
        size = sums.shape[axis] // len(even)
        parts = [lax.slice_in_dim(sums, i * size, (i + 1) * size, axis=axis) for i in range(len(even))]
        return [parts[0]] + [to_plane(item.astype(BF16), d, b) for (d, b), item in list(zip(even, parts))[1:]]

    def total_of(terms):
        total = terms[0].astype(F32)
        for item in terms[1:]:
            total = total + item.astype(F32)
        return total

    def dp_exchange(chunks):
        return [chunks[0]] + [
            lax.ppermute(chunks[d], "dp", [(y, y ^ d) for y in range(dps)]) for d in range(1, dps)
        ]

    def sum_everywhere(values):
        for axis, size in (("dp", dps), ("col", cols), ("row", rows)):
            step = 2 if axis == "col" else 1
            while step < size:
                values = values + lax.ppermute(values, axis, [(i, i ^ step) for i in range(size)])
                step *= 2
        return values

    def at(array, index, axis=0):
        return lax.dynamic_index_in_dim(array, index, axis, keepdims=False)

    def per_device(
        hidden_in,
        upstream,
        segment_ids,
        qkv_weight,
        proj_weight,
        up_weight,
        down_weight,
        vectors,
        up_bias,
        qkv_moments,
        proj_moments,
        up_moments,
        down_moments,
        vector_moments,
        bias_moments,
    ):
        z, y, c = lax.axis_index("row"), lax.axis_index("dp"), lax.axis_index("col")
        tokens, feats = hidden_in.shape
        few = tokens // rows
        half = feats // dps
        hidden = down_weight.shape[0]
        group = segment_ids.shape[0]

        def swapped(blocks, axis):
            return jnp.stack([at(blocks, y ^ d, axis) for d in range(dps)], axis=axis)

        def rolled(array, axis):
            return jnp.stack([at(array, (z + k) % rows, axis) for k in range(rows)], axis=axis)

        def unrolled(pieces, axis):
            stacked = jnp.stack(pieces)
            return jnp.concatenate([at(stacked, (t - z) % rows) for t in range(rows)], axis=axis)

        def chunks_of(array, axis):
            size = array.shape[axis] // rows
            return [
                lax.dynamic_slice_in_dim(array, ((z + k) % rows) * size, size, axis) for k in range(rows)
            ]

        me = c.astype(jnp.int32).reshape(1)
        weight_table = at(at(at(jnp.asarray(to_weight), z), y), c)
        heads_table = at(at(at(jnp.asarray(to_heads), z), y), c)

        vec_swap = swapped(rolled(vectors.reshape(8, rows, feats), 1).reshape(8, rows, dps, half), 2)
        vec_swap = vec_swap.transpose(0, 2, 1, 3).reshape(8, D)
        query_ids = lax.dynamic_slice_in_dim(segment_ids, c * tokens, tokens)
        start = jnp.sum((segment_ids[:, None] < query_ids[None, :]).astype(jnp.int32), axis=0)[None, :]

        columns = rolled(at(jnp.asarray(source), c), 0).reshape(rows * packed)
        local_cols = qkv_weight.shape[1]
        select = (
            lax.broadcasted_iota(jnp.int32, (local_cols, rows * packed), 0) == columns[None, :]
        ).astype(BF16)
        sorted_cols = mm("fn,nm->fm", qkv_weight.astype(BF16), select).astype(BF16)
        arrived = row_exchange([sorted_cols[:, k * packed : (k + 1) * packed] for k in range(rows)])
        top_pieces = row_exchange(chunks_of(upstream.T, 1))
        up_parts = up_weight.astype(BF16).reshape(half, dps, hidden).transpose(1, 0, 2)
        up_arrived = dp_exchange([at(up_parts, y ^ d) for d in range(dps)])
        up_rows = swapped(jnp.stack(up_arrived), 0).reshape(feats, hidden)
        arrived, up_rows, down_rows, top_pieces = lax.optimization_barrier(
            (arrived, up_rows, down_weight.astype(BF16).T, top_pieces)
        )

        x_own = swapped(hidden_in.T.reshape(dps, half, tokens), 0)
        qkv_sent = plane_send(jnp.stack(arrived).reshape(1, rows * half, packed))
        x_pieces = row_gather(x_own)
        both_rows = jnp.concatenate([up_rows, down_rows], axis=0)
        qkv_sent, x_pieces, proj_own, both_rows = lax.optimization_barrier(
            (qkv_sent, x_pieces, proj_weight.astype(BF16), both_rows)
        )
        w_both = lax.all_gather(both_rows, "row", axis=0, tiled=True).reshape(rows, 2, feats, hidden)

        proj_pieces = row_gather(proj_own)
        qkv_first = jnp.concatenate(qkv_sent, axis=0)
        qkv_second = core_send(qkv_first)
        halves = [item.reshape(dps, cols // 2, rows * half, packed) for item in (qkv_first, qkv_second)]
        x_all = jnp.stack(x_pieces, axis=1).reshape(dps, rows * half, tokens)
        x_f = x_all.astype(F32).reshape(D, tokens)
        mean_one = jnp.mean(x_f, axis=0, keepdims=True)
        spread_one = jnp.mean(x_f * x_f, axis=0, keepdims=True) - mean_one * mean_one
        inverse_one = lax.rsqrt(spread_one + EPS_NORM)
        h1 = ((x_f - mean_one) * inverse_one * vec_swap[0][:, None] + vec_swap[1][:, None]).astype(BF16)
        h1 = h1.reshape(dps, rows * half, tokens)
        qkv_packed = [qkv_product(item, h1) for item in halves]

        order = np.argsort(np.asarray(offsets)).astype(np.int32)
        where_block = at(jnp.asarray(unpack_block), z)
        unpack = jnp.where(
            where_block >= 0,
            jnp.asarray(order)[c ^ jnp.maximum(where_block, 0)] * width + at(jnp.asarray(unpack_rank), z),
            -1,
        )

        def own_heads(vector):
            padded = jnp.pad(vector, (0, (rows * slots - HEADS) * HEAD_DIM))
            return at(padded.reshape(slots, rows, HEAD_DIM), z, 1).reshape(wide)

        shift = jnp.concatenate([own_heads(vectors[2]), jnp.zeros((wide,), F32), own_heads(vectors[3])])
        qkv_rows = move_units(unpack, qkv_packed, shift[:, None], 3 * wide, BF16)
        qkv_rows, proj_pieces = lax.optimization_barrier((qkv_rows, proj_pieces))

        query, own_kv = qkv_rows[:wide], qkv_rows[wide:]
        swap_cores = [(i, i ^ 1) for i in range(cols)]
        near_offsets = [0, 1]
        far_offsets = list(range(2, cols, 2)) + list(range(3, cols, 2))
        far_near = [
            lax.ppermute(own_kv, "col", [(i, i ^ b) for i in range(cols) if (i ^ b) > i])
            for b in range(2, cols, 2)
        ]
        near_kv = [own_kv, lax.ppermute(own_kv, "col", swap_cores)]
        carried = attention_forward(me, start, query, near_kv, near_offsets)
        proj_rows = unrolled(proj_pieces, 1)
        carried, far_near, top_pieces, proj_rows = lax.optimization_barrier(
            (carried, far_near, top_pieces, proj_rows)
        )

        far_kv = far_near + [lax.ppermute(item, "col", swap_cores) for item in far_near]
        proj_sent = plane_send(proj_rows)
        attn, lse = attention_forward(me, start, query, far_kv, far_offsets, carried)
        attn, top_pieces, x_late = lax.optimization_barrier((attn, top_pieces, x_all))

        attn_pieces = row_exchange(chunks_of(attn, 1))
        x_few = lax.dynamic_slice_in_dim(x_late, z * few, few, 2).reshape(dps, rows, half, few)
        x_few = swapped(x_few, 0).transpose(1, 0, 2, 3).reshape(rows, feats, few)
        x_few = unrolled([x_few[k] for k in range(rows)], 0).T
        top_turned = lax.optimization_barrier(unrolled(top_pieces, 0))
        top_few = jnp.pad(top_turned.T, ((0, 0), (0, WIDE - D)))
        attn_pieces, proj_sent, x_few, top_few = lax.optimization_barrier((attn_pieces, proj_sent, x_few, top_few))
        if n_rows % 8:
            proj_sent = [jnp.concatenate(proj_sent, axis=0)]
        proj_halves = proj_sent + [core_send(item) for item in proj_sent]
        top_sent = plane_send(top_few)

        attn_few, mid, h2, mean_two, inverse_two = project(
            weight_table, weight_table, attn_pieces, proj_halves, x_few, jnp.stack([vectors[4], vectors[5], vectors[6]]), unit
        )
        h2, top_sent = lax.optimization_barrier((h2, top_sent))

        top_first = jnp.concatenate(top_sent, axis=0)
        top_second = core_send(top_first)
        h2_sent, top_second, w_both = lax.optimization_barrier((plane_send(h2), top_second, w_both))

        h2_first = jnp.concatenate(h2_sent, axis=0)
        h2_second = core_send(h2_first)
        up_shift = lax.dynamic_slice_in_dim(up_bias, (c * dps + y) * hidden, hidden)[None, :]
        act_near, pre_near, bias_near = hidden_units(h2_first, top_first, w_both, up_shift)
        act_far, pre_far, bias_far = hidden_units(h2_second, top_second, w_both, up_shift)
        bias_part = (bias_near + bias_far)[0]
        back_far = features_back(pre_far, w_both, 0)
        back_received = core_send(back_far)
        back_near = features_back(pre_near, w_both, 0)
        act_near, act_far, pre_near, pre_far, back_near, back_received = lax.optimization_barrier(
            (act_near, act_far, pre_near, pre_far, back_near, back_received)
        )

        back_terms = plane_scatter(back_near, back_received, 0)
        down_far = features_back(act_far, w_both, 1)
        down_received = core_send(down_far)
        down_near = features_back(act_near, w_both, 1)
        both_part = weight_parts(
            [([h2_first, h2_second], [pre_near, pre_far]), ([top_first, top_second], [act_near, act_far])], rows
        )
        back_terms, down_received, down_near, both_part = lax.optimization_barrier(
            (back_terms, down_received, down_near, both_part)
        )
        both_sum = lax.psum_scatter(
            both_part.reshape(rows * 2 * feats, hidden), "row", scatter_dimension=0, tiled=True
        )

        grad_mid_half, heads_out, mid_sums = project_back(
            heads_table,
            back_terms,
            top_few,
            mid,
            mean_two,
            inverse_two,
            vectors[5][None, :],
            proj_halves,
            rows * wide,
            unit,
        )
        down_terms = plane_scatter(down_near, down_received, 0)
        head_pieces = row_exchange([heads_out[k * wide : (k + 1) * wide] for k in range(rows)])
        middle_rows = len(even) * n_rows
        proj_far = mm("rt,tf->rf", attn_few[middle_rows:], grad_mid_half).astype(BF16)
        proj_received = core_send(proj_far)
        proj_near = mm("rt,tf->rf", attn_few[:middle_rows], grad_mid_half).astype(BF16)
        head_pieces, proj_near, proj_received = lax.optimization_barrier((head_pieces, proj_near, proj_received))
        grad_heads = unrolled(head_pieces, 1)

        far = attention_backward(me, start, query, far_kv, far_offsets, attn, lse, grad_heads)
        far, down_terms, proj_near, proj_received = lax.optimization_barrier(
            (far, down_terms, proj_near, proj_received)
        )
        proj_terms = plane_scatter(proj_near, proj_received, 0)
        half_far = len(far_offsets) // 2
        far_grads = [jnp.concatenate(far[2 * i : 2 * i + 2], axis=0) for i in range(len(far_offsets))]
        far_value_total, carried_query = far[-2:]
        far_received = [lax.ppermute(item, "col", swap_cores) for item in far_grads[half_far:]]
        far_sent = []
        for i in range(half_far):
            b = far_offsets[i]
            both = (far_grads[i].astype(F32) + far_received[i].astype(F32)).astype(BF16)
            far_sent.append(lax.ppermute(both, "col", [(j, j ^ b) for j in range(cols) if (j ^ b) < j]))
        out_few = (mid + total_of([item[:, :D] for item in down_terms]) + vectors[7]).astype(BF16)
        side_rows = jnp.concatenate(
            [grad_mid_half.T.reshape(rows, feats, few), out_few.T.reshape(rows, feats, few)], axis=1
        )
        sides = row_exchange([at(side_rows, (z + k) % rows) for k in range(rows)])

        carried_query, _ = lax.optimization_barrier((carried_query, far_received))
        near = attention_backward(
            me, start, query, near_kv, near_offsets, attn, lse, grad_heads, carried_query
        )
        near, far_sent, sides = lax.optimization_barrier((near, far_sent, sides))
        proj_sum = total_of(proj_terms).astype(BF16)
        near_value_total, grad_query, query_total = near[-3:]
        value_total = near_value_total + far_value_total
        near_received = lax.ppermute(jnp.concatenate(near[2:4], axis=0), "col", swap_cores)
        own_sum = jnp.concatenate(near[0:2], axis=0).astype(F32) + near_received.astype(F32)
        for item in far_sent:
            own_sum = own_sum + item.astype(F32)
        grad_qkv = jnp.concatenate([grad_query, own_sum.astype(BF16)], axis=0)
        finals = at(jnp.asarray(pack_final), z)
        finals = jnp.concatenate([at(finals, c ^ b) for b in offsets])
        grad_packed = move_units(finals, [grad_qkv], None, cols * packed, BF16)
        grad_packed = lax.optimization_barrier(grad_packed)

        gain_one = vec_swap[0].reshape(dps, rows * half, 1)
        near_cols = cols // 2 * packed
        flat = (dps * (cols // 2), rows * half, packed)
        part_half, sum_norm, sum_plain = qkv_back(
            halves, grad_packed, x_all, mean_one, inverse_one, gain_one, rows
        )
        part_half, grad_packed = lax.optimization_barrier((part_half, grad_packed))
        ln_terms = [part_half[0]] + [to_row(part_half[k], k) for k in range(1, rows)]
        qkv_far = qkv_weight_part(h1, grad_packed[near_cols:], cols // 2, packed)
        qkv_received = core_send(qkv_far.reshape(flat))
        qkv_near = qkv_weight_part(h1, grad_packed[:near_cols], cols // 2, packed)
        sum_norm, sum_plain, query_total, value_total, mid_sums, bias_part, top_own, qkv_near = (
            lax.optimization_barrier(
                (sum_norm, sum_plain, query_total, value_total, mid_sums, bias_part, upstream, qkv_near)
            )
        )
        qkv_terms = plane_scatter(qkv_near.reshape(flat), qkv_received, 0)
        up_home, down_sum_part = both_sum[:feats], both_sum[feats:]

        def back_from_rel(vector):
            blocks = vector.reshape(rows, feats)
            return jnp.concatenate([at(blocks, (t - z) % rows) for t in range(rows)])

        def back_from_swap(vector):
            return back_from_rel(swapped(vector.reshape(dps, rows, half), 0).transpose(1, 0, 2).reshape(D))

        def from_heads(vector):
            blocks = vector.reshape(slots, 1, HEAD_DIM)
            mine = (jnp.arange(rows) == z)[None, :, None]
            return jnp.where(mine, blocks, 0.0).reshape(rows * wide)[:D]

        def token_sums(sum_norm, sum_plain):
            top_sum = jnp.sum(top_own.astype(F32), axis=0)
            parts = jnp.stack(
                [
                    back_from_swap(sum_norm),
                    back_from_swap(sum_plain),
                    from_heads(query_total[:, 0]),
                    from_heads(value_total[:, 0]),
                    mid_sums[0],
                    mid_sums[1],
                    mid_sums[2],
                    lax.dynamic_update_slice_in_dim(jnp.zeros((D,), F32), top_sum, z * feats, 0),
                ]
            )
            bias_full = lax.dynamic_update_slice_in_dim(
                jnp.zeros((up_bias.shape[0],), F32), bias_part, (c * dps + y) * hidden, 0
            )
            return jnp.concatenate([parts.reshape(-1), bias_full])

        vector_sums = token_sums(sum_norm, sum_plain)
        qkv_terms, ln_terms, vector_sums, up_home, proj_sum = lax.optimization_barrier(
            (qkv_terms, ln_terms, vector_sums, up_home, proj_sum)
        )
        up_blocks = up_home.reshape(dps, half, hidden)
        up_back = dp_exchange([at(up_blocks, y ^ d) for d in range(dps)])
        up_grad = swapped(jnp.stack(up_back), 0).transpose(1, 0, 2).reshape(half, dps * hidden).astype(F32)
        qkv_sum = total_of(qkv_terms)[0].astype(BF16).reshape(rows, half, packed)

        qkv_home = jnp.concatenate(row_exchange([qkv_sum[k] for k in range(rows)]), axis=1)
        qkv_grad = mm("fm,nm->fn", qkv_home, select)
        new_up, up_state = adam_matrix(up_weight, up_grad, up_moments)
        proj_cols = proj_sum.reshape(n_rows, rows, feats).transpose(1, 0, 2)
        proj_grad = total_of(row_exchange([at(proj_cols, (z + k) % rows) for k in range(rows)]))
        own_gain = gain_one.reshape(dps, rows, half, 1)[:, 0]
        where = jnp.stack([((z + k) % rows) * few for k in range(rows)] + [y]).astype(jnp.int32)
        input_grad, block_out = finish(where, ln_terms, x_own, mean_one, inverse_one, own_gain, sides)
        input_grad, block_out = input_grad.T, block_out.T

        vector_sums = vector_sums + lax.ppermute(vector_sums, "col", swap_cores)
        summed = sum_everywhere(vector_sums)
        vector_grad = summed[: 8 * D].reshape(8, D)
        bias_grad = summed[8 * D :]

        down_turned = down_sum_part.astype(F32)
        down_grad = down_turned.T
        new_down, down_state = adam_matrix(down_weight.T, down_turned, down_moments.transpose(0, 2, 1))
        new_down, down_state = new_down.T, down_state.transpose(0, 2, 1)
        new_proj, proj_state = adam_matrix(proj_weight, proj_grad, proj_moments)
        new_qkv, qkv_state = adam_matrix(qkv_weight, qkv_grad, qkv_moments)
        new_vectors, vector_state = adam_step(vectors, vector_grad, vector_moments, LR_VECTOR)
        new_bias, bias_state = adam_step(up_bias, bias_grad, bias_moments, LR_VECTOR)
        return (
            block_out,
            input_grad,
            qkv_grad,
            proj_grad,
            up_grad,
            down_grad,
            vector_grad,
            bias_grad,
            new_qkv,
            new_proj,
            new_up,
            new_down,
            new_vectors,
            new_bias,
            qkv_state,
            proj_state,
            up_state,
            down_state,
            vector_state,
            bias_state,
        )

    return per_device


def solution(mesh):
    acts = P(("dp", "col"), "row")
    wide = P(("row", "dp"), "col")
    tall = P(("col", "dp"), "row")
    wide_pair = P(None, ("row", "dp"), "col")
    tall_pair = P(None, ("col", "dp"), "row")
    return jax.shard_map(
        make_block(mesh),
        mesh=mesh,
        in_specs=(
            acts,
            acts,
            P("dp"),
            wide,
            tall,
            wide,
            tall,
            P(),
            P(),
            wide_pair,
            tall_pair,
            wide_pair,
            tall_pair,
            P(),
            P(),
        ),
        out_specs=(
            acts,
            acts,
            wide,
            tall,
            wide,
            tall,
            P(),
            P(),
            wide,
            tall,
            wide,
            tall,
            P(),
            P(),
            wide_pair,
            tall_pair,
            wide_pair,
            tall_pair,
            P(),
            P(),
        ),
        check_vma=False,
    )
```
